32 devices in a mesh: section: 2 (over x), shard: 4 (over z), replica: 4 (over y, core).
Axes of the slice: x: 2, y: 2, z: 4, core: 2. Of those that a mesh axis runs over, the one named last changes fastest.
Arguments:
- edges: bfloat16 [2, 8, 1536, 768], P('section', 'replica', 'shard'), may hold values from -6 to 6
- attn_in: bfloat16 [2, 768, 2304], P('section', 'shard'), may hold values from -0.21875 to 0.21875
- attn_out: bfloat16 [2, 768, 768], P('section', 'shard'), may hold values from -0.625 to 0.625
- mlp_up: bfloat16 [2, 768, 3072], P('section', 'shard'), may hold values from -0.21875 to 0.21875
- mlp_down: bfloat16 [2, 3072, 768], P('section', 'shard'), may hold values from -0.109375 to 0.109375
- vectors: float32 [2, 12, 768], P('section'), may hold values from -0.3 to 1.4
- key_mask: int32 [8, 1536], P('replica'), may hold values from 0 to 1, as said below
Outputs:
- edges_out: bfloat16 [2, 8, 1536, 768], P('section', 'replica', 'shard')
- grad_attn_in: float32 [2, 768, 2304], P('section', 'shard')
- grad_attn_out: float32 [2, 768, 768], P('section', 'shard')
- grad_mlp_up: float32 [2, 768, 3072], P('section', 'shard')
- grad_mlp_down: float32 [2, 3072, 768], P('section', 'shard')
- grad_vectors: float32 [2, 12, 768], P('section', None, 'shard')
The draws below stay inside these ranges and needn't reach their ends.
Inputs may be any that keep to these rules, and one draw needn't show every extreme that they name: `key_mask`: in each row the ones form a prefix of at least 1440 frames.
All inputs are finite; a program needn't handle non-finite values.
Results may differ from the reference program's by a relative error of at most 0.017.
Values may be sent and summed in bfloat16 or wider, within the bound.
No kernel may reach another device: no remote copies, remote signals or barrier semaphores. Data moves between devices by JAX's collectives and lax.ppermute only.
A program may use at most 320 MiB of HBM per device.

```python
import math
import jax
import jax.numpy as jnp
from jax import lax

D = 768
H = 12
FF = 3072
SEQ = 1536
CLIPS = 8
N_SECTION = 2


def draw_vectors(key, part):
    key = jax.random.fold_in(key, 11)
    gain_key, bias_key = jax.random.split(key)
    gain_draw = jax.random.uniform(gain_key, (N_SECTION, 12, D), jnp.float32, 0.6, 1.4)
    biases = jax.random.uniform(bias_key, (N_SECTION, 12, D), jnp.float32, -0.3, 0.3)
    row_ids = jnp.arange(12)[None, :, None]
    return jnp.where((row_ids == 0) | (row_ids == 5), gain_draw, biases)


def draw_key_mask(key, part):
    key = jax.random.fold_in(key, 23)
    cut_count = jax.random.randint(key, (CLIPS,), 0, SEQ // 16 + 1)
    return (jnp.arange(SEQ)[None, :] < (SEQ - cut_count)[:, None]).astype(jnp.int32)


def block_scale(own_key, dims, cuts, least, largest):
    level, own = 1.0, jax.random.fold_in(own_key, 6)
    for position, blocks in cuts:
        heights = jnp.exp(jax.random.uniform(jax.random.fold_in(own, position), (blocks,), jnp.float32, least / len(cuts), largest / len(cuts)))
        level = level * jnp.repeat(heights, dims[position] // blocks).reshape([-1 if axis == position else 1 for axis in range(len(dims))])
    return level


def scatter_about(key, shape, scale, most, shards=(), dtype=jnp.bfloat16):
    entries = jax.random.normal(key, shape, jnp.float32) * scale
    if len(shards) > 0:
        entries = block_scale(key, shape, shards, -0.22, 0.18) * entries
    return jnp.clip(entries, min=-most, max=most).astype(dtype)


def setup_inputs(seed: int = 0) -> dict:
    key_list = jax.random.split(jax.random.key(seed), 8)
    return {
        "edges": scatter_about(key_list[0], (N_SECTION, CLIPS, SEQ, D), 1.0, 6.0, ((0, 2), (1, 4), (2, 4))),
        "attn_in": scatter_about(key_list[1], (N_SECTION, D, 3 * D), D ** -0.5, 0.21875, ((0, 2), (1, 4))),
        "attn_out": scatter_about(key_list[2], (N_SECTION, D, D), (D // 8) ** -0.5, 0.625, ((0, 2), (1, 4))),
        "mlp_up": scatter_about(key_list[3], (N_SECTION, D, FF), D ** -0.5, 0.21875, ((0, 2), (1, 4))),
        "mlp_down": scatter_about(key_list[4], (N_SECTION, FF, D), FF ** -0.5, 0.109375, ((0, 2), (1, 4))),
        "vectors": draw_vectors(jax.random.fold_in(key_list[7], 71), 0),
        "key_mask": draw_key_mask(jax.random.fold_in(key_list[7], 71), 0),
    }


EPS = 1e-05
MASKED = -1e+30
HIGH = lax.Precision.HIGHEST

@jax.custom_vjp
def low(v):
    return lax.optimization_barrier(v.astype(jnp.bfloat16)).astype(jnp.float32)

@jax.custom_vjp
def low_back(v):
    return v

def low_keep(v):
    return (low(v), None)

def low_pass(kept, grad):
    return (grad,)

def back_keep(v):
    return (v, None)

def back_low(kept, grad):
    return (low(grad),)
low.defvjp(low_keep, low_pass)
low_back.defvjp(back_keep, back_low)

def layer_norm(values, gain_row, offset):
    center = values - lax.optimization_barrier(jnp.mean(values, -1, keepdims=True))
    spread = lax.optimization_barrier(jnp.mean(center * center, -1, keepdims=True))
    return center * lax.rsqrt(spread + EPS) * gain_row + offset

def gelu_exact(values):
    return jax.nn.gelu(values, approximate=False)

def layer(frames, w_in, w_out, w_up, w_down, vector_rows, valid_keys):
    row_count, model_width = frames.shape
    head_size = model_width // H
    normed = low(layer_norm(frames, vector_rows[0], vector_rows[1]))
    bias_in = jnp.concatenate([vector_rows[2], jnp.zeros_like(vector_rows[2]), vector_rows[3]])
    projected = low_back(low(jnp.dot(normed, w_in, precision=HIGH) + bias_in))
    query_heads = projected[:, :model_width].reshape(row_count, H, head_size)
    key_heads = projected[:, model_width:2 * model_width].reshape(row_count, H, head_size)
    value_heads = projected[:, 2 * model_width:].reshape(row_count, H, head_size)
    block_rows = min(512, row_count)

    def attend(query_block):
        scores = jnp.einsum('qhd,khd->hqk', query_block, key_heads, precision=HIGH) / math.sqrt(head_size)
        scores = low_back(jnp.where(valid_keys[None, None, :] > 0, scores, MASKED))
        exp_scores = jnp.exp(scores - lax.optimization_barrier(jnp.max(scores, -1, keepdims=True)))
        attention_probs = low(exp_scores / lax.optimization_barrier(jnp.sum(exp_scores, -1, keepdims=True)))
        return jnp.einsum('hqk,khd->qhd', attention_probs, value_heads, precision=HIGH)
    blocks = query_heads.reshape(row_count // block_rows, block_rows, H, head_size)
    attended = lax.map(jax.checkpoint(attend), blocks).reshape(row_count, model_width)
    attended = low_back(low(attended))
    middle = frames + low_back(jnp.dot(attended, w_out, precision=HIGH) + vector_rows[4])
    normed_two = low(layer_norm(middle, vector_rows[5], vector_rows[6]))
    upward = low_back(jnp.dot(normed_two, w_up, precision=HIGH) + vector_rows[8:].reshape(-1))
    active = low(gelu_exact(upward))
    return middle + low_back(jnp.dot(active, w_down, precision=HIGH) + vector_rows[7])

def reference(edges, attn_in, attn_out, mlp_up, mlp_down, vectors, key_mask):
    inputs_all = edges[0].astype(jnp.float32)
    cotangent = edges[1].astype(jnp.float32)

    def forward(inputs_all, w_in, w_out, w_up, w_down, vector_all):

        def one_clip(pair):
            frames, valid_keys = pair
            hidden = layer(frames, w_in[0], w_out[0], w_up[0], w_down[0], vector_all[0], valid_keys)
            hidden = low_back(low(hidden))
            return layer(hidden, w_in[1], w_out[1], w_up[1], w_down[1], vector_all[1], valid_keys)
        return lax.map(jax.checkpoint(one_clip), (inputs_all, key_mask))
    output, pullback = jax.vjp(forward, inputs_all, attn_in.astype(jnp.float32), attn_out.astype(jnp.float32), mlp_up.astype(jnp.float32), mlp_down.astype(jnp.float32), vectors)
    grad_input, grad_in_w, grad_out_w, grad_up_w, grad_down_w, grad_vec = pullback(cotangent)
    edges_out = jnp.stack([grad_input.astype(jnp.bfloat16), output.astype(jnp.bfloat16)])
    return (edges_out, grad_in_w, grad_out_w, grad_up_w, grad_down_w, grad_vec)
```

```python
import functools

import jax
import jax.numpy as jnp
from jax import lax
from jax.experimental import pallas as pl
from jax.experimental.pallas import tpu as pltpu
from jax.sharding import PartitionSpec as P

H = 12
EPS = 1e-05
MASKED = -1e30
QUARTERS = 4
BF16 = jnp.bfloat16
F32 = jnp.float32
AXES = ("section", "shard", "replica")
NN = (((1,), (0,)), ((), ()))
NT = (((1,), (1,)), ((), ()))
TN = (((0,), (0,)), ((), ()))


def dot(a, b, dims=NN):
    return lax.dot_general(a, b, dims, preferred_element_type=F32)


def layer_norm(values, gain, shift):
    center = values - jnp.mean(values, -1, keepdims=True)
    spread = jnp.mean(center * center, -1, keepdims=True)
    return center * lax.rsqrt(spread + EPS) * gain + shift


def key_chunks(sources, size):
    chunks, base = [], 0
    for source in range(len(sources)):
        rows = sources[source].shape[0]
        for start in range(0, rows, size):
            chunks.append((source, start, base + start))
        base += rows
    return chunks


def attend_kernel(own_ref, other_ref, bias_ref, out_ref, exp_ref, inv_ref, score_ref, *, heads, frames, chunk):
    dim = own_ref.shape[1] // (3 * heads)
    wide = heads * dim
    sources = (own_ref, other_ref)
    chunks = key_chunks(sources, chunk)
    outs = []
    for head in range(heads):
        at = head * dim
        query = own_ref[0:frames, at:at + dim] * (dim ** -0.5)
        lane = lax.broadcasted_iota(jnp.int32, (frames, dim), 1)
        query = jnp.concatenate([query.astype(BF16), (lane == 0).astype(BF16)], 1)
        top = None
        for source, start, row in chunks:
            shift = wide if source == 0 else 0
            key = sources[source][start:start + chunk, shift + at:shift + at + dim]
            key = jnp.concatenate([key, bias_ref[row:row + chunk, :]], 1)
            score = dot(key, query, NT)
            score_ref[row:row + chunk, :] = score
            part = jnp.max(score, 0, keepdims=True)
            top = part if top is None else jnp.maximum(top, part)
        total = None
        for source, start, row in chunks:
            shift = 2 * wide if source == 0 else wide
            weight = jnp.exp(score_ref[row:row + chunk, :] - top).astype(BF16)
            exp_ref[head, row:row + chunk, :] = weight
            value = sources[source][start:start + chunk, shift + at:shift + at + dim]
            value = jnp.concatenate([value, jnp.ones_like(value)], 1)
            part = dot(value, weight, TN)
            total = part if total is None else total + part
        inverse = 1.0 / total[dim:dim + 1, :]
        inv_ref[head:head + 1, :] = inverse
        outs.append((total[0:dim, :] * inverse).T)
    out_ref[...] = jnp.concatenate(outs, 1).astype(BF16)


def attend(own, other, bias, heads, frames):
    keys = own.shape[0] + other.shape[0]
    wide = own.shape[1] // 3
    chunk = min(256, frames)
    if own.shape[0] % chunk:
        chunk = frames
    return pl.pallas_call(
        functools.partial(attend_kernel, heads=heads, frames=frames, chunk=chunk),
        out_shape=(
            jax.ShapeDtypeStruct((frames, wide), BF16),
            jax.ShapeDtypeStruct((heads, keys, frames), BF16),
            jax.ShapeDtypeStruct((heads, frames), F32),
        ),
        scratch_shapes=[pltpu.VMEM((keys, frames), F32)],
        compiler_params=pltpu.CompilerParams(vmem_limit_bytes=40 * 2**20),
        cost_estimate=pl.CostEstimate(
            flops=16 * keys * frames * wide, bytes_accessed=2 * heads * keys * frames, transcendentals=heads * keys * frames
        ),
        name="attend",
    )(own, other, bias)


def attend_back_kernel(own_ref, other_ref, exp_ref, inv_ref, dout_ref, dq_ref, dk_ref, dv_ref, prod_ref, *, heads, frames, chunk):
    dim = own_ref.shape[1] // (3 * heads)
    wide = heads * dim
    scale = dim ** -0.5
    sources = (own_ref, other_ref)
    chunks = key_chunks(sources, chunk)
    dqs = []
    dks, dvs = [[] for _ in chunks], [[] for _ in chunks]
    for head in range(heads):
        at = head * dim
        query = (own_ref[0:frames, at:at + dim] * scale).astype(BF16)
        inverse = inv_ref[head:head + 1, :]
        dout_t = dout_ref[:, at:at + dim].astype(F32).T * inverse
        dout = dout_t.T.astype(BF16)
        dout_t = dout_t.astype(BF16)
        delta = None
        for index, (source, start, row) in enumerate(chunks):
            shift = 2 * wide if source == 0 else wide
            value = sources[source][start:start + chunk, shift + at:shift + at + dim]
            weight = exp_ref[head, row:row + chunk, :]
            prod = dot(value, dout_t) * weight.astype(F32)
            prod_ref[row:row + chunk, :] = prod
            part = jnp.sum(prod, 0, keepdims=True)
            delta = part if delta is None else delta + part
            dvs[index].append(dot(weight, dout))
        delta = delta * inverse
        dq_t = None
        for index, (source, start, row) in enumerate(chunks):
            shift = wide if source == 0 else 0
            key = sources[source][start:start + chunk, shift + at:shift + at + dim]
            weight = exp_ref[head, row:row + chunk, :].astype(F32)
            ds = (prod_ref[row:row + chunk, :] - weight * delta).astype(BF16)
            dks[index].append(dot(ds, query))
            part = dot(key, ds, TN)
            dq_t = part if dq_t is None else dq_t + part
        dqs.append(dq_t.T * scale)
    dq_ref[...] = jnp.concatenate(dqs, 1).astype(BF16)
    for index, (source, start, row) in enumerate(chunks):
        dk_ref[row:row + chunk, :] = jnp.concatenate(dks[index], 1).astype(BF16)
        dv_ref[row:row + chunk, :] = jnp.concatenate(dvs[index], 1).astype(BF16)


def attend_back(own, other, weights, inverse, dout, heads, frames):
    keys = own.shape[0] + other.shape[0]
    wide = own.shape[1] // 3
    chunk = min(256, frames)
    if own.shape[0] % chunk:
        chunk = frames
    return pl.pallas_call(
        functools.partial(attend_back_kernel, heads=heads, frames=frames, chunk=chunk),
        out_shape=(
            jax.ShapeDtypeStruct((frames, wide), BF16),
            jax.ShapeDtypeStruct((keys, wide), BF16),
            jax.ShapeDtypeStruct((keys, wide), BF16),
        ),
        scratch_shapes=[pltpu.VMEM((keys, frames), F32)],
        compiler_params=pltpu.CompilerParams(vmem_limit_bytes=40 * 2**20),
        cost_estimate=pl.CostEstimate(
            flops=32 * keys * frames * wide, bytes_accessed=2 * heads * keys * frames, transcendentals=0
        ),
        name="attend_back",
    )(own, other, weights, inverse, dout)


def up_kernel(in_ref, weight_ref, bias_ref, act_ref, slope_ref):
    up = dot(in_ref[...], weight_ref[...]) + bias_ref[...]
    cdf = 0.5 + 0.5 * lax.erf(up * (0.5 ** 0.5))
    pdf = jnp.exp(-0.5 * up * up) * 0.3989422804014327
    act_ref[...] = (up * cdf).astype(BF16)
    slope_ref[...] = (cdf + up * pdf).astype(BF16)


def up_gelu(values, weight, bias):
    rows, depth = values.shape
    columns = weight.shape[1]
    tile = 256 if columns % 256 == 0 else columns
    return pl.pallas_call(
        up_kernel,
        grid=(columns // tile,),
        in_specs=[
            pl.BlockSpec((rows, depth), lambda i: (0, 0)),
            pl.BlockSpec((depth, tile), lambda i: (0, i)),
            pl.BlockSpec((1, tile), lambda i: (0, i)),
        ],
        out_specs=[pl.BlockSpec((rows, tile), lambda i: (0, i))] * 2,
        out_shape=[jax.ShapeDtypeStruct((rows, columns), BF16)] * 2,
        compiler_params=pltpu.CompilerParams(vmem_limit_bytes=32 * 2**20),
        cost_estimate=pl.CostEstimate(
            flops=2 * rows * depth * columns, bytes_accessed=2 * (rows * depth + depth * columns + 2 * rows * columns),
            transcendentals=2 * rows * columns,
        ),
        name="up_gelu",
    )(values, weight, bias)


def across(block, bit):
    count = lax.axis_size("replica")
    return lax.ppermute(block, "replica", [(i, i ^ bit) for i in range(count)])


def swap_sections(block):
    return lax.ppermute(block, "section", [(0, 1), (1, 0)])


def transposed(block, source, target):
    shards, replicas = lax.axis_size("shard"), lax.axis_size("replica")

    def flat(section, shard, replica):
        return (section * shards + shard) * replicas + replica

    route = []
    for shard in range(shards):
        for replica in range(replicas):
            group, place = divmod(replica, shards)
            here, there = (shard, replica), (place, group * shards + shard)
            if source is None:
                route += [(flat(s, *here), flat(s, *there)) for s in range(2)]
            else:
                route.append((flat(source, *here), flat(target, *there)))
    return lax.ppermute(block, AXES, route)


def in_order(pieces, quarter):
    odd, high = (quarter & 1) == 1, (quarter & 2) == 2
    a, b, c, d = pieces
    a, b, c, d = jnp.where(odd, b, a), jnp.where(odd, a, b), jnp.where(odd, d, c), jnp.where(odd, c, d)
    return jnp.where(high, c, a), jnp.where(high, d, b), jnp.where(high, a, c), jnp.where(high, b, d)


def spread(piece):
    far = across(piece, 2)
    return piece, across(piece, 1), far, across(far, 1)


def reduced(pieces):
    near = [across(pieces[1], 1), across(pieces[3], 1)]
    own = (pieces[0].astype(F32) + near[0].astype(F32)).astype(BF16)
    far = (pieces[2].astype(F32) + near[1].astype(F32)).astype(BF16)
    own = (own.astype(F32) + across(far, 2).astype(F32)).astype(BF16)
    bit = QUARTERS
    while bit < lax.axis_size("replica"):
        own = (own.astype(F32) + across(own, bit).astype(F32)).astype(BF16)
        bit *= 2
    return own


def body(edges, attn_in, attn_out, mlp_up, mlp_down, vectors, key_mask):
    section = lax.axis_index("section")
    first = section == 0
    replica = lax.axis_index("replica")
    shards, replicas = lax.axis_size("shard"), lax.axis_size("replica")
    quarter = replica % QUARTERS
    edges_here = edges[0]
    clips, frames, width = edges_here.shape
    hidden = mlp_up.shape[2]
    dim = width // H
    heads = H // QUARTERS
    wide = heads * dim
    unit = hidden // (shards * QUARTERS)
    rows = attn_in.shape[1]
    assert clips == 2 and lax.axis_size("section") == 2 and replicas % shards == 0 and replicas % QUARTERS == 0

    inputs = jnp.where(first, transposed(edges_here[0], 0, 0), transposed(edges_here[1], 0, 1))
    mask_row = transposed(
        lax.dynamic_index_in_dim(key_mask, section, 0, keepdims=False).astype(F32)[None], None, None
    )[0]

    def pick(block, axis):
        return lax.dynamic_index_in_dim(block, quarter, axis, keepdims=False)

    def gathered(block):
        return lax.all_gather(block, "shard", axis=0, tiled=True)

    own_parts = (
        gathered(pick(attn_in[0].reshape(rows, 3, QUARTERS, wide), 2).reshape(rows, 3 * wide)),
        gathered(attn_out[0]),
        gathered(pick(mlp_up[0].reshape(rows, shards, QUARTERS, unit), 2).reshape(rows, shards * unit)),
        gathered(pick(mlp_down[0].reshape(QUARTERS, unit, width), 0)),
    )
    other_parts = tuple(swap_sections(part) for part in own_parts)
    vector_other = swap_sections(vectors[0])
    layers = []
    for layer in range(2):
        mine = first if layer == 0 else ~first
        w_in, w_out, w_up, w_down = (jnp.where(mine, a, b) for a, b in zip(own_parts, other_parts))
        layers.append((spread(w_in), w_out, spread(w_up), spread(w_down), jnp.where(mine, vectors[0], vector_other)))

    members = [0]
    bit = 2
    while bit < shards:
        members = members + [m ^ bit for m in members]
        bit *= 2
    members = members + [m ^ 1 for m in members]
    place = replica % shards
    bias_row = jnp.concatenate(
        [lax.dynamic_slice_in_dim(mask_row, (place ^ m) * frames, frames, 0) for m in members]
    )
    bias_row = jnp.where(bias_row > 0, 0.0, MASKED).astype(BF16)
    lane = jnp.arange(dim)[None, :]
    key_bias = jnp.where(lane == 0, bias_row[:, None], jnp.zeros((), BF16))

    def chips_rows(block):
        bit = 2
        while bit < shards:
            block = jnp.concatenate([block, across(block, bit)], 0)
            bit *= 2
        return block

    def forward(x_low, layer):
        w_in, w_out, w_up, w_down, vec = layers[layer]
        x_set = chips_rows(x_low)
        normed = layer_norm(x_set.astype(F32), vec[0], vec[1]).astype(BF16)
        zeros = jnp.zeros((QUARTERS, wide), F32)
        bias_in = jnp.stack([vec[2].reshape(QUARTERS, wide), zeros, vec[3].reshape(QUARTERS, wide)], 1)
        own_qkv, other_kv = [], [None] * QUARTERS
        for p in range(QUARTERS):
            bias = lax.dynamic_index_in_dim(bias_in, quarter ^ p, 0, keepdims=False).reshape(3 * wide)
            own_qkv.append((dot(normed, w_in[p]) + bias).astype(BF16))
            other_kv[p ^ 1] = across(own_qkv[p][:, wide:], 1)
        outs, weights, inverses = [], [], []
        for p in range(QUARTERS):
            out, weight, inverse = attend(own_qkv[p], other_kv[p], key_bias, heads, frames)
            outs.append(out)
            weights.append(weight)
            inverses.append(inverse)
        attended = jnp.concatenate(in_order(outs, quarter), 1)
        x = x_low.astype(F32)
        middle = x + dot(attended, w_out) + vec[4]
        normed_two = layer_norm(middle, vec[5], vec[6]).astype(BF16)
        bias_up = vec[8:].reshape(shards, QUARTERS, unit)
        acts, slopes = [], []
        result = middle + vec[7]
        for p in range(QUARTERS):
            bias = lax.dynamic_index_in_dim(bias_up, quarter ^ p, 1, keepdims=False).reshape(1, shards * unit)
            act, slope = up_gelu(normed_two, w_up[p], bias)
            acts.append(act)
            slopes.append(slope)
            result = result + dot(act, w_down[p])
        kept = (x, normed, own_qkv, other_kv, weights, inverses, attended, middle, normed_two, acts, slopes)
        return result.astype(BF16), kept

    def norm_back(values, gain, grad):
        center = values - jnp.mean(values, -1, keepdims=True)
        inv = lax.rsqrt(jnp.mean(center * center, -1, keepdims=True) + EPS)
        unit_values = center * inv
        scaled = grad * gain
        back = inv * (
            scaled - jnp.mean(scaled, -1, keepdims=True)
            - unit_values * jnp.mean(scaled * unit_values, -1, keepdims=True)
        )
        return back, jnp.sum(grad * unit_values, 0), jnp.sum(grad, 0)

    def backward(cot, layer, kept):
        w_in, w_out, w_up, w_down, vec = layers[layer]
        x, normed, own_qkv, other_kv, weights, inverses, attended, middle, normed_two, acts, slopes = kept
        d_mlp = cot.astype(BF16)
        g_down, g_up, up_sums = [], [], []
        d_normed_two = None
        for p in range(QUARTERS):
            d_up = (dot(d_mlp, w_down[p], NT) * slopes[p].astype(F32)).astype(BF16)
            part = dot(d_up, w_up[p], NT)
            d_normed_two = part if d_normed_two is None else d_normed_two + part
            g_down.append(dot(acts[p], d_mlp, TN).astype(BF16))
            g_up.append(dot(normed_two, d_up, TN).astype(BF16))
            up_sums.append(jnp.sum(d_up.astype(F32), 0))
        back, g_gain_two, g_shift_two = norm_back(middle, vec[5], d_normed_two)
        d_middle = cot + back
        d_attn = d_middle.astype(BF16)
        d_attn_parts = in_order([d_attn[:, p * wide:(p + 1) * wide] for p in range(QUARTERS)], quarter)
        g_out = [dot(attended, part, TN).astype(BF16) for part in d_attn_parts]
        d_attended = dot(d_attn, w_out, NT).astype(BF16)
        d_heads = in_order([d_attended[:, p * wide:(p + 1) * wide] for p in range(QUARTERS)], quarter)
        half = own_qkv[0].shape[0]
        d_normed, g_in, sums_in = None, [], []
        d_normed_own = None
        results = [
            attend_back(own_qkv[p], other_kv[p], weights[p], inverses[p], d_heads[p], heads, frames)
            for p in range(QUARTERS)
        ]
        for p in range(QUARTERS):
            d_query, d_key, d_value = results[p]
            r_key, r_value = results[p ^ 1][1], results[p ^ 1][2]
            d_key = (d_key[:half].astype(F32) + across(r_key[half:], 1).astype(F32)).astype(BF16)
            d_value = (d_value[:half].astype(F32) + across(r_value[half:], 1).astype(F32)).astype(BF16)
            d_both = jnp.concatenate([d_key, d_value], 1)
            part = dot(d_both, w_in[p][:, wide:], NT)
            d_normed = part if d_normed is None else d_normed + part
            part = dot(d_query, w_in[p][:, :wide], NT)
            d_normed_own = part if d_normed_own is None else d_normed_own + part
            g_in.append(
                jnp.concatenate(
                    [dot(normed[:frames], d_query, TN).astype(BF16), dot(normed, d_both, TN).astype(BF16)], 1
                )
            )
            sums_in.append(
                (jnp.sum(d_query.astype(F32), 0), jnp.sum(d_value.astype(F32), 0))
            )
        block = d_normed
        bit = shards // 2
        while bit >= 2:
            cut = block.shape[0] // 2
            block = block[:cut] + across(block[cut:].astype(BF16), bit).astype(F32)
            bit //= 2
        back, g_gain_one, g_shift_one = norm_back(x, vec[0], block + d_normed_own)
        g_x = d_middle + back
        sum_query = jnp.concatenate(in_order([s[0] for s in sums_in], quarter))
        sum_value = jnp.concatenate(in_order([s[1] for s in sums_in], quarter))
        sum_up = jnp.stack(in_order([s.reshape(shards, unit) for s in up_sums], quarter), 1).reshape(-1, width)
        g_vec = jnp.concatenate(
            [
                jnp.stack(
                    [
                        g_gain_one, g_shift_one, sum_query, sum_value,
                        jnp.sum(d_attn.astype(F32), 0), g_gain_two, g_shift_two,
                        jnp.sum(d_mlp.astype(F32), 0),
                    ]
                ),
                sum_up,
            ]
        )
        return g_x, (g_in, g_out, g_up, g_down), g_vec

    def owned(grads, layer):
        route = [(0, 1)] if layer == 1 else [(1, 0)]
        done = []
        for pieces in grads:
            part = reduced(pieces)
            part = (part.astype(F32) + lax.ppermute(part, "section", route).astype(F32)).astype(BF16)
            done.append(lax.psum_scatter(part, "shard", scatter_dimension=0, tiled=True))
        return done

    x_one, kept_zero = forward(inputs, 0)
    y_one, kept_one = forward(x_one, 1)
    cot = jnp.where(first, transposed(edges_here[0], 1, 0), transposed(edges_here[1], 1, 1))
    out_slots = [transposed(y_one, 0, 1), transposed(y_one, 1, 1)]
    g_one, grads_one, vec_one = backward(cot.astype(F32), 1, kept_one)
    owned_one = owned(grads_one, 1)
    g_zero, grads_zero, vec_zero = backward(g_one.astype(BF16).astype(F32), 0, kept_zero)
    owned_zero = owned(grads_zero, 0)
    g_low = g_zero.astype(BF16)
    back_slots = [transposed(g_low, 0, 0), transposed(g_low, 1, 0)]
    edges_out = jnp.stack([jnp.where(first, b, o) for b, o in zip(back_slots, out_slots)])

    vec_all = lax.psum(jnp.concatenate([vec_zero, vec_one]), AXES)
    vec_all = jnp.where(first, vec_all[:12], vec_all[12:])
    slice_width = width // shards
    g_vectors = lax.dynamic_slice_in_dim(vec_all, lax.axis_index("shard") * slice_width, slice_width, 1)

    finals = []
    for zero, one in zip(owned_zero, owned_one):
        part = jnp.where(first, zero, one)
        finals.append(jnp.stack(in_order(spread(part), quarter)).astype(F32))
    f_in, f_out, f_up, f_down = finals
    f_in = f_in.reshape(QUARTERS, rows, 3, wide).transpose(1, 2, 0, 3).reshape(rows, 3 * width)
    f_out = f_out.transpose(1, 0, 2).reshape(rows, width)
    f_up = f_up.reshape(QUARTERS, rows, shards, unit).transpose(1, 2, 0, 3).reshape(rows, hidden)
    f_down = f_down.reshape(-1, width)
    return edges_out[None], f_in[None], f_out[None], f_up[None], f_down[None], g_vectors[None]


def solution(mesh):
    placed = (
        P("section", "replica", "shard", None),
        P("section", "shard", None),
        P("section", "shard", None),
        P("section", "shard", None),
        P("section", "shard", None),
        P("section", None, None),
        P("replica", None),
    )
    return jax.shard_map(
        body,
        mesh=mesh,
        in_specs=placed,
        out_specs=(
            P("section", "replica", "shard", None),
            P("section", "shard", None),
            P("section", "shard", None),
            P("section", "shard", None),
            P("section", "shard", None),
            P("section", None, "shard"),
        ),
        check_vma=False,
    )
```

```python
import functools

import jax
import jax.numpy as jnp
from jax import lax
from jax.experimental import pallas as pl
from jax.experimental.pallas import tpu as pltpu
from jax.sharding import PartitionSpec as P

H = 12
EPS = 1e-05
MASKED = -1e30
QUARTERS = 4
BF16 = jnp.bfloat16
F32 = jnp.float32
AXES = ("section", "shard", "replica")
NN = (((1,), (0,)), ((), ()))
NT = (((1,), (1,)), ((), ()))
TN = (((0,), (0,)), ((), ()))


def dot(a, b, dims=NN):
    return lax.dot_general(a, b, dims, preferred_element_type=F32)


def layer_norm(values, gain, shift):
    center = values - jnp.mean(values, -1, keepdims=True)
    spread = jnp.mean(center * center, -1, keepdims=True)
    return center * lax.rsqrt(spread + EPS) * gain + shift


def key_chunks(sources, size):
    chunks, base = [], 0
    for source in range(len(sources)):
        rows = sources[source].shape[0]
        for start in range(0, rows, size):
            chunks.append((source, start, base + start))
        base += rows
    return chunks


def attend_kernel(own_ref, other_ref, bias_ref, out_ref, exp_ref, inv_ref, score_ref, *, heads, frames, chunk):
    dim = own_ref.shape[1] // (3 * heads)
    wide = heads * dim
    sources = (own_ref, other_ref)
    chunks = key_chunks(sources, chunk)
    outs = []
    for head in range(heads):
        at = head * dim
        query = own_ref[0:frames, 2 * wide + at:2 * wide + at + dim] * (dim ** -0.5)
        lane = lax.broadcasted_iota(jnp.int32, (frames, dim), 1)
        query = jnp.concatenate([query.astype(BF16), (lane == 0).astype(BF16)], 1)
        top = None
        for source, start, row in chunks:
            key = sources[source][start:start + chunk, at:at + dim]
            key = jnp.concatenate([key, bias_ref[row:row + chunk, :]], 1)
            score = dot(key, query, NT)
            score_ref[row:row + chunk, :] = score
            part = jnp.max(score, 0, keepdims=True)
            top = part if top is None else jnp.maximum(top, part)
        total = None
        for source, start, row in chunks:
            weight = jnp.exp(score_ref[row:row + chunk, :] - top).astype(BF16)
            exp_ref[head, row:row + chunk, :] = weight
            value = sources[source][start:start + chunk, wide + at:wide + at + dim]
            value = jnp.concatenate([value, jnp.ones_like(value)], 1)
            part = dot(value, weight, TN)
            total = part if total is None else total + part
        inverse = 1.0 / total[dim:dim + 1, :]
        inv_ref[head:head + 1, :] = inverse
        outs.append((total[0:dim, :] * inverse).T)
    out_ref[...] = jnp.concatenate(outs, 1).astype(BF16)


def attend(own, other, bias, heads, frames):
    keys = own.shape[0] + other.shape[0]
    wide = own.shape[1] // 3
    chunk = min(256, frames)
    if own.shape[0] % chunk:
        chunk = frames
    return pl.pallas_call(
        functools.partial(attend_kernel, heads=heads, frames=frames, chunk=chunk),
        out_shape=(
            jax.ShapeDtypeStruct((frames, wide), BF16),
            jax.ShapeDtypeStruct((heads, keys, frames), BF16),
            jax.ShapeDtypeStruct((heads, frames), F32),
        ),
        scratch_shapes=[pltpu.VMEM((keys, frames), F32)],
        compiler_params=pltpu.CompilerParams(vmem_limit_bytes=40 * 2**20),
        cost_estimate=pl.CostEstimate(
            flops=16 * keys * frames * wide, bytes_accessed=2 * heads * keys * frames, transcendentals=heads * keys * frames
        ),
        name="attend",
    )(own, other, bias)


def attend_back_kernel(own_ref, other_ref, exp_ref, inv_ref, dout_ref, dq_ref, down_ref, dother_ref, prod_ref, *, heads, frames, chunk):
    dim = own_ref.shape[1] // (3 * heads)
    wide = heads * dim
    scale = dim ** -0.5
    sources = (own_ref, other_ref)
    chunks = key_chunks(sources, chunk)
    dqs = []
    dks, dvs = [[] for _ in chunks], [[] for _ in chunks]
    for head in range(heads):
        at = head * dim
        query = (own_ref[0:frames, 2 * wide + at:2 * wide + at + dim] * scale).astype(BF16)
        inverse = inv_ref[head:head + 1, :]
        dout_t = dout_ref[:, at:at + dim].astype(F32).T * inverse
        dout = dout_t.T.astype(BF16)
        dout_t = dout_t.astype(BF16)
        delta = None
        for index, (source, start, row) in enumerate(chunks):
            value = sources[source][start:start + chunk, wide + at:wide + at + dim]
            weight = exp_ref[head, row:row + chunk, :]
            prod = dot(value, dout_t) * weight.astype(F32)
            prod_ref[row:row + chunk, :] = prod
            part = jnp.sum(prod, 0, keepdims=True)
            delta = part if delta is None else delta + part
            dvs[index].append(dot(weight, dout))
        delta = delta * inverse
        dq_t = None
        for index, (source, start, row) in enumerate(chunks):
            key = sources[source][start:start + chunk, at:at + dim]
            weight = exp_ref[head, row:row + chunk, :].astype(F32)
            ds = (prod_ref[row:row + chunk, :] - weight * delta).astype(BF16)
            dks[index].append(dot(ds, query))
            part = dot(key, ds, TN)
            dq_t = part if dq_t is None else dq_t + part
        dqs.append(dq_t.T * scale)
    dq_ref[...] = jnp.concatenate(dqs, 1).astype(BF16)
    for index, (source, start, row) in enumerate(chunks):
        target = down_ref if source == 0 else dother_ref
        target[start:start + chunk, :] = jnp.concatenate(dks[index] + dvs[index], 1).astype(BF16)


def attend_back(own, other, weights, inverse, dout, heads, frames):
    keys = own.shape[0] + other.shape[0]
    wide = own.shape[1] // 3
    chunk = min(256, frames)
    if own.shape[0] % chunk:
        chunk = frames
    return pl.pallas_call(
        functools.partial(attend_back_kernel, heads=heads, frames=frames, chunk=chunk),
        out_shape=(
            jax.ShapeDtypeStruct((frames, wide), BF16),
            jax.ShapeDtypeStruct((own.shape[0], 2 * wide), BF16),
            jax.ShapeDtypeStruct((other.shape[0], 2 * wide), BF16),
        ),
        scratch_shapes=[pltpu.VMEM((keys, frames), F32)],
        compiler_params=pltpu.CompilerParams(vmem_limit_bytes=40 * 2**20),
        cost_estimate=pl.CostEstimate(
            flops=32 * keys * frames * wide, bytes_accessed=2 * heads * keys * frames, transcendentals=0
        ),
        name="attend_back",
    )(own, other, weights, inverse, dout)


def up_kernel(in_ref, weight_ref, bias_ref, act_ref, slope_ref):
    up = dot(in_ref[...], weight_ref[...]) + bias_ref[...]
    cdf = 0.5 + 0.5 * lax.erf(up * (0.5 ** 0.5))
    pdf = jnp.exp(-0.5 * up * up) * 0.3989422804014327
    act_ref[...] = (up * cdf).astype(BF16)
    slope_ref[...] = (cdf + up * pdf).astype(BF16)


def up_gelu(values, weight, bias):
    rows, depth = values.shape
    columns = weight.shape[1]
    tile = 256 if columns % 256 == 0 else columns
    return pl.pallas_call(
        up_kernel,
        grid=(columns // tile,),
        in_specs=[
            pl.BlockSpec((rows, depth), lambda i: (0, 0)),
            pl.BlockSpec((depth, tile), lambda i: (0, i)),
            pl.BlockSpec((1, tile), lambda i: (0, i)),
        ],
        out_specs=[pl.BlockSpec((rows, tile), lambda i: (0, i))] * 2,
        out_shape=[jax.ShapeDtypeStruct((rows, columns), BF16)] * 2,
        compiler_params=pltpu.CompilerParams(vmem_limit_bytes=32 * 2**20),
        cost_estimate=pl.CostEstimate(
            flops=2 * rows * depth * columns, bytes_accessed=2 * (rows * depth + depth * columns + 2 * rows * columns),
            transcendentals=2 * rows * columns,
        ),
        name="up_gelu",
    )(values, weight, bias)


def across(block, bit):
    count = lax.axis_size("replica")
    return lax.ppermute(block, "replica", [(i, i ^ bit) for i in range(count)])


def swap_sections(block):
    return lax.ppermute(block, "section", [(0, 1), (1, 0)])


def transposed(block, source, target):
    shards, replicas = lax.axis_size("shard"), lax.axis_size("replica")

    def flat(section, shard, replica):
        return (section * shards + shard) * replicas + replica

    route = []
    for shard in range(shards):
        for replica in range(replicas):
            group, place = divmod(replica, shards)
            here, there = (shard, replica), (place, group * shards + shard)
            if source is None:
                route += [(flat(s, *here), flat(s, *there)) for s in range(2)]
            else:
                route.append((flat(source, *here), flat(target, *there)))
    return lax.ppermute(block, AXES, route)


def in_order(pieces, quarter):
    odd, high = (quarter & 1) == 1, (quarter & 2) == 2
    a, b, c, d = pieces
    a, b, c, d = jnp.where(odd, b, a), jnp.where(odd, a, b), jnp.where(odd, d, c), jnp.where(odd, c, d)
    return jnp.where(high, c, a), jnp.where(high, d, b), jnp.where(high, a, c), jnp.where(high, b, d)


def after(value, *others):
    return lax.optimization_barrier((value, others))[0]


def spread(piece, far):
    return piece, across(piece, 1), far, across(far, 1)


def low_sum(*parts):
    total = parts[0].astype(F32)
    for part in parts[1:]:
        total = total + part.astype(F32)
    return total.astype(BF16)


def body(edges, attn_in, attn_out, mlp_up, mlp_down, vectors, key_mask):
    section = lax.axis_index("section")
    first = section == 0
    replica = lax.axis_index("replica")
    shards, replicas = lax.axis_size("shard"), lax.axis_size("replica")
    quarter = replica % QUARTERS
    edges_here = edges[0]
    clips, frames, width = edges_here.shape
    hidden = mlp_up.shape[2]
    dim = width // H
    heads = H // QUARTERS
    wide = heads * dim
    unit = hidden // (shards * QUARTERS)
    rows = attn_in.shape[1]
    assert clips == 2 and lax.axis_size("section") == 2 and replicas % shards == 0 and replicas % QUARTERS == 0

    inputs = jnp.where(first, transposed(edges_here[0], 0, 0), transposed(edges_here[1], 0, 1))
    mask_row = transposed(
        lax.dynamic_index_in_dim(key_mask, section, 0, keepdims=False).astype(F32)[None], None, None
    )[0]

    def pick(block, axis):
        return lax.dynamic_index_in_dim(block, quarter, axis, keepdims=False)

    def gathered(block):
        return lax.all_gather(block, "shard", axis=0, tiled=True)

    def by_layer(own, other):
        return jnp.where(first, own, other), jnp.where(first, other, own)

    query_in, key_in, value_in = (
        pick(attn_in[0][:, i * width:(i + 1) * width].reshape(rows, QUARTERS, wide), 1) for i in range(3)
    )
    own_proj = jnp.concatenate(
        [key_in, value_in, query_in, pick(attn_out[0].reshape(rows, QUARTERS, width // QUARTERS), 1)], 1
    )
    own_up = pick(mlp_up[0].reshape(rows, shards, QUARTERS, unit), 2).reshape(rows, shards * unit)
    own_down = pick(mlp_down[0].reshape(QUARTERS, unit, width), 0)
    proj_zero, proj_one = by_layer(own_proj, swap_sections(own_proj))
    vec_by_layer = by_layer(vectors[0], swap_sections(vectors[0]))
    proj_zero = gathered(proj_zero)
    own_up = gathered(after(own_up, proj_zero))
    own_down = gathered(after(own_down, own_up))
    proj_one = gathered(after(proj_one, own_down))
    up_zero, up_one = by_layer(own_up, swap_sections(own_up))
    down_zero, down_one = by_layer(own_down, swap_sections(own_down))
    far = [across(proj_zero, 2)]
    far.append(across(up_zero, 2))
    far.append(across(after(down_zero, far[1]), 2))
    far.append(across(after(proj_one, far[2]), 2))
    far.append(across(after(up_one, far[2]), 2))
    far.append(across(after(down_one, far[3], far[4]), 2))
    blocks = (proj_zero, up_zero, down_zero, proj_one, up_one, down_one)
    blocks = [spread(block, other) for block, other in zip(blocks, far)]
    layers = []
    for layer in range(2):
        proj, up, down = blocks[3 * layer:3 * layer + 3]
        w_out = jnp.concatenate(in_order([piece[:, 3 * wide:] for piece in proj], quarter), 1)
        layers.append((proj, w_out, up, down, vec_by_layer[layer]))

    members = [0]
    bit = 2
    while bit < shards:
        members = members + [m ^ bit for m in members]
        bit *= 2
    members = members + [m ^ 1 for m in members]
    place = replica % shards
    bias_row = jnp.concatenate(
        [lax.dynamic_slice_in_dim(mask_row, (place ^ m) * frames, frames, 0) for m in members]
    )
    bias_row = jnp.where(bias_row > 0, 0.0, MASKED).astype(BF16)
    lane = jnp.arange(dim)[None, :]
    key_bias = jnp.where(lane == 0, bias_row[:, None], jnp.zeros((), BF16))

    def chips_rows(block):
        bit = 2
        while bit < shards:
            block = jnp.concatenate([block, across(block, bit)], 0)
            bit *= 2
        return block

    def forward(x_low, layer):
        proj, w_out, w_up, w_down, vec = layers[layer]
        x_set = chips_rows(x_low)
        normed = layer_norm(x_set.astype(F32), vec[0], vec[1]).astype(BF16)
        zeros = jnp.zeros((QUARTERS, wide), F32)
        bias_in = jnp.stack([zeros, vec[3].reshape(QUARTERS, wide), vec[2].reshape(QUARTERS, wide)], 1)
        own_qkv, other_kv = [], [None] * QUARTERS
        for p in range(QUARTERS):
            bias = lax.dynamic_index_in_dim(bias_in, quarter ^ p, 0, keepdims=False).reshape(3 * wide)
            own_qkv.append((dot(normed, proj[p][:, :3 * wide]) + bias).astype(BF16))
            other_kv[p ^ 1] = across(own_qkv[p][:, :2 * wide], 1)
        outs, weights, inverses = [], [], []
        for p in range(QUARTERS):
            out, weight, inverse = attend(own_qkv[p], other_kv[p], key_bias, heads, frames)
            outs.append(out)
            weights.append(weight)
            inverses.append(inverse)
        attended = jnp.concatenate(in_order(outs, quarter), 1)
        x = x_low.astype(F32)
        middle = x + dot(attended, w_out) + vec[4]
        normed_two = layer_norm(middle, vec[5], vec[6]).astype(BF16)
        bias_up = vec[8:].reshape(shards, QUARTERS, unit)
        acts, slopes = [], []
        result = middle + vec[7]
        for p in range(QUARTERS):
            bias = lax.dynamic_index_in_dim(bias_up, quarter ^ p, 1, keepdims=False).reshape(1, shards * unit)
            act, slope = up_gelu(normed_two, w_up[p], bias)
            acts.append(act)
            slopes.append(slope)
            result = result + dot(act, w_down[p])
        kept = (x, normed, own_qkv, other_kv, weights, inverses, attended, middle, normed_two, acts, slopes)
        return result.astype(BF16), kept

    def norm_back(values, gain, grad):
        center = values - jnp.mean(values, -1, keepdims=True)
        inv = lax.rsqrt(jnp.mean(center * center, -1, keepdims=True) + EPS)
        unit_values = center * inv
        scaled = grad * gain
        back = inv * (
            scaled - jnp.mean(scaled, -1, keepdims=True)
            - unit_values * jnp.mean(scaled * unit_values, -1, keepdims=True)
        )
        return back, jnp.sum(grad * unit_values, 0), jnp.sum(grad, 0)

    def scattered(block):
        bit = QUARTERS
        while bit < replicas:
            block = low_sum(block, across(block, bit))
            bit *= 2
        return lax.psum_scatter(block, "shard", scatter_dimension=0, tiled=True)

    def half_sum(block):
        cut = block.shape[1] // 2
        left, right = block[:, :cut], block[:, cut:]
        return low_sum(jnp.where(first, left, right), swap_sections(jnp.where(first, right, left)))

    def backward(cot, layer, kept, pending):
        proj, w_out, w_up, w_down, vec = layers[layer]
        x, normed, own_qkv, other_kv, weights, inverses, attended, middle, normed_two, acts, slopes = kept
        d_mlp = cot.astype(BF16)
        up_sums, d_ups = [], []
        d_normed_two = None
        for p in range(QUARTERS):
            d_up = (dot(d_mlp, w_down[p], NT) * slopes[p].astype(F32)).astype(BF16)
            part = dot(d_up, w_up[p], NT)
            d_normed_two = part if d_normed_two is None else d_normed_two + part
            d_ups.append(d_up)
            up_sums.append(jnp.sum(d_up.astype(F32), 0))
        near_down = [across(dot(acts[p], d_mlp, TN).astype(BF16), 1) for p in (1, 3)]
        near_up = [across(dot(normed_two, d_ups[p], TN).astype(BF16), 1) for p in (1, 3)]
        above = None
        back, g_gain_two, g_shift_two = norm_back(middle, vec[5], d_normed_two)
        d_middle = cot + back
        d_attn = d_middle.astype(BF16)
        d_attn_parts = in_order([d_attn[:, p * wide:(p + 1) * wide] for p in range(QUARTERS)], quarter)
        d_attended = dot(d_attn, w_out, NT).astype(BF16)
        d_heads = in_order([d_attended[:, p * wide:(p + 1) * wide] for p in range(QUARTERS)], quarter)

        far_down = low_sum(dot(acts[2], d_mlp, TN), near_down[1])
        far_down = across(far_down, 2)
        results = []
        for p in range(QUARTERS):
            head = d_heads[p]
            if p == 0:
                head = after(head, *near_down)
            elif p == 1:
                head = after(head, *near_up)
            elif pending is not None:
                head = after(head, pending[p - 2][1])
            results.append(attend_back(own_qkv[p], other_kv[p], weights[p], inverses[p], head, heads, frames))
        d_normed, d_normed_own = None, None
        d_boths, sums_in = [], []
        for p in range(QUARTERS):
            d_query = results[p][0]
            d_both = low_sum(results[p][1], across(results[p ^ 1][2], 1))
            d_boths.append(d_both)
            part = dot(d_both, proj[p][:, :2 * wide], NT)
            d_normed = part if d_normed is None else d_normed + part
            part = dot(d_query, proj[p][:, 2 * wide:3 * wide], NT)
            d_normed_own = part if d_normed_own is None else d_normed_own + part
            sums_in.append((jnp.sum(d_query.astype(F32), 0), jnp.sum(d_both[:, wide:].astype(F32), 0)))

        def g_proj(p):
            return jnp.concatenate(
                [
                    dot(normed, d_boths[p], TN), dot(normed[:frames], results[p][0], TN),
                    dot(attended, d_attn_parts[p], TN),
                ],
                1,
            )

        block = d_normed
        if pending is not None:
            halves = [half_sum(make(far)) for make, far in pending]
            block = after(block, *halves)
            above = scattered(jnp.concatenate(halves, 1))
        bit = shards // 2
        while bit >= 2:
            cut = block.shape[0] // 2
            block = block[:cut] + across(block[cut:].astype(BF16), bit).astype(F32)
            bit //= 2
        near_proj = [across(g_proj(p).astype(BF16), 1) for p in (1, 3)]
        far_up = low_sum(dot(after(normed_two, block), d_ups[2], TN), near_up[1])
        far_up = across(far_up, 2)
        block = after(block, far_down)
        down_done = scattered(half_sum(low_sum(dot(acts[0], d_mlp, TN), near_down[0], far_down)))
        far_proj = across(low_sum(g_proj(2), near_proj[1]), 2)
        back, g_gain_one, g_shift_one = norm_back(x, vec[0], block + d_normed_own)
        g_x = d_middle + back
        sum_query = jnp.concatenate(in_order([s[0] for s in sums_in], quarter))
        sum_value = jnp.concatenate(in_order([s[1] for s in sums_in], quarter))
        sum_up = jnp.stack(in_order([s.reshape(shards, unit) for s in up_sums], quarter), 1).reshape(-1, width)
        g_vec = jnp.concatenate(
            [
                jnp.stack(
                    [
                        g_gain_one, g_shift_one, sum_query, sum_value,
                        jnp.sum(d_attn.astype(F32), 0), g_gain_two, g_shift_two,
                        jnp.sum(d_mlp.astype(F32), 0),
                    ]
                ),
                sum_up,
            ]
        )

        def finish_proj(other):
            return low_sum(g_proj(0), near_proj[0], other)

        def finish_up(other):
            return low_sum(dot(normed_two, d_ups[0], TN), near_up[0], other)

        return g_x, down_done, ((finish_up, far_up), (finish_proj, far_proj)), above, g_vec

    x_one, kept_zero = forward(inputs, 0)
    y_one, kept_one = forward(x_one, 1)
    cot = jnp.where(first, transposed(edges_here[0], 1, 0), transposed(edges_here[1], 1, 1))
    out_slots = [transposed(y_one, 0, 1), transposed(y_one, 1, 1)]
    g_one, down_one, pending, _, vec_one = backward(cot.astype(F32), 1, kept_one, None)
    g_zero, down_zero, pending, rest_one, vec_zero = backward(
        g_one.astype(BF16).astype(F32), 0, kept_zero, pending
    )
    g_low = g_zero.astype(BF16)
    back_slots = [transposed(g_low, 0, 0), transposed(g_low, 1, 0)]
    edges_out = jnp.stack([jnp.where(first, b, o) for b, o in zip(back_slots, out_slots)])
    vec_all = lax.psum(after(jnp.concatenate([vec_zero, vec_one]), rest_one, down_one), AXES)
    rest_zero = jnp.concatenate([half_sum(make(far)) for make, far in pending], 1)
    rest_zero = scattered(after(rest_zero, down_zero))
    vec_all = jnp.where(first, vec_all[:12], vec_all[12:])
    slice_width = width // shards
    g_vectors = lax.dynamic_slice_in_dim(vec_all, lax.axis_index("shard") * slice_width, slice_width, 1)

    def finished(zero, one):
        own, other = jnp.where(first, zero, one), swap_sections(jnp.where(first, one, zero))
        cut = width // 2
        parts = []
        for start in range(0, own.shape[1], cut):
            a, b = own[:, start:start + cut], other[:, start:start + cut]
            parts += [jnp.where(first, a, b), jnp.where(first, b, a)]
        part = jnp.concatenate(parts, 1)
        return in_order(spread(part, across(part, 2)), quarter)

    f_down = jnp.stack(finished(down_zero, down_one)).astype(F32).reshape(-1, width)
    f_rest = finished(rest_zero, rest_one)
    f_up = jnp.stack([piece[:, :shards * unit].reshape(rows, shards, unit) for piece in f_rest], 2)
    f_up = f_up.astype(F32).reshape(rows, hidden)
    f_proj = [piece[:, shards * unit:] for piece in f_rest]
    f_in = jnp.concatenate(
        [piece[:, i * wide:(i + 1) * wide] for i in (2, 0, 1) for piece in f_proj], 1
    ).astype(F32)
    f_out = jnp.concatenate([piece[:, 3 * wide:] for piece in f_proj], 1).astype(F32)
    return edges_out[None], f_in[None], f_out[None], f_up[None], f_down[None], g_vectors[None]


def solution(mesh):
    placed = (
        P("section", "replica", "shard", None),
        P("section", "shard", None),
        P("section", "shard", None),
        P("section", "shard", None),
        P("section", "shard", None),
        P("section", None, None),
        P("replica", None),
    )
    return jax.shard_map(
        body,
        mesh=mesh,
        in_specs=placed,
        out_specs=(
            P("section", "replica", "shard", None),
            P("section", "shard", None),
            P("section", "shard", None),
            P("section", "shard", None),
            P("section", "shard", None),
            P("section", None, "shard"),
        ),
        check_vma=False,
    )
```

```python
import functools
import math

import jax
import jax.numpy as jnp
from jax import lax
from jax.experimental import pallas as pl
from jax.experimental.pallas import tpu as pltpu
from jax.sharding import PartitionSpec as P

H = 12
EPS = 1e-05
MASKED = -1e30
QUARTERS = 4
BF16 = jnp.bfloat16
F32 = jnp.float32
AXES = ("section", "shard", "replica")
NN = (((1,), (0,)), ((), ()))
NT = (((1,), (1,)), ((), ()))
TN = (((0,), (0,)), ((), ()))


def dot(a, b, dims=NN):
    return lax.dot_general(a, b, dims, preferred_element_type=F32)


def layer_norm(values, gain, shift):
    center = values - jnp.mean(values, -1, keepdims=True)
    spread = jnp.mean(center * center, -1, keepdims=True)
    return center * lax.rsqrt(spread + EPS) * gain + shift


def key_chunks(sources, size):
    chunks, base = [], 0
    for source in range(len(sources)):
        rows = sources[source].shape[0]
        for start in range(0, rows, size):
            chunks.append((source, start, base + start))
        base += rows
    return chunks


def attend_kernel(own_ref, other_ref, bias_ref, out_ref, exp_ref, inv_ref, score_ref, *, heads, frames, chunk):
    dim = own_ref.shape[1] // (3 * heads)
    wide = heads * dim
    sources = (own_ref, other_ref)
    chunks = key_chunks(sources, chunk)
    outs = []
    for head in range(heads):
        at = head * dim
        query = own_ref[0:frames, 2 * wide + at:2 * wide + at + dim] * (dim ** -0.5)
        lane = lax.broadcasted_iota(jnp.int32, (frames, dim), 1)
        query = jnp.concatenate([query.astype(BF16), (lane == 0).astype(BF16)], 1)
        top = None
        for source, start, row in chunks:
            key = sources[source][start:start + chunk, at:at + dim]
            key = jnp.concatenate([key, bias_ref[row:row + chunk, :]], 1)
            score = dot(key, query, NT)
            score_ref[row:row + chunk, :] = score
            part = jnp.max(score, 0, keepdims=True)
            top = part if top is None else jnp.maximum(top, part)
        total = None
        for source, start, row in chunks:
            weight = jnp.exp(score_ref[row:row + chunk, :] - top).astype(BF16)
            exp_ref[head, row:row + chunk, :] = weight
            value = sources[source][start:start + chunk, wide + at:wide + at + dim]
            value = jnp.concatenate([value, jnp.ones_like(value)], 1)
            part = dot(value, weight, TN)
            total = part if total is None else total + part
        inverse = 1.0 / total[dim:dim + 1, :]
        inv_ref[head:head + 1, :] = inverse
        outs.append((total[0:dim, :] * inverse).T)
    out_ref[...] = jnp.concatenate(outs, 1).astype(BF16)


def attend(own, other, bias, heads, frames):
    keys = own.shape[0] + other.shape[0]
    wide = own.shape[1] // 3
    chunk = min(256, frames)
    if own.shape[0] % chunk:
        chunk = frames
    return pl.pallas_call(
        functools.partial(attend_kernel, heads=heads, frames=frames, chunk=chunk),
        out_shape=(
            jax.ShapeDtypeStruct((frames, wide), BF16),
            jax.ShapeDtypeStruct((heads, keys, frames), BF16),
            jax.ShapeDtypeStruct((heads, frames), F32),
        ),
        scratch_shapes=[pltpu.VMEM((keys, frames), F32)],
        compiler_params=pltpu.CompilerParams(vmem_limit_bytes=40 * 2**20),
        cost_estimate=pl.CostEstimate(
            flops=16 * keys * frames * wide, bytes_accessed=2 * heads * keys * frames, transcendentals=heads * keys * frames
        ),
        name="attend",
    )(own, other, bias)


def attend_back_kernel(own_ref, other_ref, exp_ref, inv_ref, dout_ref, dq_ref, down_ref, dother_ref, prod_ref, *, heads, frames, chunk):
    dim = own_ref.shape[1] // (3 * heads)
    wide = heads * dim
    scale = dim ** -0.5
    sources = (own_ref, other_ref)
    chunks = key_chunks(sources, chunk)
    dqs = []
    dks, dvs = [[] for _ in chunks], [[] for _ in chunks]
    for head in range(heads):
        at = head * dim
        query = (own_ref[0:frames, 2 * wide + at:2 * wide + at + dim] * scale).astype(BF16)
        inverse = inv_ref[head:head + 1, :]
        dout_t = dout_ref[:, at:at + dim].astype(F32).T * inverse
        dout = dout_t.T.astype(BF16)
        dout_t = dout_t.astype(BF16)
        delta = None
        for index, (source, start, row) in enumerate(chunks):
            value = sources[source][start:start + chunk, wide + at:wide + at + dim]
            weight = exp_ref[head, row:row + chunk, :]
            prod = dot(value, dout_t) * weight.astype(F32)
            prod_ref[row:row + chunk, :] = prod
            part = jnp.sum(prod, 0, keepdims=True)
            delta = part if delta is None else delta + part
            dvs[index].append(dot(weight, dout))
        delta = delta * inverse
        dq_t = None
        for index, (source, start, row) in enumerate(chunks):
            key = sources[source][start:start + chunk, at:at + dim]
            weight = exp_ref[head, row:row + chunk, :].astype(F32)
            ds = (prod_ref[row:row + chunk, :] - weight * delta).astype(BF16)
            dks[index].append(dot(ds, query))
            part = dot(key, ds, TN)
            dq_t = part if dq_t is None else dq_t + part
        dqs.append(dq_t.T * scale)
    dq_ref[...] = jnp.concatenate(dqs, 1).astype(BF16)
    for index, (source, start, row) in enumerate(chunks):
        target = down_ref if source == 0 else dother_ref
        target[start:start + chunk, :] = jnp.concatenate(dks[index] + dvs[index], 1).astype(BF16)


def attend_back(own, other, weights, inverse, dout, heads, frames):
    keys = own.shape[0] + other.shape[0]
    wide = own.shape[1] // 3
    chunk = min(256, frames)
    if own.shape[0] % chunk:
        chunk = frames
    return pl.pallas_call(
        functools.partial(attend_back_kernel, heads=heads, frames=frames, chunk=chunk),
        out_shape=(
            jax.ShapeDtypeStruct((frames, wide), BF16),
            jax.ShapeDtypeStruct((own.shape[0], 2 * wide), BF16),
            jax.ShapeDtypeStruct((other.shape[0], 2 * wide), BF16),
        ),
        scratch_shapes=[pltpu.VMEM((keys, frames), F32)],
        compiler_params=pltpu.CompilerParams(vmem_limit_bytes=40 * 2**20),
        cost_estimate=pl.CostEstimate(
            flops=32 * keys * frames * wide, bytes_accessed=2 * heads * keys * frames, transcendentals=0
        ),
        name="attend_back",
    )(own, other, weights, inverse, dout)


def column_tile(columns):
    return 256 if columns % 256 == 0 else columns


def mlp_kernel(in_ref, up_ref, bias_ref, down_ref, before_ref, act_ref, slope_ref, sum_ref):
    up = dot(in_ref[...], up_ref[...]) + bias_ref[...]
    cdf = 0.5 + 0.5 * lax.erf(up * (0.5 ** 0.5))
    pdf = jnp.exp(-0.5 * up * up) * 0.3989422804014327
    act = (up * cdf).astype(BF16)
    act_ref[...] = act
    slope_ref[...] = (cdf + up * pdf).astype(BF16)
    part = dot(act, down_ref[...])

    @pl.when(pl.program_id(0) == 0)
    def _():
        sum_ref[...] = before_ref[...] + part

    @pl.when(pl.program_id(0) > 0)
    def _():
        sum_ref[...] += part


def mlp_part(values, up, bias, down, before):
    rows, depth = values.shape
    columns = up.shape[1]
    tile = column_tile(columns)
    whole = pl.BlockSpec((rows, depth), lambda i: (0, 0))
    hidden = pl.BlockSpec((rows, tile), lambda i: (0, i))
    return pl.pallas_call(
        mlp_kernel,
        grid=(columns // tile,),
        in_specs=[
            whole,
            pl.BlockSpec((depth, tile), lambda i: (0, i)),
            pl.BlockSpec((1, tile), lambda i: (0, i)),
            pl.BlockSpec((tile, depth), lambda i: (i, 0)),
            whole,
        ],
        out_specs=[hidden, hidden, whole],
        out_shape=[
            jax.ShapeDtypeStruct((rows, columns), BF16),
            jax.ShapeDtypeStruct((rows, columns), BF16),
            jax.ShapeDtypeStruct((rows, depth), F32),
        ],
        compiler_params=pltpu.CompilerParams(vmem_limit_bytes=32 * 2**20),
        cost_estimate=pl.CostEstimate(
            flops=4 * rows * depth * columns, bytes_accessed=4 * (3 * rows * depth + depth * columns + rows * columns),
            transcendentals=2 * rows * columns,
        ),
        name="mlp_part",
    )(values, up, bias, down, before)


def mlp_back_kernel(grad_ref, in_ref, act_ref, slope_ref, up_ref, down_ref, before_ref, gd_ref, gu_ref, row_ref, sum_ref):
    grad = grad_ref[...]
    d_up = (dot(grad, down_ref[...], NT) * slope_ref[...].astype(F32)).astype(BF16)
    gd_ref[...] = dot(act_ref[...], grad, TN).astype(BF16)
    gu_ref[...] = dot(in_ref[...], d_up, TN).astype(BF16)
    row_ref[...] = jnp.sum(d_up.astype(F32), 0, keepdims=True)
    part = dot(d_up, up_ref[...], NT)

    @pl.when(pl.program_id(0) == 0)
    def _():
        sum_ref[...] = before_ref[...] + part

    @pl.when(pl.program_id(0) > 0)
    def _():
        sum_ref[...] += part


def mlp_back_part(grad, values, act, slope, up, down, before):
    rows, depth = values.shape
    columns = up.shape[1]
    tile = column_tile(columns)
    whole = pl.BlockSpec((rows, depth), lambda i: (0, 0))
    hidden = pl.BlockSpec((rows, tile), lambda i: (0, i))
    up_tile = pl.BlockSpec((depth, tile), lambda i: (0, i))
    down_tile = pl.BlockSpec((tile, depth), lambda i: (i, 0))
    return pl.pallas_call(
        mlp_back_kernel,
        grid=(columns // tile,),
        in_specs=[whole, whole, hidden, hidden, up_tile, down_tile, whole],
        out_specs=[down_tile, up_tile, pl.BlockSpec((1, tile), lambda i: (0, i)), whole],
        out_shape=[
            jax.ShapeDtypeStruct((columns, depth), BF16),
            jax.ShapeDtypeStruct((depth, columns), BF16),
            jax.ShapeDtypeStruct((1, columns), F32),
            jax.ShapeDtypeStruct((rows, depth), F32),
        ],
        compiler_params=pltpu.CompilerParams(vmem_limit_bytes=40 * 2**20),
        cost_estimate=pl.CostEstimate(
            flops=8 * rows * depth * columns, bytes_accessed=4 * (3 * rows * depth + 2 * depth * columns + rows * columns),
            transcendentals=0,
        ),
        name="mlp_back_part",
    )(grad, values, act, slope, up, down, before)


def proj_back_kernel(in_ref, own_ref, other_ref, query_ref, out_ref, grad_ref, weight_ref, before_ref, g_ref, row_ref, sum_ref):
    frames, wide = query_ref.shape
    both = (own_ref[...].astype(F32) + other_ref[...].astype(F32)).astype(BF16)
    query = query_ref[...]
    values = in_ref[...]
    g_ref[...] = jnp.concatenate(
        [dot(values, both, TN), dot(values[:frames], query, TN), dot(out_ref[...], grad_ref[...], TN)], 1
    ).astype(BF16)
    row_ref[...] = jnp.concatenate(
        [jnp.sum(both.astype(F32), 0, keepdims=True), jnp.sum(query.astype(F32), 0, keepdims=True)], 1
    )
    total = before_ref[...] + dot(both, weight_ref[:, :2 * wide], NT)
    own = total[:frames] + dot(query, weight_ref[:, 2 * wide:3 * wide], NT)
    sum_ref[0:frames, :] = own
    sum_ref[frames:, :] = total[frames:]


def proj_back(values, own, other, query, out, grad, weight, before):
    rows, depth = values.shape
    wide = query.shape[1]
    return pl.pallas_call(
        proj_back_kernel,
        out_shape=[
            jax.ShapeDtypeStruct(weight.shape, BF16),
            jax.ShapeDtypeStruct((1, 3 * wide), F32),
            jax.ShapeDtypeStruct((rows, depth), F32),
        ],
        compiler_params=pltpu.CompilerParams(vmem_limit_bytes=40 * 2**20),
        cost_estimate=pl.CostEstimate(
            flops=8 * rows * depth * 2 * wide, bytes_accessed=12 * rows * depth + 4 * depth * weight.shape[1],
            transcendentals=0,
        ),
        name="proj_back",
    )(values, own, other, query, out, grad, weight, before)


def place_proj_kernel(quarter_ref, in_ref, qkv_ref, out_ref):
    pieces = [in_ref[place ^ quarter_ref[0]].astype(F32) for place in range(QUARTERS)]
    wide = pieces[0].shape[1] // 4
    width = QUARTERS * wide
    for column, part in ((0, 2), (1, 0), (2, 1)):
        qkv_ref[:, column * width:(column + 1) * width] = jnp.concatenate(
            [piece[:, part * wide:(part + 1) * wide] for piece in pieces], 1
        )
    out_ref[...] = jnp.concatenate([piece[:, 3 * wide:] for piece in pieces], 1)


def place_mlp_kernel(quarter_ref, in_ref, down_ref, up_ref, *, shards):
    pieces = [in_ref[place ^ quarter_ref[0]].astype(F32) for place in range(QUARTERS)]
    rows, width = pieces[0].shape[0], pieces[0].shape[1] // 2
    unit = width // shards
    for place in range(QUARTERS):
        down_ref[place * rows:(place + 1) * rows, :] = pieces[place][:, :width]
    for shard in range(shards):
        start = width + shard * unit
        up_ref[:, shard * QUARTERS * unit:(shard + 1) * QUARTERS * unit] = jnp.concatenate(
            [piece[:, start:start + unit] for piece in pieces], 1
        )


def placed_parts(kernel, quarter, pieces, shapes):
    stacked = jnp.stack(pieces)
    size = sum(math.prod(shape) for shape in shapes)
    return pl.pallas_call(
        kernel,
        in_specs=[pl.BlockSpec(memory_space=pltpu.SMEM), pl.BlockSpec(memory_space=pltpu.VMEM)],
        out_shape=[jax.ShapeDtypeStruct(shape, F32) for shape in shapes],
        compiler_params=pltpu.CompilerParams(vmem_limit_bytes=32 * 2**20),
        cost_estimate=pl.CostEstimate(flops=size, bytes_accessed=6 * size, transcendentals=0),
        name="placed_parts",
    )(quarter.reshape(1), stacked)


def across(block, bit):
    count = lax.axis_size("replica")
    return lax.ppermute(block, "replica", [(i, i ^ bit) for i in range(count)])


def swap_sections(block):
    return lax.ppermute(block, "section", [(0, 1), (1, 0)])


def transposed(block, source, target):
    shards, replicas = lax.axis_size("shard"), lax.axis_size("replica")

    def flat(section, shard, replica):
        return (section * shards + shard) * replicas + replica

    route = []
    for shard in range(shards):
        for replica in range(replicas):
            group, place = divmod(replica, shards)
            here, there = (shard, replica), (place, group * shards + shard)
            if source is None:
                route += [(flat(s, *here), flat(s, *there)) for s in range(2)]
            else:
                route.append((flat(source, *here), flat(target, *there)))
    return lax.ppermute(block, AXES, route)


def in_order(pieces, quarter):
    odd, high = (quarter & 1) == 1, (quarter & 2) == 2
    a, b, c, d = pieces
    a, b, c, d = jnp.where(odd, b, a), jnp.where(odd, a, b), jnp.where(odd, d, c), jnp.where(odd, c, d)
    return jnp.where(high, c, a), jnp.where(high, d, b), jnp.where(high, a, c), jnp.where(high, b, d)


def after(value, *others):
    return lax.optimization_barrier((value, others))[0]


def spread(piece, far):
    return piece, across(piece, 1), far, across(far, 1)


def low_sum(*parts):
    total = parts[0].astype(F32)
    for part in parts[1:]:
        total = total + part.astype(F32)
    return total.astype(BF16)


def body(edges, attn_in, attn_out, mlp_up, mlp_down, vectors, key_mask):
    section = lax.axis_index("section")
    first = section == 0
    replica = lax.axis_index("replica")
    shards, replicas = lax.axis_size("shard"), lax.axis_size("replica")
    quarter = replica % QUARTERS
    edges_here = edges[0]
    clips, frames, width = edges_here.shape
    hidden = mlp_up.shape[2]
    dim = width // H
    heads = H // QUARTERS
    wide = heads * dim
    unit = hidden // (shards * QUARTERS)
    rows = attn_in.shape[1]
    assert clips == 2 and lax.axis_size("section") == 2 and replicas % shards == 0 and replicas % QUARTERS == 0

    def by_layer(own, other):
        return jnp.where(first, own, other), jnp.where(first, other, own)

    vec_by_layer = by_layer(vectors[0], swap_sections(vectors[0]))
    mask_row = transposed(
        lax.dynamic_index_in_dim(key_mask, section, 0, keepdims=False).astype(F32)[None], None, None
    )[0]
    inputs = after(edges_here, mask_row, *vec_by_layer)
    inputs = jnp.where(first, transposed(inputs[0], 0, 0), transposed(inputs[1], 0, 1))

    def pick(block, axis):
        return lax.dynamic_index_in_dim(block, quarter, axis, keepdims=False)

    def gathered(block):
        return lax.all_gather(block, "shard", axis=0, tiled=True)

    query_in, key_in, value_in = (
        pick(attn_in[0][:, i * width:(i + 1) * width].reshape(rows, QUARTERS, wide), 1) for i in range(3)
    )
    own_proj = jnp.concatenate(
        [key_in, value_in, query_in, pick(attn_out[0].reshape(rows, QUARTERS, width // QUARTERS), 1)], 1
    )
    own_up = pick(mlp_up[0].reshape(rows, shards, QUARTERS, unit), 2).reshape(rows, shards * unit)
    own_down = pick(mlp_down[0].reshape(QUARTERS, unit, width), 0)
    proj_zero, proj_one = by_layer(own_proj, swap_sections(own_proj))
    proj_zero = gathered(proj_zero)
    own_up = gathered(after(own_up, proj_zero))
    own_down = gathered(after(own_down, own_up))
    proj_one = gathered(after(proj_one, own_down))
    up_zero, up_one = by_layer(own_up, swap_sections(own_up))
    down_zero, down_one = by_layer(own_down, swap_sections(own_down))
    far = [across(proj_zero, 2)]
    far.append(across(up_zero, 2))
    far.append(across(after(down_zero, far[1]), 2))
    far.append(across(after(proj_one, far[2]), 2))
    far.append(across(after(up_one, far[2]), 2))
    far.append(across(after(down_one, far[3], far[4]), 2))
    blocks = (proj_zero, up_zero, down_zero, proj_one, up_one, down_one)
    blocks = [spread(block, other) for block, other in zip(blocks, far)]
    layers = []
    for layer in range(2):
        proj, up, down = blocks[3 * layer:3 * layer + 3]
        w_out = jnp.concatenate(in_order([piece[:, 3 * wide:] for piece in proj], quarter), 1)
        layers.append((proj, w_out, up, down, vec_by_layer[layer]))

    members = [0]
    bit = 2
    while bit < shards:
        members = members + [m ^ bit for m in members]
        bit *= 2
    members = members + [m ^ 1 for m in members]
    place = replica % shards
    bias_row = jnp.concatenate(
        [lax.dynamic_slice_in_dim(mask_row, (place ^ m) * frames, frames, 0) for m in members]
    )
    bias_row = jnp.where(bias_row > 0, 0.0, MASKED).astype(BF16)
    lane = jnp.arange(dim)[None, :]
    key_bias = jnp.where(lane == 0, bias_row[:, None], jnp.zeros((), BF16))

    def chips_rows(block):
        bit = 2
        while bit < shards:
            block = jnp.concatenate([block, across(block, bit)], 0)
            bit *= 2
        return block

    def forward(x_low, layer):
        proj, w_out, w_up, w_down, vec = layers[layer]
        x_set = chips_rows(x_low)
        normed = layer_norm(x_set.astype(F32), vec[0], vec[1]).astype(BF16)
        zeros = jnp.zeros((QUARTERS, wide), F32)
        bias_in = jnp.stack([zeros, vec[3].reshape(QUARTERS, wide), vec[2].reshape(QUARTERS, wide)], 1)
        own_qkv, other_kv = [], [None] * QUARTERS
        for p in range(QUARTERS):
            bias = lax.dynamic_index_in_dim(bias_in, quarter ^ p, 0, keepdims=False).reshape(3 * wide)
            own_qkv.append((dot(normed, proj[p][:, :3 * wide]) + bias).astype(BF16))
            other_kv[p ^ 1] = across(own_qkv[p][:, :2 * wide], 1)
        outs, weights, inverses = [], [], []
        for p in range(QUARTERS):
            out, weight, inverse = attend(own_qkv[p], other_kv[p], key_bias, heads, frames)
            outs.append(out)
            weights.append(weight)
            inverses.append(inverse)
        attended = jnp.concatenate(in_order(outs, quarter), 1)
        x = x_low.astype(F32)
        middle = x + dot(attended, w_out) + vec[4]
        normed_two = layer_norm(middle, vec[5], vec[6]).astype(BF16)
        bias_up = vec[8:].reshape(shards, QUARTERS, unit)
        acts, slopes = [], []
        result = middle + vec[7]
        for p in range(QUARTERS):
            bias = lax.dynamic_index_in_dim(bias_up, quarter ^ p, 1, keepdims=False).reshape(1, shards * unit)
            act, slope, result = mlp_part(normed_two, w_up[p], bias, w_down[p], result)
            acts.append(act)
            slopes.append(slope)
        kept = (x, normed, own_qkv, other_kv, weights, inverses, attended, middle, normed_two, acts, slopes)
        return result.astype(BF16), kept

    def norm_back(values, gain, grad):
        center = values - jnp.mean(values, -1, keepdims=True)
        inv = lax.rsqrt(jnp.mean(center * center, -1, keepdims=True) + EPS)
        unit_values = center * inv
        scaled = grad * gain
        back = inv * (
            scaled - jnp.mean(scaled, -1, keepdims=True)
            - unit_values * jnp.mean(scaled * unit_values, -1, keepdims=True)
        )
        return back, jnp.sum(grad * unit_values, 0), jnp.sum(grad, 0)

    def scattered(block):
        bit = QUARTERS
        while bit < replicas:
            block = low_sum(block, across(block, bit))
            bit *= 2
        return lax.psum_scatter(block, "shard", scatter_dimension=0, tiled=True)

    def half_sum(block):
        cut = block.shape[1] // 2
        left, right = block[:, :cut], block[:, cut:]
        return low_sum(jnp.where(first, left, right), swap_sections(jnp.where(first, right, left)))

    def backward(cot, layer, kept, pending):
        proj, w_out, w_up, w_down, vec = layers[layer]
        x, normed, own_qkv, other_kv, weights, inverses, attended, middle, normed_two, acts, slopes = kept
        order = (1, 3, 2, 0)
        d_mlp = cot.astype(BF16)
        g_down, g_up, up_sums, near_down, near_up = {}, {}, {}, {}, {}
        d_normed_two = jnp.zeros((frames, width), F32)
        for p in order:
            g_down[p], g_up[p], up_sums[p], d_normed_two = mlp_back_part(
                d_mlp, normed_two, acts[p], slopes[p], w_up[p], w_down[p], d_normed_two
            )
            if p & 1:
                near_down[p ^ 1] = across(g_down[p], 1)
                near_up[p ^ 1] = across(g_up[p], 1)
        back, g_gain_two, g_shift_two = norm_back(middle, vec[5], d_normed_two)
        d_middle = cot + back
        d_attn = d_middle.astype(BF16)
        d_attn_parts = in_order([d_attn[:, p * wide:(p + 1) * wide] for p in range(QUARTERS)], quarter)
        d_attended = dot(d_attn, w_out, NT).astype(BF16)
        d_heads = in_order([d_attended[:, p * wide:(p + 1) * wide] for p in range(QUARTERS)], quarter)

        far_down = across(low_sum(g_down[2], near_down[2]), 2)
        far_up = across(low_sum(g_up[2], near_up[2]), 2)
        above = None
        results = {}
        for p in order:
            head = d_heads[p]
            if p == 1:
                head = after(head, *near_down.values())
                if pending is not None:
                    head = after(head, pending[1])
            elif p == 3:
                head = after(head, *near_up.values())
            elif p == 2 and pending is not None:
                make, far = pending[0]
                above = half_sum(make(far))
            results[p] = attend_back(own_qkv[p], other_kv[p], weights[p], inverses[p], head, heads, frames)
        from_other = {p: across(results[p ^ 1][2], 1) for p in range(QUARTERS)}
        g_proj, sums_in, near_proj = {}, {}, {}
        d_normed = jnp.zeros(normed.shape, F32)
        for p in order:
            g_proj[p], sums_in[p], d_normed = proj_back(
                normed, results[p][1], from_other[p], results[p][0], attended, d_attn_parts[p], proj[p], d_normed
            )
            if p & 1:
                near_proj[p ^ 1] = across(g_proj[p], 1)
        block = after(d_normed, far_down)
        if above is not None:
            block = after(block, above)
            above = scattered(above)
        bit = shards // 2
        while bit >= 2:
            cut = block.shape[0] // 2
            block = block[:cut] + across(block[cut:].astype(BF16), bit).astype(F32)
            bit //= 2
        far_proj = across(low_sum(g_proj[2], near_proj[2]), 2)
        mlp_half = jnp.concatenate(
            [
                half_sum(low_sum(g_down[0], near_down[0], far_down)),
                half_sum(low_sum(g_up[0], near_up[0], far_up)),
            ],
            1,
        )
        mlp_done = scattered(mlp_half)
        back, g_gain_one, g_shift_one = norm_back(x, vec[0], block)
        g_x = d_middle + back
        sums = [jnp.concatenate(in_order([sums_in[p][0, i * wide:(i + 1) * wide] for p in range(4)], quarter)) for i in range(3)]
        sum_up = jnp.stack(in_order([up_sums[p].reshape(shards, unit) for p in range(4)], quarter), 1).reshape(-1, width)
        g_vec = jnp.concatenate(
            [
                jnp.stack(
                    [
                        g_gain_one, g_shift_one, sums[2], sums[1],
                        jnp.sum(d_attn.astype(F32), 0), g_gain_two, g_shift_two,
                        jnp.sum(d_mlp.astype(F32), 0),
                    ]
                ),
                sum_up,
            ]
        )

        def finish_proj(other):
            return low_sum(g_proj[0], near_proj[0], other)

        return g_x, mlp_done, ((finish_proj, far_proj), mlp_half), above, g_vec

    x_one, kept_zero = forward(inputs, 0)
    y_one, kept_one = forward(x_one, 1)
    cot = after(edges_here, x_one)
    cot = jnp.where(first, transposed(cot[0], 1, 0), transposed(cot[1], 1, 1))
    out_slots = [transposed(y_one, 0, 1), transposed(y_one, 1, 1)]
    g_one, mlp_one, pending, _, vec_one = backward(cot.astype(F32), 1, kept_one, None)
    g_zero, mlp_zero, pending, proj_one, vec_zero = backward(
        g_one.astype(BF16).astype(F32), 0, kept_zero, pending
    )
    g_low = g_zero.astype(BF16)
    back_slots = [transposed(g_low, 0, 0), transposed(g_low, 1, 0)]
    edges_out = jnp.stack([jnp.where(first, b, o) for b, o in zip(back_slots, out_slots)])
    vec_all = jnp.concatenate([vec_zero, vec_one])
    bit = 1
    while bit < replicas:
        vec_all = vec_all + across(vec_all, bit)
        bit *= 2
    vec_all = vec_all + swap_sections(vec_all)
    vec_all = jnp.pad(vec_all.T, ((0, 0), (0, 128 - vec_all.shape[0]))).astype(BF16)
    make, far = pending[0]
    rest = jnp.concatenate([half_sum(make(far)), vec_all], 1)
    rest = lax.psum_scatter(after(rest, mlp_zero), "shard", scatter_dimension=0, tiled=True)
    proj_zero = rest[:, :width // 2]
    g_vectors = rest[:, width // 2:].astype(F32).T
    g_vectors = jnp.where(first, g_vectors[:12], g_vectors[12:24])

    def finished(zero, one):
        own, other = jnp.where(first, zero, one), swap_sections(jnp.where(first, one, zero))
        cut = width // 2
        parts = []
        for start in range(0, own.shape[1], cut):
            a, b = own[:, start:start + cut], other[:, start:start + cut]
            parts += [jnp.where(first, a, b), jnp.where(first, b, a)]
        part = jnp.concatenate(parts, 1)
        return spread(part, across(part, 2))

    f_down, f_up = placed_parts(
        functools.partial(place_mlp_kernel, shards=shards), quarter, finished(mlp_zero, mlp_one),
        [mlp_down.shape[1:], mlp_up.shape[1:]],
    )
    f_in, f_out = placed_parts(
        place_proj_kernel, quarter, finished(proj_zero, proj_one), [attn_in.shape[1:], attn_out.shape[1:]]
    )
    return edges_out[None], f_in[None], f_out[None], f_up[None], f_down[None], g_vectors[None]


def solution(mesh):
    placed = (
        P("section", "replica", "shard", None),
        P("section", "shard", None),
        P("section", "shard", None),
        P("section", "shard", None),
        P("section", "shard", None),
        P("section", None, None),
        P("replica", None),
    )
    return jax.shard_map(
        body,
        mesh=mesh,
        in_specs=placed,
        out_specs=(
            P("section", "replica", "shard", None),
            P("section", "shard", None),
            P("section", "shard", None),
            P("section", "shard", None),
            P("section", "shard", None),
            P("section", None, "shard"),
        ),
        check_vma=False,
    )
```

```python
import functools
import math

import jax
import jax.numpy as jnp
from jax import lax
from jax.experimental import pallas as pl
from jax.experimental.pallas import tpu as pltpu
from jax.sharding import PartitionSpec as P

H = 12
EPS = 1e-05
MASKED = -1e30
QUARTERS = 4
BF16 = jnp.bfloat16
F32 = jnp.float32
AXES = ("section", "shard", "replica")
NN = (((1,), (0,)), ((), ()))
NT = (((1,), (1,)), ((), ()))
TN = (((0,), (0,)), ((), ()))


def dot(a, b, dims=NN):
    return lax.dot_general(a, b, dims, preferred_element_type=F32)


def layer_norm(values, gain, shift):
    center = values - jnp.mean(values, -1, keepdims=True)
    spread = jnp.mean(center * center, -1, keepdims=True)
    return center * lax.rsqrt(spread + EPS) * gain + shift


def key_chunks(sources, size):
    chunks, base = [], 0
    for source in range(len(sources)):
        rows = sources[source].shape[0]
        for start in range(0, rows, size):
            chunks.append((source, start, base + start))
        base += rows
    return chunks


def attend_kernel(own_ref, other_ref, bias_ref, out_ref, exp_ref, inv_ref, score_ref, *, heads, frames, chunk):
    dim = own_ref.shape[1] // (3 * heads)
    wide = heads * dim
    sources = (own_ref, other_ref)
    chunks = key_chunks(sources, chunk)

    def one_head(head):
        at = head * dim
        query = own_ref[0:frames, 2 * wide + at:2 * wide + at + dim] * (dim ** -0.5)
        lane = lax.broadcasted_iota(jnp.int32, (frames, dim), 1)
        query = jnp.concatenate([query.astype(BF16), (lane == 0).astype(BF16)], 1)
        top = None
        for source, start, row in chunks:
            key = sources[source][start:start + chunk, at:at + dim]
            key = jnp.concatenate([key, bias_ref[row:row + chunk, :]], 1)
            score = dot(key, query, NT)
            score_ref[row:row + chunk, :] = score
            part = jnp.max(score, 0, keepdims=True)
            top = part if top is None else jnp.maximum(top, part)
        total = None
        for source, start, row in chunks:
            weight = jnp.exp(score_ref[row:row + chunk, :] - top).astype(BF16)
            exp_ref[0, row:row + chunk, :] = weight
            value = sources[source][start:start + chunk, wide + at:wide + at + dim]
            value = jnp.concatenate([value, jnp.ones_like(value)], 1)
            part = dot(value, weight, TN)
            total = part if total is None else total + part
        inverse = 1.0 / total[dim:dim + 1, :]
        inv_ref[head:head + 1, :] = inverse
        out_ref[:, at:at + dim] = (total[0:dim, :] * inverse).T.astype(BF16)

    for head in range(heads):
        pl.when(pl.program_id(0) == head)(functools.partial(one_head, head))


def whole_block(shape):
    return pl.BlockSpec(shape, lambda i: (0,) * len(shape))


def chunk_size(own, frames):
    chunk = min(256, frames)
    return frames if own.shape[0] % chunk else chunk


def attend(own, other, bias, heads, frames):
    keys = own.shape[0] + other.shape[0]
    wide = own.shape[1] // 3
    return pl.pallas_call(
        functools.partial(attend_kernel, heads=heads, frames=frames, chunk=chunk_size(own, frames)),
        grid=(heads,),
        in_specs=[whole_block(own.shape), whole_block(other.shape), whole_block(bias.shape)],
        out_specs=[
            whole_block((frames, wide)),
            pl.BlockSpec((1, keys, frames), lambda i: (i, 0, 0)),
            whole_block((heads, frames)),
        ],
        out_shape=(
            jax.ShapeDtypeStruct((frames, wide), BF16),
            jax.ShapeDtypeStruct((heads, keys, frames), BF16),
            jax.ShapeDtypeStruct((heads, frames), F32),
        ),
        scratch_shapes=[pltpu.VMEM((keys, frames), F32)],
        compiler_params=pltpu.CompilerParams(vmem_limit_bytes=40 * 2**20),
        cost_estimate=pl.CostEstimate(
            flops=16 * keys * frames * wide, bytes_accessed=2 * heads * keys * frames, transcendentals=heads * keys * frames
        ),
        name="attend",
    )(own, other, bias)


def attend_back_kernel(own_ref, other_ref, exp_ref, inv_ref, dout_ref, dq_ref, down_ref, dother_ref, prod_ref, *, heads, frames, chunk):
    dim = own_ref.shape[1] // (3 * heads)
    wide = heads * dim
    scale = dim ** -0.5
    sources = (own_ref, other_ref)
    targets = (down_ref, dother_ref)
    chunks = key_chunks(sources, chunk)

    def one_head(head):
        at = head * dim
        query = (own_ref[0:frames, 2 * wide + at:2 * wide + at + dim] * scale).astype(BF16)
        inverse = inv_ref[head:head + 1, :]
        dout_t = dout_ref[:, at:at + dim].astype(F32).T * inverse
        dout = dout_t.T.astype(BF16)
        dout_t = dout_t.astype(BF16)
        delta = None
        for source, start, row in chunks:
            value = sources[source][start:start + chunk, wide + at:wide + at + dim]
            weight = exp_ref[0, row:row + chunk, :]
            prod = dot(value, dout_t) * weight.astype(F32)
            prod_ref[row:row + chunk, :] = prod
            part = jnp.sum(prod, 0, keepdims=True)
            delta = part if delta is None else delta + part
            targets[source][start:start + chunk, wide + at:wide + at + dim] = dot(weight, dout).astype(BF16)
        delta = delta * inverse
        dq_t = None
        for source, start, row in chunks:
            key = sources[source][start:start + chunk, at:at + dim]
            weight = exp_ref[0, row:row + chunk, :].astype(F32)
            ds = (prod_ref[row:row + chunk, :] - weight * delta).astype(BF16)
            targets[source][start:start + chunk, at:at + dim] = dot(ds, query).astype(BF16)
            part = dot(key, ds, TN)
            dq_t = part if dq_t is None else dq_t + part
        dq_ref[:, at:at + dim] = (dq_t.T * scale).astype(BF16)

    for head in range(heads):
        pl.when(pl.program_id(0) == head)(functools.partial(one_head, head))


def attend_back(own, other, weights, inverse, dout, heads, frames):
    keys = own.shape[0] + other.shape[0]
    wide = own.shape[1] // 3
    results = ((frames, wide), (own.shape[0], 2 * wide), (other.shape[0], 2 * wide))
    return pl.pallas_call(
        functools.partial(attend_back_kernel, heads=heads, frames=frames, chunk=chunk_size(own, frames)),
        grid=(heads,),
        in_specs=[
            whole_block(own.shape), whole_block(other.shape),
            pl.BlockSpec((1, keys, frames), lambda i: (i, 0, 0)),
            whole_block(inverse.shape), whole_block(dout.shape),
        ],
        out_specs=[whole_block(shape) for shape in results],
        out_shape=[jax.ShapeDtypeStruct(shape, BF16) for shape in results],
        scratch_shapes=[pltpu.VMEM((keys, frames), F32)],
        compiler_params=pltpu.CompilerParams(vmem_limit_bytes=40 * 2**20),
        cost_estimate=pl.CostEstimate(
            flops=32 * keys * frames * wide, bytes_accessed=2 * heads * keys * frames, transcendentals=0
        ),
        name="attend_back",
    )(own, other, weights, inverse, dout)


def out_kernel(quarter_ref, a_ref, b_ref, c_ref, d_ref, weight_ref, x_ref, vec_ref, att_ref, mid_ref, norm_ref):
    parts = [ref[...] for ref in (a_ref, b_ref, c_ref, d_ref)]
    attended = jnp.concatenate(in_order(parts, quarter_ref[0]), 1)
    att_ref[...] = attended
    middle = x_ref[...].astype(F32) + dot(attended, weight_ref[...]) + vec_ref[4:5, :]
    mid_ref[...] = middle
    norm_ref[...] = layer_norm(middle, vec_ref[5:6, :], vec_ref[6:7, :]).astype(BF16)


def scalar_first(count):
    return [pl.BlockSpec(memory_space=pltpu.SMEM)] + [pl.BlockSpec(memory_space=pltpu.VMEM)] * count


def out_part(quarter, outs, weight, x_low, vec):
    shape = x_low.shape
    return pl.pallas_call(
        out_kernel,
        in_specs=scalar_first(7),
        out_shape=[jax.ShapeDtypeStruct(shape, kind) for kind in (BF16, F32, BF16)],
        compiler_params=pltpu.CompilerParams(vmem_limit_bytes=32 * 2**20),
        cost_estimate=pl.CostEstimate(
            flops=2 * math.prod(shape) * shape[1], bytes_accessed=14 * math.prod(shape), transcendentals=0
        ),
        name="out_part",
    )(quarter.reshape(1), *outs, weight, x_low, vec)


def norm_back(values, gain, grad):
    center = values - jnp.mean(values, -1, keepdims=True)
    inv = lax.rsqrt(jnp.mean(center * center, -1, keepdims=True) + EPS)
    unit_values = center * inv
    scaled = grad * gain
    back = inv * (
        scaled - jnp.mean(scaled, -1, keepdims=True)
        - unit_values * jnp.mean(scaled * unit_values, -1, keepdims=True)
    )
    return back, jnp.sum(grad * unit_values, 0, keepdims=True), jnp.sum(grad, 0, keepdims=True)


def middle_back_kernel(quarter_ref, grad_ref, mid_ref, cot_ref, vec_ref, weight_ref, dmid_ref, rows_ref, *part_refs):
    cot = cot_ref[...].astype(F32)
    back, gain, shift = norm_back(mid_ref[...], vec_ref[5:6, :], grad_ref[...])
    d_middle = cot + back
    dmid_ref[...] = d_middle
    d_attn = d_middle.astype(BF16)
    d_low = d_attn.astype(F32)
    rows_ref[...] = jnp.concatenate(
        [gain, shift, jnp.sum(d_low, 0, keepdims=True), jnp.sum(cot, 0, keepdims=True)], 0
    )
    d_attended = dot(d_attn, weight_ref[...], NT).astype(BF16)
    for refs, whole in ((part_refs[:QUARTERS], d_attended), (part_refs[QUARTERS:], d_attn)):
        wide = whole.shape[1] // QUARTERS
        parts = in_order([whole[:, p * wide:(p + 1) * wide] for p in range(QUARTERS)], quarter_ref[0])
        for ref, part in zip(refs, parts):
            ref[...] = part


def middle_back(quarter, grad, middle, cot, vec, weight):
    frames, width = middle.shape
    part = jax.ShapeDtypeStruct((frames, width // QUARTERS), BF16)
    results = pl.pallas_call(
        middle_back_kernel,
        in_specs=scalar_first(5),
        out_shape=[jax.ShapeDtypeStruct((frames, width), F32), jax.ShapeDtypeStruct((4, width), F32)]
        + [part] * (2 * QUARTERS),
        compiler_params=pltpu.CompilerParams(vmem_limit_bytes=32 * 2**20),
        cost_estimate=pl.CostEstimate(
            flops=2 * frames * width * width, bytes_accessed=18 * frames * width, transcendentals=0
        ),
        name="middle_back",
    )(quarter.reshape(1), grad, middle, cot, vec, weight)
    return results[0], results[1], results[2:2 + QUARTERS], results[2 + QUARTERS:]


def column_tile(columns):
    return 256 if columns % 256 == 0 else columns


def mlp_kernel(in_ref, up_ref, bias_ref, down_ref, before_ref, act_ref, slope_ref, sum_ref):
    up = dot(in_ref[...], up_ref[...]) + bias_ref[...]
    cdf = 0.5 + 0.5 * lax.erf(up * (0.5 ** 0.5))
    pdf = jnp.exp(-0.5 * up * up) * 0.3989422804014327
    act = (up * cdf).astype(BF16)
    act_ref[...] = act
    slope_ref[...] = (cdf + up * pdf).astype(BF16)
    part = dot(act, down_ref[...])

    @pl.when(pl.program_id(0) == 0)
    def _():
        sum_ref[...] = before_ref[...] + part

    @pl.when(pl.program_id(0) > 0)
    def _():
        sum_ref[...] += part


def mlp_part(values, up, bias, down, before):
    rows, depth = values.shape
    columns = up.shape[1]
    tile = column_tile(columns)
    whole = pl.BlockSpec((rows, depth), lambda i: (0, 0))
    hidden = pl.BlockSpec((rows, tile), lambda i: (0, i))
    return pl.pallas_call(
        mlp_kernel,
        grid=(columns // tile,),
        in_specs=[
            whole,
            pl.BlockSpec((depth, tile), lambda i: (0, i)),
            pl.BlockSpec((1, tile), lambda i: (0, i)),
            pl.BlockSpec((tile, depth), lambda i: (i, 0)),
            whole,
        ],
        out_specs=[hidden, hidden, whole],
        out_shape=[
            jax.ShapeDtypeStruct((rows, columns), BF16),
            jax.ShapeDtypeStruct((rows, columns), BF16),
            jax.ShapeDtypeStruct((rows, depth), F32),
        ],
        compiler_params=pltpu.CompilerParams(vmem_limit_bytes=32 * 2**20),
        cost_estimate=pl.CostEstimate(
            flops=4 * rows * depth * columns, bytes_accessed=4 * (3 * rows * depth + depth * columns + rows * columns),
            transcendentals=2 * rows * columns,
        ),
        name="mlp_part",
    )(values, up, bias, down, before)


def mlp_back_kernel(grad_ref, in_ref, act_ref, slope_ref, up_ref, down_ref, before_ref, gd_ref, gu_ref, row_ref, sum_ref):
    grad = grad_ref[...]
    d_up = (dot(grad, down_ref[...], NT) * slope_ref[...].astype(F32)).astype(BF16)
    gd_ref[...] = dot(act_ref[...], grad, TN).astype(BF16)
    gu_ref[...] = dot(in_ref[...], d_up, TN).astype(BF16)
    row_ref[...] = jnp.sum(d_up.astype(F32), 0, keepdims=True)
    part = dot(d_up, up_ref[...], NT)

    @pl.when(pl.program_id(0) == 0)
    def _():
        sum_ref[...] = before_ref[...] + part

    @pl.when(pl.program_id(0) > 0)
    def _():
        sum_ref[...] += part


def mlp_back_part(grad, values, act, slope, up, down, before):
    rows, depth = values.shape
    columns = up.shape[1]
    tile = column_tile(columns)
    whole = pl.BlockSpec((rows, depth), lambda i: (0, 0))
    hidden = pl.BlockSpec((rows, tile), lambda i: (0, i))
    up_tile = pl.BlockSpec((depth, tile), lambda i: (0, i))
    down_tile = pl.BlockSpec((tile, depth), lambda i: (i, 0))
    return pl.pallas_call(
        mlp_back_kernel,
        grid=(columns // tile,),
        in_specs=[whole, whole, hidden, hidden, up_tile, down_tile, whole],
        out_specs=[down_tile, up_tile, pl.BlockSpec((1, tile), lambda i: (0, i)), whole],
        out_shape=[
            jax.ShapeDtypeStruct((columns, depth), BF16),
            jax.ShapeDtypeStruct((depth, columns), BF16),
            jax.ShapeDtypeStruct((1, columns), F32),
            jax.ShapeDtypeStruct((rows, depth), F32),
        ],
        compiler_params=pltpu.CompilerParams(vmem_limit_bytes=40 * 2**20),
        cost_estimate=pl.CostEstimate(
            flops=8 * rows * depth * columns, bytes_accessed=4 * (3 * rows * depth + 2 * depth * columns + rows * columns),
            transcendentals=0,
        ),
        name="mlp_back_part",
    )(grad, values, act, slope, up, down, before)


def proj_back_kernel(in_ref, own_ref, other_ref, query_ref, out_ref, grad_ref, weight_ref, before_ref, g_ref, row_ref, sum_ref):
    frames, wide = query_ref.shape
    both = (own_ref[...].astype(F32) + other_ref[...].astype(F32)).astype(BF16)
    query = query_ref[...]
    values = in_ref[...]
    g_ref[...] = jnp.concatenate(
        [dot(values, both, TN), dot(values[:frames], query, TN), dot(out_ref[...], grad_ref[...], TN)], 1
    ).astype(BF16)
    row_ref[...] = jnp.concatenate(
        [jnp.sum(both.astype(F32), 0, keepdims=True), jnp.sum(query.astype(F32), 0, keepdims=True)], 1
    )
    total = before_ref[...] + dot(both, weight_ref[:, :2 * wide], NT)
    own = total[:frames] + dot(query, weight_ref[:, 2 * wide:3 * wide], NT)
    sum_ref[0:frames, :] = own
    sum_ref[frames:, :] = total[frames:]


def proj_back(values, own, other, query, out, grad, weight, before):
    rows, depth = values.shape
    wide = query.shape[1]
    return pl.pallas_call(
        proj_back_kernel,
        out_shape=[
            jax.ShapeDtypeStruct(weight.shape, BF16),
            jax.ShapeDtypeStruct((1, 3 * wide), F32),
            jax.ShapeDtypeStruct((rows, depth), F32),
        ],
        compiler_params=pltpu.CompilerParams(vmem_limit_bytes=40 * 2**20),
        cost_estimate=pl.CostEstimate(
            flops=8 * rows * depth * 2 * wide, bytes_accessed=12 * rows * depth + 4 * depth * weight.shape[1],
            transcendentals=0,
        ),
        name="proj_back",
    )(values, own, other, query, out, grad, weight, before)


def place_proj_kernel(quarter_ref, a_ref, b_ref, c_ref, d_ref, qkv_ref, out_ref, vec_ref):
    pieces = [ref[...].astype(F32) for ref in (a_ref, b_ref, c_ref, d_ref)]
    width = out_ref.shape[1]
    wide = width // QUARTERS
    total = pieces[0][:, width:] + pieces[1][:, width:] + pieces[2][:, width:] + pieces[3][:, width:]
    vec_ref[...] = total.T
    pieces = in_order([piece[:, :width] for piece in pieces], quarter_ref[0])
    for column, part in ((0, 2), (1, 0), (2, 1)):
        qkv_ref[:, column * width:(column + 1) * width] = jnp.concatenate(
            [piece[:, part * wide:(part + 1) * wide] for piece in pieces], 1
        )
    out_ref[...] = jnp.concatenate([piece[:, 3 * wide:] for piece in pieces], 1)


def place_mlp_kernel(quarter_ref, a_ref, b_ref, c_ref, d_ref, down_ref, up_ref, *, shards):
    pieces = in_order([ref[...].astype(F32) for ref in (a_ref, b_ref, c_ref, d_ref)], quarter_ref[0])
    rows, width = pieces[0].shape[0], pieces[0].shape[1] // 2
    unit = width // shards
    for place in range(QUARTERS):
        down_ref[place * rows:(place + 1) * rows, :] = pieces[place][:, :width]
    for shard in range(shards):
        start = width + shard * unit
        up_ref[:, shard * QUARTERS * unit:(shard + 1) * QUARTERS * unit] = jnp.concatenate(
            [piece[:, start:start + unit] for piece in pieces], 1
        )


def placed_parts(kernel, quarter, pieces, shapes):
    size = sum(math.prod(shape) for shape in shapes)
    return pl.pallas_call(
        kernel,
        in_specs=scalar_first(QUARTERS),
        out_shape=[jax.ShapeDtypeStruct(shape, F32) for shape in shapes],
        compiler_params=pltpu.CompilerParams(vmem_limit_bytes=32 * 2**20),
        cost_estimate=pl.CostEstimate(flops=size, bytes_accessed=6 * size, transcendentals=0),
        name="placed_parts",
    )(quarter.reshape(1), *pieces)


def across(block, bit):
    count = lax.axis_size("replica")
    return lax.ppermute(block, "replica", [(i, i ^ bit) for i in range(count)])


def swap_sections(block):
    return lax.ppermute(block, "section", [(0, 1), (1, 0)])


def reversed_bits(index, count):
    result, bit = index * 0, 1
    while bit < count:
        result = result * 2 + index // bit % 2
        bit *= 2
    return result


def transposed(block, source, target):
    shards, replicas = lax.axis_size("shard"), lax.axis_size("replica")

    def flat(section, shard, replica):
        return (section * shards + shard) * replicas + replica

    route = []
    for shard in range(shards):
        for replica in range(replicas):
            group, place = divmod(replica, shards)
            here = (shard, replica)
            there = (reversed_bits(place, shards), group * shards + reversed_bits(shard, shards))
            if source is None:
                route += [(flat(s, *here), flat(s, *there)) for s in range(2)]
            else:
                route.append((flat(source, *here), flat(target, *there)))
    return lax.ppermute(block, AXES, route)


def in_order(pieces, quarter):
    odd, high = (quarter & 1) == 1, (quarter & 2) == 2
    a, b, c, d = pieces
    a, b, c, d = jnp.where(odd, b, a), jnp.where(odd, a, b), jnp.where(odd, d, c), jnp.where(odd, c, d)
    return jnp.where(high, c, a), jnp.where(high, d, b), jnp.where(high, a, c), jnp.where(high, b, d)


def after(value, *others):
    return lax.optimization_barrier((value, others))[0]


def spread(piece, far):
    return piece, across(piece, 1), far, across(far, 1)


def low_sum(*parts):
    total = parts[0].astype(F32)
    for part in parts[1:]:
        total = total + part.astype(F32)
    return total.astype(BF16)


def body(edges, attn_in, attn_out, mlp_up, mlp_down, vectors, key_mask):
    section = lax.axis_index("section")
    first = section == 0
    replica = lax.axis_index("replica")
    shards, replicas = lax.axis_size("shard"), lax.axis_size("replica")
    quarter = replica % QUARTERS
    edges_here = edges[0]
    clips, frames, width = edges_here.shape
    hidden = mlp_up.shape[2]
    dim = width // H
    heads = H // QUARTERS
    wide = heads * dim
    unit = hidden // (shards * QUARTERS)
    rows = attn_in.shape[1]
    assert clips == 2 and lax.axis_size("section") == 2 and replicas % shards == 0 and replicas % QUARTERS == 0

    def by_layer(own, other):
        return jnp.where(first, own, other), jnp.where(first, other, own)

    vec_by_layer = by_layer(vectors[0], swap_sections(vectors[0]))
    mask_row = transposed(
        lax.dynamic_index_in_dim(key_mask, section, 0, keepdims=False).astype(F32)[None], None, None
    )[0]
    inputs = jnp.where(first, transposed(edges_here[0], 0, 0), transposed(edges_here[1], 0, 1))

    def pick(block, axis):
        return lax.dynamic_index_in_dim(block, quarter, axis, keepdims=False)

    def gathered(block):
        return lax.all_gather(block, "shard", axis=0, tiled=True)

    query_in, key_in, value_in = (
        pick(attn_in[0][:, i * width:(i + 1) * width].reshape(rows, QUARTERS, wide), 1) for i in range(3)
    )
    own_proj = jnp.concatenate(
        [key_in, value_in, query_in, pick(attn_out[0].reshape(rows, QUARTERS, width // QUARTERS), 1)], 1
    )
    own_up = pick(mlp_up[0].reshape(rows, shards, QUARTERS, unit), 2).reshape(rows, shards * unit)
    own_down = pick(mlp_down[0].reshape(QUARTERS, unit, width), 0)
    proj_zero, proj_one = by_layer(own_proj, swap_sections(own_proj))
    proj_zero = gathered(proj_zero)
    own_up = gathered(after(own_up, proj_zero))
    own_down = gathered(after(own_down, own_up))
    proj_one = gathered(after(proj_one, own_down))
    up_zero, up_one = by_layer(own_up, swap_sections(own_up))
    down_zero, down_one = by_layer(own_down, swap_sections(own_down))
    blocks = [proj_zero, up_zero, down_zero, proj_one, up_one]
    blocks = [spread(block, across(block, 2)) for block in blocks]

    layers = []
    for layer in range(2):
        proj = blocks[3 * layer]
        w_out = jnp.concatenate(in_order([piece[:, 3 * wide:] for piece in proj], quarter), 1)
        layers.append([proj, w_out, blocks[3 * layer + 1], blocks[2], vec_by_layer[layer]])

    members = [0]
    bit = 2
    while bit < shards:
        members = members + [m ^ bit for m in members]
        bit *= 2
    members = members + [m ^ 1 for m in members]
    place = replica % shards
    bias_row = jnp.concatenate(
        [lax.dynamic_slice_in_dim(mask_row, reversed_bits(place ^ m, shards) * frames, frames, 0) for m in members]
    )
    bias_row = jnp.where(bias_row > 0, 0.0, MASKED).astype(BF16)
    lane = jnp.arange(dim)[None, :]
    key_bias = jnp.where(lane == 0, bias_row[:, None], jnp.zeros((), BF16))

    def chips_rows(block):
        bit = 2
        while bit < shards:
            block = jnp.concatenate([block, across(block, bit)], 0)
            bit *= 2
        return block

    def forward(x_low, layer):
        x_set = chips_rows(x_low)
        if layer == 1:
            down = after(down_one, x_set)
            layers[1][3] = spread(down, across(down, 2))
        proj, w_out, w_up, w_down, vec = layers[layer]
        normed = layer_norm(x_set.astype(F32), vec[0], vec[1]).astype(BF16)
        zeros = jnp.zeros((QUARTERS, wide), F32)
        bias_in = jnp.stack([zeros, vec[3].reshape(QUARTERS, wide), vec[2].reshape(QUARTERS, wide)], 1)
        own_qkv, other_kv = [], [None] * QUARTERS
        for p in range(QUARTERS):
            bias = lax.dynamic_index_in_dim(bias_in, quarter ^ p, 0, keepdims=False).reshape(3 * wide)
            own_qkv.append((dot(normed, proj[p][:, :3 * wide]) + bias).astype(BF16))
            other_kv[p ^ 1] = across(own_qkv[p][:, :2 * wide], 1)
        outs, weights, inverses = [], [], []
        for p in range(QUARTERS):
            out, weight, inverse = attend(own_qkv[p], other_kv[p], key_bias, heads, frames)
            outs.append(out)
            weights.append(weight)
            inverses.append(inverse)
        attended, middle, normed_two = out_part(quarter, outs, w_out, x_low, vec)
        bias_up = vec[8:].reshape(shards, QUARTERS, unit)
        acts, slopes = [], []
        result = middle + vec[7]
        for p in range(QUARTERS):
            bias = lax.dynamic_index_in_dim(bias_up, quarter ^ p, 1, keepdims=False).reshape(1, shards * unit)
            act, slope, result = mlp_part(normed_two, w_up[p], bias, w_down[p], result)
            acts.append(act)
            slopes.append(slope)
        kept = (x_low, normed, own_qkv, other_kv, weights, inverses, attended, middle, normed_two, acts, slopes)
        return result.astype(BF16), kept

    def scattered(block):
        bit = QUARTERS
        while bit < replicas:
            block = low_sum(block, across(block, bit))
            bit *= 2
        return lax.psum_scatter(block, "shard", scatter_dimension=0, tiled=True)

    def half_sum(block):
        cut = block.shape[1] // 2
        left, right = block[:, :cut], block[:, cut:]
        return low_sum(jnp.where(first, left, right), swap_sections(jnp.where(first, right, left)))

    def backward(cot, layer, kept, pending):
        proj, w_out, w_up, w_down, vec = layers[layer]
        x_low, normed, own_qkv, other_kv, weights, inverses, attended, middle, normed_two, acts, slopes = kept
        order = (1, 3, 2, 0)
        g_down, g_up, up_sums, near_down, near_up = {}, {}, {}, {}, {}
        d_normed_two = jnp.zeros((frames, width), F32)
        for p in order:
            g_down[p], g_up[p], up_sums[p], d_normed_two = mlp_back_part(
                cot, normed_two, acts[p], slopes[p], w_up[p], w_down[p], d_normed_two
            )
            if p & 1:
                near_down[p ^ 1] = across(g_down[p], 1)
                near_up[p ^ 1] = across(g_up[p], 1)
        d_middle, mid_rows, d_heads, d_attn_parts = middle_back(quarter, d_normed_two, middle, cot, vec, w_out)

        far_down = across(low_sum(g_down[2], near_down[2]), 2)
        far_up = across(low_sum(g_up[2], near_up[2]), 2)
        above = None
        results = {}
        for p in order:
            head = d_heads[p]
            if p == 1:
                head = after(head, *near_down.values())
                if pending is not None:
                    head = after(head, pending[1])
            elif p == 3:
                head = after(head, *near_up.values())
            elif p == 2 and pending is not None:
                make, far, vec_block = pending[0]
                above = half_sum(make(far))
                head = after(head, above)
                above = jnp.concatenate([above, vec_block], 1)
            elif p == 0:
                head = after(head, far_down)
                if pending is not None:
                    head = after(head, pending[2])
            results[p] = attend_back(own_qkv[p], other_kv[p], weights[p], inverses[p], head, heads, frames)
        from_other = {p: across(results[p ^ 1][2], 1) for p in range(QUARTERS)}
        half_down = half_sum(low_sum(g_down[0], near_down[0], far_down))
        if above is not None:
            above = scattered(above)
        g_proj, sums_in, near_proj = {}, {}, {}
        d_normed = jnp.zeros(normed.shape, F32)
        for p in order:
            g_proj[p], sums_in[p], d_normed = proj_back(
                normed, results[p][1], from_other[p], results[p][0], attended, d_attn_parts[p], proj[p], d_normed
            )
            if p & 1:
                near_proj[p ^ 1] = across(g_proj[p], 1)
        block = after(d_normed, half_down, far_up)
        if above is not None:
            block = after(block, above)
        bit = shards // 2
        while bit >= 2:
            cut = block.shape[0] // 2
            block = block[:cut] + across(block[cut:].astype(BF16), bit).astype(F32)
            bit //= 2
        half_up = half_sum(low_sum(g_up[0], near_up[0], far_up))
        block = after(block, half_up)
        mlp_done = scattered(jnp.concatenate([half_down, half_up], 1))
        far_proj = low_sum(g_proj[2], near_proj[2])
        if layer == 1:
            far_proj = after(far_proj, block)
        back, g_gain_one, g_shift_one = norm_back(x_low.astype(F32), vec[0], block)
        g_low = (d_middle + back).astype(BF16)
        if layer == 1:
            g_low = after(g_low, far_proj)
        far_proj = across(far_proj, 2)
        sums = [
            jnp.concatenate(in_order([sums_in[p][:, i * wide:(i + 1) * wide] for p in range(QUARTERS)], quarter), 1)
            for i in range(1, 3)
        ]
        sum_up = jnp.stack(in_order([up_sums[p].reshape(shards, unit) for p in range(QUARTERS)], quarter), 1)
        g_vec = jnp.concatenate(
            [
                g_gain_one, g_shift_one, sums[1], sums[0], mid_rows[2:3], mid_rows[0:2], mid_rows[3:4],
                sum_up.reshape(-1, width),
            ]
        )
        vec_block = jnp.pad(g_vec.T.astype(BF16), ((0, 0), (0, 128 - g_vec.shape[0])))

        def finish_proj(other):
            return low_sum(g_proj[0], near_proj[0], other)

        return g_low, ((finish_proj, far_proj, vec_block), half_up, mlp_done), above

    x_one, kept_zero = forward(inputs, 0)
    y_one, kept_one = forward(x_one, 1)
    cot = after(edges_here, x_one)
    cot = jnp.where(first, transposed(cot[0], 1, 0), transposed(cot[1], 1, 1))
    g_one, pending, _ = backward(cot, 1, kept_one, None)
    mlp_one = pending[2]
    g_zero, pending, proj_one = backward(g_one, 0, kept_zero, pending)
    y_one = after(y_one, g_one)
    out_slots = [transposed(y_one, 0, 1), transposed(y_one, 1, 1)]
    back_slots = [transposed(g_zero, 0, 0), transposed(g_zero, 1, 0)]
    edges_out = jnp.stack([jnp.where(first, b, o) for b, o in zip(back_slots, out_slots)])
    (make, far, vec_block), _, mlp_zero = pending
    proj_zero = scattered(jnp.concatenate([half_sum(make(far)), vec_block], 1))

    def exchanged(zero, one):
        return jnp.where(first, zero, one), swap_sections(jnp.where(first, one, zero))

    def joined(own, other):
        cut = width // 2
        parts = []
        for start in range(0, own.shape[1], cut):
            a, b = own[:, start:start + cut], other[:, start:start + cut]
            parts += [jnp.where(first, a, b), jnp.where(first, b, a)]
        return parts

    part = jnp.concatenate(joined(*exchanged(mlp_zero, mlp_one)), 1)
    f_down, f_up = placed_parts(
        functools.partial(place_mlp_kernel, shards=shards), quarter, spread(part, across(part, 2)),
        [mlp_down.shape[1:], mlp_up.shape[1:]],
    )
    own, other = exchanged(proj_zero, proj_one)
    cut = width // 2
    part = jnp.concatenate(
        joined(own[:, :cut], other[:, :cut]) + [low_sum(own[:, cut:], other[:, cut:])], 1
    )
    f_in, f_out, f_vec = placed_parts(
        place_proj_kernel, quarter, spread(part, across(part, 2)),
        [attn_in.shape[1:], attn_out.shape[1:], (128, rows)],
    )
    f_vec = f_vec[:vectors.shape[1]]
    return edges_out[None], f_in[None], f_out[None], f_up[None], f_down[None], f_vec[None]


def solution(mesh):
    placed = (
        P("section", "replica", "shard", None),
        P("section", "shard", None),
        P("section", "shard", None),
        P("section", "shard", None),
        P("section", "shard", None),
        P("section", None, None),
        P("replica", None),
    )
    return jax.shard_map(
        body,
        mesh=mesh,
        in_specs=placed,
        out_specs=(
            P("section", "replica", "shard", None),
            P("section", "shard", None),
            P("section", "shard", None),
            P("section", "shard", None),
            P("section", "shard", None),
            P("section", None, "shard"),
        ),
        check_vma=False,
    )
```

```python
import functools
import math

import jax
import jax.numpy as jnp
from jax import lax
from jax.experimental import pallas as pl
from jax.experimental.pallas import tpu as pltpu
from jax.sharding import PartitionSpec as P

H = 12
EPS = 1e-05
MASKED = -1e30
QUARTERS = 4
ATTEND_VMEM = 58 * 2**20
BF16 = jnp.bfloat16
F32 = jnp.float32
AXES = ("section", "shard", "replica")
NN = (((1,), (0,)), ((), ()))
NT = (((1,), (1,)), ((), ()))
TN = (((0,), (0,)), ((), ()))


def dot(a, b, dims=NN):
    return lax.dot_general(a, b, dims, preferred_element_type=F32)


def layer_norm(values, gain, shift):
    center = values - jnp.mean(values, -1, keepdims=True)
    spread = jnp.mean(center * center, -1, keepdims=True)
    return center * lax.rsqrt(spread + EPS) * gain + shift


def key_chunks(sources, size):
    chunks, base = [], 0
    for source in range(len(sources)):
        rows = sources[source].shape[0]
        for start in range(0, rows, size):
            chunks.append((source, start, base + start))
        base += rows
    return chunks


def attend_kernel(own_ref, other_ref, bias_ref, out_ref, exp_ref, inv_ref, score_ref, *, heads, frames, chunk):
    dim = own_ref.shape[1] // (3 * heads)
    wide = heads * dim
    sources = (own_ref, other_ref)
    chunks = key_chunks(sources, chunk)

    def one_head(head):
        at = head * dim
        query = own_ref[0:frames, 2 * wide + at:2 * wide + at + dim] * (dim ** -0.5)
        lane = lax.broadcasted_iota(jnp.int32, (frames, dim), 1)
        query = jnp.concatenate([query.astype(BF16), (lane == 0).astype(BF16)], 1)
        top = None
        for source, start, row in chunks:
            key = sources[source][start:start + chunk, at:at + dim]
            key = jnp.concatenate([key, bias_ref[row:row + chunk, :]], 1)
            score = dot(key, query, NT)
            score_ref[row:row + chunk, :] = score
            part = jnp.max(score, 0, keepdims=True)
            top = part if top is None else jnp.maximum(top, part)
        total = None
        for source, start, row in chunks:
            weight = jnp.exp(score_ref[row:row + chunk, :] - top).astype(BF16)
            exp_ref[0, row:row + chunk, :] = weight
            value = sources[source][start:start + chunk, wide + at:wide + at + dim]
            value = jnp.concatenate([value, jnp.ones_like(value)], 1)
            part = dot(value, weight, TN)
            total = part if total is None else total + part
        inverse = 1.0 / total[dim:dim + 1, :]
        inv_ref[head:head + 1, :] = inverse
        out_ref[:, at:at + dim] = (total[0:dim, :] * inverse).T.astype(BF16)

    for head in range(heads):
        pl.when(pl.program_id(0) == head)(functools.partial(one_head, head))


def whole_block(shape):
    return pl.BlockSpec(shape, lambda i: (0,) * len(shape))


def chunk_size(own, frames):
    chunk = min(256, frames)
    return frames if own.shape[0] % chunk else chunk


def attend(own, other, bias, heads, frames):
    keys = own.shape[0] + other.shape[0]
    wide = own.shape[1] // 3
    return pl.pallas_call(
        functools.partial(attend_kernel, heads=heads, frames=frames, chunk=chunk_size(own, frames)),
        grid=(heads,),
        in_specs=[whole_block(own.shape), whole_block(other.shape), whole_block(bias.shape)],
        out_specs=[
            whole_block((frames, wide)),
            pl.BlockSpec((1, keys, frames), lambda i: (i, 0, 0)),
            whole_block((heads, frames)),
        ],
        out_shape=(
            jax.ShapeDtypeStruct((frames, wide), BF16),
            jax.ShapeDtypeStruct((heads, keys, frames), BF16),
            jax.ShapeDtypeStruct((heads, frames), F32),
        ),
        scratch_shapes=[pltpu.VMEM((keys, frames), F32)],
        compiler_params=pltpu.CompilerParams(vmem_limit_bytes=ATTEND_VMEM),
        cost_estimate=pl.CostEstimate(
            flops=16 * keys * frames * wide, bytes_accessed=2 * heads * keys * frames, transcendentals=heads * keys * frames
        ),
        name="attend",
    )(own, other, bias)


def attend_back_kernel(own_ref, other_ref, exp_ref, inv_ref, dout_ref, dq_ref, down_ref, dother_ref, prod_ref, *, heads, frames, chunk):
    dim = own_ref.shape[1] // (3 * heads)
    wide = heads * dim
    scale = dim ** -0.5
    sources = (own_ref, other_ref)
    targets = (down_ref, dother_ref)
    chunks = key_chunks(sources, chunk)

    def one_head(head):
        at = head * dim
        query = (own_ref[0:frames, 2 * wide + at:2 * wide + at + dim] * scale).astype(BF16)
        inverse = inv_ref[head:head + 1, :]
        dout_t = dout_ref[:, at:at + dim].astype(F32).T * inverse
        dout = dout_t.T.astype(BF16)
        dout_t = dout_t.astype(BF16)
        delta = None
        for source, start, row in chunks:
            value = sources[source][start:start + chunk, wide + at:wide + at + dim]
            weight = exp_ref[0, row:row + chunk, :]
            prod = dot(value, dout_t) * weight.astype(F32)
            prod_ref[row:row + chunk, :] = prod
            part = jnp.sum(prod, 0, keepdims=True)
            delta = part if delta is None else delta + part
            targets[source][start:start + chunk, wide + at:wide + at + dim] = dot(weight, dout).astype(BF16)
        delta = delta * inverse
        dq_t = None
        for source, start, row in chunks:
            key = sources[source][start:start + chunk, at:at + dim]
            weight = exp_ref[0, row:row + chunk, :].astype(F32)
            ds = (prod_ref[row:row + chunk, :] - weight * delta).astype(BF16)
            targets[source][start:start + chunk, at:at + dim] = dot(ds, query).astype(BF16)
            part = dot(key, ds, TN)
            dq_t = part if dq_t is None else dq_t + part
        dq_ref[:, at:at + dim] = (dq_t.T * scale).astype(BF16)

    for head in range(heads):
        pl.when(pl.program_id(0) == head)(functools.partial(one_head, head))


def attend_back(own, other, weights, inverse, dout, heads, frames):
    keys = own.shape[0] + other.shape[0]
    wide = own.shape[1] // 3
    results = ((frames, wide), (own.shape[0], 2 * wide), (other.shape[0], 2 * wide))
    return pl.pallas_call(
        functools.partial(attend_back_kernel, heads=heads, frames=frames, chunk=chunk_size(own, frames)),
        grid=(heads,),
        in_specs=[
            whole_block(own.shape), whole_block(other.shape),
            pl.BlockSpec((1, keys, frames), lambda i: (i, 0, 0)),
            whole_block(inverse.shape), whole_block(dout.shape),
        ],
        out_specs=[whole_block(shape) for shape in results],
        out_shape=[jax.ShapeDtypeStruct(shape, BF16) for shape in results],
        scratch_shapes=[pltpu.VMEM((keys, frames), F32)],
        compiler_params=pltpu.CompilerParams(vmem_limit_bytes=ATTEND_VMEM),
        cost_estimate=pl.CostEstimate(
            flops=32 * keys * frames * wide, bytes_accessed=2 * heads * keys * frames, transcendentals=0
        ),
        name="attend_back",
    )(own, other, weights, inverse, dout)


def out_kernel(quarter_ref, a_ref, b_ref, c_ref, d_ref, weight_ref, x_ref, vec_ref, att_ref, mid_ref, norm_ref):
    parts = [ref[...] for ref in (a_ref, b_ref, c_ref, d_ref)]
    attended = jnp.concatenate(in_order(parts, quarter_ref[0]), 1)
    att_ref[...] = attended
    middle = x_ref[...].astype(F32) + dot(attended, weight_ref[...]) + vec_ref[4:5, :]
    mid_ref[...] = middle
    norm_ref[...] = layer_norm(middle, vec_ref[5:6, :], vec_ref[6:7, :]).astype(BF16)


def scalar_first(count):
    return [pl.BlockSpec(memory_space=pltpu.SMEM)] + [pl.BlockSpec(memory_space=pltpu.VMEM)] * count


def out_part(quarter, outs, weight, x_low, vec):
    shape = x_low.shape
    return pl.pallas_call(
        out_kernel,
        in_specs=scalar_first(7),
        out_shape=[jax.ShapeDtypeStruct(shape, kind) for kind in (BF16, F32, BF16)],
        compiler_params=pltpu.CompilerParams(vmem_limit_bytes=32 * 2**20),
        cost_estimate=pl.CostEstimate(
            flops=2 * math.prod(shape) * shape[1], bytes_accessed=14 * math.prod(shape), transcendentals=0
        ),
        name="out_part",
    )(quarter.reshape(1), *outs, weight, x_low, vec)


def norm_back(values, gain, grad):
    center = values - jnp.mean(values, -1, keepdims=True)
    inv = lax.rsqrt(jnp.mean(center * center, -1, keepdims=True) + EPS)
    unit_values = center * inv
    scaled = grad * gain
    back = inv * (
        scaled - jnp.mean(scaled, -1, keepdims=True)
        - unit_values * jnp.mean(scaled * unit_values, -1, keepdims=True)
    )
    return back, jnp.sum(grad * unit_values, 0, keepdims=True), jnp.sum(grad, 0, keepdims=True)


def middle_back_kernel(quarter_ref, grad_ref, mid_ref, cot_ref, vec_ref, weight_ref, dmid_ref, rows_ref, *part_refs):
    cot = cot_ref[...].astype(F32)
    back, gain, shift = norm_back(mid_ref[...], vec_ref[5:6, :], grad_ref[...])
    d_middle = cot + back
    dmid_ref[...] = d_middle
    d_attn = d_middle.astype(BF16)
    d_low = d_attn.astype(F32)
    rows_ref[...] = jnp.concatenate(
        [gain, shift, jnp.sum(d_low, 0, keepdims=True), jnp.sum(cot, 0, keepdims=True)], 0
    )
    d_attended = dot(d_attn, weight_ref[...], NT).astype(BF16)
    for refs, whole in ((part_refs[:QUARTERS], d_attended), (part_refs[QUARTERS:], d_attn)):
        wide = whole.shape[1] // QUARTERS
        parts = in_order([whole[:, p * wide:(p + 1) * wide] for p in range(QUARTERS)], quarter_ref[0])
        for ref, part in zip(refs, parts):
            ref[...] = part


def middle_back(quarter, grad, middle, cot, vec, weight):
    frames, width = middle.shape
    part = jax.ShapeDtypeStruct((frames, width // QUARTERS), BF16)
    results = pl.pallas_call(
        middle_back_kernel,
        in_specs=scalar_first(5),
        out_shape=[jax.ShapeDtypeStruct((frames, width), F32), jax.ShapeDtypeStruct((4, width), F32)]
        + [part] * (2 * QUARTERS),
        compiler_params=pltpu.CompilerParams(vmem_limit_bytes=32 * 2**20),
        cost_estimate=pl.CostEstimate(
            flops=2 * frames * width * width, bytes_accessed=18 * frames * width, transcendentals=0
        ),
        name="middle_back",
    )(quarter.reshape(1), grad, middle, cot, vec, weight)
    return results[0], results[1], results[2:2 + QUARTERS], results[2 + QUARTERS:]


def vector_kernel(quarter_ref, *refs, shards):
    ins, up_ins = refs[:QUARTERS], refs[QUARTERS:2 * QUARTERS]
    gain_ref, shift_ref, mid_ref, out_ref = refs[2 * QUARTERS:]
    width = out_ref.shape[0]
    wide, unit = width // QUARTERS, width // shards
    ins = in_order([ref[...] for ref in ins], quarter_ref[0])
    value_row, query_row = (
        jnp.concatenate([piece[:, i * wide:(i + 1) * wide] for piece in ins], 1) for i in range(1, 3)
    )
    ups = in_order([ref[...] for ref in up_ins], quarter_ref[0])
    up_row = jnp.concatenate(
        [piece[:, shard * unit:(shard + 1) * unit] for shard in range(shards) for piece in ups], 1
    )
    rows = [gain_ref[...], shift_ref[...], query_row, value_row, mid_ref[2:3, :], mid_ref[0:2, :], mid_ref[3:4, :]]
    rows += [up_row[:, start:start + width] for start in range(0, up_row.shape[1], width)]
    rows = jnp.concatenate(rows, 0)
    rows = jnp.concatenate([rows, jnp.zeros((128 - rows.shape[0], width), F32)], 0)
    out_ref[...] = rows.T.astype(BF16)


def vector_block(quarter, sums_in, up_sums, gain, shift, mid_rows, shards):
    width = gain.shape[1]
    return pl.pallas_call(
        functools.partial(vector_kernel, shards=shards),
        in_specs=scalar_first(2 * QUARTERS + 3),
        out_shape=jax.ShapeDtypeStruct((width, 128), BF16),
        compiler_params=pltpu.CompilerParams(vmem_limit_bytes=32 * 2**20),
        cost_estimate=pl.CostEstimate(flops=128 * width, bytes_accessed=512 * width, transcendentals=0),
        name="vector_block",
    )(quarter.reshape(1), *sums_in, *up_sums, gain, shift, mid_rows)


def column_tile(columns):
    return 256 if columns % 256 == 0 else columns


def mlp_kernel(in_ref, up_ref, bias_ref, down_ref, before_ref, act_ref, slope_ref, sum_ref):
    up = dot(in_ref[...], up_ref[...]) + bias_ref[...]
    cdf = 0.5 + 0.5 * lax.erf(up * (0.5 ** 0.5))
    pdf = jnp.exp(-0.5 * up * up) * 0.3989422804014327
    act = (up * cdf).astype(BF16)
    act_ref[...] = act
    slope_ref[...] = (cdf + up * pdf).astype(BF16)
    part = dot(act, down_ref[...])

    @pl.when(pl.program_id(0) == 0)
    def _():
        sum_ref[...] = before_ref[...] + part

    @pl.when(pl.program_id(0) > 0)
    def _():
        sum_ref[...] += part


def mlp_part(values, up, bias, down, before):
    rows, depth = values.shape
    columns = up.shape[1]
    tile = column_tile(columns)
    whole = pl.BlockSpec((rows, depth), lambda i: (0, 0))
    hidden = pl.BlockSpec((rows, tile), lambda i: (0, i))
    return pl.pallas_call(
        mlp_kernel,
        grid=(columns // tile,),
        in_specs=[
            whole,
            pl.BlockSpec((depth, tile), lambda i: (0, i)),
            pl.BlockSpec((1, tile), lambda i: (0, i)),
            pl.BlockSpec((tile, depth), lambda i: (i, 0)),
            whole,
        ],
        out_specs=[hidden, hidden, whole],
        out_shape=[
            jax.ShapeDtypeStruct((rows, columns), BF16),
            jax.ShapeDtypeStruct((rows, columns), BF16),
            jax.ShapeDtypeStruct((rows, depth), F32),
        ],
        compiler_params=pltpu.CompilerParams(vmem_limit_bytes=32 * 2**20),
        cost_estimate=pl.CostEstimate(
            flops=4 * rows * depth * columns, bytes_accessed=4 * (3 * rows * depth + depth * columns + rows * columns),
            transcendentals=2 * rows * columns,
        ),
        name="mlp_part",
    )(values, up, bias, down, before)


def mlp_back_kernel(grad_ref, in_ref, act_ref, slope_ref, up_ref, down_ref, before_ref, gd_ref, gu_ref, row_ref, sum_ref):
    grad = grad_ref[...]
    d_up = (dot(grad, down_ref[...], NT) * slope_ref[...].astype(F32)).astype(BF16)
    gd_ref[...] = dot(act_ref[...], grad, TN).astype(BF16)
    gu_ref[...] = dot(in_ref[...], d_up, TN).astype(BF16)
    row_ref[...] = jnp.sum(d_up.astype(F32), 0, keepdims=True)
    part = dot(d_up, up_ref[...], NT)

    @pl.when(pl.program_id(0) == 0)
    def _():
        sum_ref[...] = before_ref[...] + part

    @pl.when(pl.program_id(0) > 0)
    def _():
        sum_ref[...] += part


def mlp_back_part(grad, values, act, slope, up, down, before):
    rows, depth = values.shape
    columns = up.shape[1]
    tile = column_tile(columns)
    whole = pl.BlockSpec((rows, depth), lambda i: (0, 0))
    hidden = pl.BlockSpec((rows, tile), lambda i: (0, i))
    up_tile = pl.BlockSpec((depth, tile), lambda i: (0, i))
    down_tile = pl.BlockSpec((tile, depth), lambda i: (i, 0))
    return pl.pallas_call(
        mlp_back_kernel,
        grid=(columns // tile,),
        in_specs=[whole, whole, hidden, hidden, up_tile, down_tile, whole],
        out_specs=[down_tile, up_tile, pl.BlockSpec((1, tile), lambda i: (0, i)), whole],
        out_shape=[
            jax.ShapeDtypeStruct((columns, depth), BF16),
            jax.ShapeDtypeStruct((depth, columns), BF16),
            jax.ShapeDtypeStruct((1, columns), F32),
            jax.ShapeDtypeStruct((rows, depth), F32),
        ],
        compiler_params=pltpu.CompilerParams(vmem_limit_bytes=40 * 2**20),
        cost_estimate=pl.CostEstimate(
            flops=8 * rows * depth * columns, bytes_accessed=4 * (3 * rows * depth + 2 * depth * columns + rows * columns),
            transcendentals=0,
        ),
        name="mlp_back_part",
    )(grad, values, act, slope, up, down, before)


def proj_back_kernel(in_ref, own_ref, other_ref, query_ref, out_ref, grad_ref, weight_ref, before_ref, g_ref, row_ref, sum_ref):
    frames, wide = query_ref.shape
    both = (own_ref[...].astype(F32) + other_ref[...].astype(F32)).astype(BF16)
    query = query_ref[...]
    values = in_ref[...]
    g_ref[...] = jnp.concatenate(
        [dot(values, both, TN), dot(values[:frames], query, TN), dot(out_ref[...], grad_ref[...], TN)], 1
    ).astype(BF16)
    row_ref[...] = jnp.concatenate(
        [jnp.sum(both.astype(F32), 0, keepdims=True), jnp.sum(query.astype(F32), 0, keepdims=True)], 1
    )
    total = before_ref[...] + dot(both, weight_ref[:, :2 * wide], NT)
    own = total[:frames] + dot(query, weight_ref[:, 2 * wide:3 * wide], NT)
    sum_ref[0:frames, :] = own
    sum_ref[frames:, :] = total[frames:]


def proj_back(values, own, other, query, out, grad, weight, before):
    rows, depth = values.shape
    wide = query.shape[1]
    return pl.pallas_call(
        proj_back_kernel,
        out_shape=[
            jax.ShapeDtypeStruct(weight.shape, BF16),
            jax.ShapeDtypeStruct((1, 3 * wide), F32),
            jax.ShapeDtypeStruct((rows, depth), F32),
        ],
        compiler_params=pltpu.CompilerParams(vmem_limit_bytes=40 * 2**20),
        cost_estimate=pl.CostEstimate(
            flops=8 * rows * depth * 2 * wide, bytes_accessed=12 * rows * depth + 4 * depth * weight.shape[1],
            transcendentals=0,
        ),
        name="proj_back",
    )(values, own, other, query, out, grad, weight, before)


def place_proj_kernel(quarter_ref, a_ref, b_ref, c_ref, d_ref, qkv_ref, out_ref, vec_ref):
    pieces = [ref[...].astype(F32) for ref in (a_ref, b_ref, c_ref, d_ref)]
    width = out_ref.shape[1]
    wide = width // QUARTERS
    total = pieces[0][:, width:] + pieces[1][:, width:] + pieces[2][:, width:] + pieces[3][:, width:]
    vec_ref[...] = total.T
    pieces = in_order([piece[:, :width] for piece in pieces], quarter_ref[0])
    for column, part in ((0, 2), (1, 0), (2, 1)):
        qkv_ref[:, column * width:(column + 1) * width] = jnp.concatenate(
            [piece[:, part * wide:(part + 1) * wide] for piece in pieces], 1
        )
    out_ref[...] = jnp.concatenate([piece[:, 3 * wide:] for piece in pieces], 1)


def place_mlp_kernel(quarter_ref, a_ref, b_ref, c_ref, d_ref, down_ref, up_ref, *, shards):
    pieces = in_order([ref[...].astype(F32) for ref in (a_ref, b_ref, c_ref, d_ref)], quarter_ref[0])
    rows, width = pieces[0].shape[0], pieces[0].shape[1] // 2
    unit = width // shards
    for place in range(QUARTERS):
        down_ref[place * rows:(place + 1) * rows, :] = pieces[place][:, :width]
    for shard in range(shards):
        start = width + shard * unit
        up_ref[:, shard * QUARTERS * unit:(shard + 1) * QUARTERS * unit] = jnp.concatenate(
            [piece[:, start:start + unit] for piece in pieces], 1
        )


def placed_parts(kernel, quarter, pieces, shapes):
    size = sum(math.prod(shape) for shape in shapes)
    return pl.pallas_call(
        kernel,
        in_specs=scalar_first(QUARTERS),
        out_shape=[jax.ShapeDtypeStruct(shape, F32) for shape in shapes],
        compiler_params=pltpu.CompilerParams(vmem_limit_bytes=32 * 2**20),
        cost_estimate=pl.CostEstimate(flops=size, bytes_accessed=6 * size, transcendentals=0),
        name="placed_parts",
    )(quarter.reshape(1), *pieces)


def across(block, bit):
    count = lax.axis_size("replica")
    return lax.ppermute(block, "replica", [(i, i ^ bit) for i in range(count)])


def swap_sections(block):
    return lax.ppermute(block, "section", [(0, 1), (1, 0)])


def reversed_bits(index, count):
    result, bit = index * 0, 1
    while bit < count:
        result = result * 2 + index // bit % 2
        bit *= 2
    return result


def transposed(block, source, target):
    shards, replicas = lax.axis_size("shard"), lax.axis_size("replica")

    def flat(section, shard, replica):
        return (section * shards + shard) * replicas + replica

    route = []
    for shard in range(shards):
        for replica in range(replicas):
            group, place = divmod(replica, shards)
            here = (shard, replica)
            there = (reversed_bits(place, shards), group * shards + reversed_bits(shard, shards))
            if source is None:
                route += [(flat(s, *here), flat(s, *there)) for s in range(2)]
            else:
                route.append((flat(source, *here), flat(target, *there)))
    return lax.ppermute(block, AXES, route)


def in_order(pieces, quarter):
    odd, high = (quarter & 1) == 1, (quarter & 2) == 2
    a, b, c, d = pieces
    a, b, c, d = jnp.where(odd, b, a), jnp.where(odd, a, b), jnp.where(odd, d, c), jnp.where(odd, c, d)
    return jnp.where(high, c, a), jnp.where(high, d, b), jnp.where(high, a, c), jnp.where(high, b, d)


def after(value, *others):
    return lax.optimization_barrier((value, others))[0]


def spread(piece, far):
    return piece, across(piece, 1), far, across(far, 1)


def low_sum(*parts):
    total = parts[0].astype(F32)
    for part in parts[1:]:
        total = total + part.astype(F32)
    return total.astype(BF16)


def body(edges, attn_in, attn_out, mlp_up, mlp_down, vectors, key_mask):
    section = lax.axis_index("section")
    first = section == 0
    replica = lax.axis_index("replica")
    shards, replicas = lax.axis_size("shard"), lax.axis_size("replica")
    quarter = replica % QUARTERS
    edges_here = edges[0]
    clips, frames, width = edges_here.shape
    hidden = mlp_up.shape[2]
    dim = width // H
    heads = H // QUARTERS
    wide = heads * dim
    unit = hidden // (shards * QUARTERS)
    rows = attn_in.shape[1]
    assert clips == 2 and lax.axis_size("section") == 2 and replicas % shards == 0 and replicas % QUARTERS == 0

    def by_layer(own, other):
        return jnp.where(first, own, other), jnp.where(first, other, own)

    vec_by_layer = by_layer(vectors[0], swap_sections(vectors[0]))
    mask_row = transposed(
        lax.dynamic_index_in_dim(key_mask, section, 0, keepdims=False).astype(F32)[None], None, None
    )[0]
    inputs = jnp.where(first, transposed(edges_here[0], 0, 0), transposed(edges_here[1], 0, 1))

    def pick(block, axis):
        return lax.dynamic_index_in_dim(block, quarter, axis, keepdims=False)

    def gathered(block):
        return lax.all_gather(block, "shard", axis=0, tiled=True)

    query_in, key_in, value_in = (
        pick(attn_in[0][:, i * width:(i + 1) * width].reshape(rows, QUARTERS, wide), 1) for i in range(3)
    )
    own_proj = jnp.concatenate(
        [key_in, value_in, query_in, pick(attn_out[0].reshape(rows, QUARTERS, width // QUARTERS), 1)], 1
    )
    own_up = pick(mlp_up[0].reshape(rows, shards, QUARTERS, unit), 2).reshape(rows, shards * unit)
    own_down = pick(mlp_down[0].reshape(QUARTERS, unit, width), 0)
    proj_zero, proj_one = by_layer(own_proj, swap_sections(own_proj))
    proj_zero = gathered(proj_zero)
    own_up = after(own_up, inputs)
    own_down = after(own_down, own_up)
    proj_one = after(proj_one, own_down)
    own_up, own_down, proj_one = gathered(own_up), gathered(own_down), gathered(proj_one)
    other_up, other_down = swap_sections(own_up), swap_sections(own_down)

    def head_weights(block):
        pieces = spread(block, across(block, 2))
        return pieces, jnp.concatenate(in_order([piece[:, 3 * wide:] for piece in pieces], quarter), 1)

    heads_by_layer = [head_weights(proj_zero), None]
    hidden_by_layer = [None, None]

    members = [0]
    bit = 2
    while bit < shards:
        members = members + [m ^ bit for m in members]
        bit *= 2
    members = members + [m ^ 1 for m in members]
    place = replica % shards
    bias_row = jnp.concatenate(
        [lax.dynamic_slice_in_dim(mask_row, reversed_bits(place ^ m, shards) * frames, frames, 0) for m in members]
    )
    bias_row = jnp.where(bias_row > 0, 0.0, MASKED).astype(BF16)
    lane = jnp.arange(dim)[None, :]
    key_bias = jnp.where(lane == 0, bias_row[:, None], jnp.zeros((), BF16))

    def chips_rows(block):
        bit = 2
        while bit < shards:
            block = jnp.concatenate([block, across(block, bit)], 0)
            bit *= 2
        return block

    def forward(x_low, layer):
        vec = vec_by_layer[layer]
        x_set = chips_rows(x_low)
        proj, w_out = heads_by_layer[layer]
        normed = layer_norm(x_set.astype(F32), vec[0], vec[1]).astype(BF16)
        zeros = jnp.zeros((QUARTERS, wide), F32)
        bias_in = jnp.stack([zeros, vec[3].reshape(QUARTERS, wide), vec[2].reshape(QUARTERS, wide)], 1)
        own_qkv, other_kv = {}, {}
        order = (0, 1, 2, 3)
        for p in order:
            bias = lax.dynamic_index_in_dim(bias_in, quarter ^ p, 0, keepdims=False).reshape(3 * wide)
            own_qkv[p] = (dot(normed, proj[p][:, :3 * wide]) + bias).astype(BF16)
            other_kv[p ^ 1] = across(own_qkv[p][:, :2 * wide], 1)
        outs, weights, inverses = {}, {}, {}
        late = {}
        for step, p in enumerate(order):
            own = own_qkv[p]
            if layer == 0 and step == 3:
                own = after(own, proj_one)
            outs[p], weights[p], inverses[p] = attend(own, other_kv[p], key_bias, heads, frames)
            if layer == 0 and step == 0:
                late["up"] = by_layer(own_up, after(other_up, outs[p]))
                late["up_far"] = across(late["up"][0], 2)
            elif layer == 0 and step == 1:
                late["down"] = by_layer(own_down, after(other_down, outs[p]))
                late["down_far"] = across(late["down"][0], 2)
            elif layer == 0 and step == 2:
                w_up = spread(late["up"][0], after(late["up_far"], outs[p]))
                late["one_far"] = across(after(proj_one, outs[p]), 2)
            elif layer == 0 and step == 3:
                w_down = spread(late["down"][0], after(late["down_far"], outs[p]))
                hidden_by_layer[0] = (w_up, w_down)
            elif layer == 1 and step == 0:
                late["down_far"] = across(after(pending_one["down"], outs[p]), 2)
            elif layer == 1 and step == 1:
                cot = after(edges_here, outs[p])
                pending_one["cot"] = [transposed(cot[0], 1, 0), transposed(cot[1], 1, 1)]
                w_up = spread(pending_one["up"], after(pending_one["up_far"], outs[p]))
            elif layer == 1 and step == 3:
                w_down = spread(pending_one["down"], after(late["down_far"], outs[p]))
                hidden_by_layer[1] = (w_up, w_down)
        attended, middle, normed_two = out_part(quarter, [outs[p] for p in range(QUARTERS)], w_out, x_low, vec)
        w_up, w_down = hidden_by_layer[layer]
        bias_up = vec[8:].reshape(shards, QUARTERS, unit)
        acts, slopes = [], []
        result = middle + vec[7]
        for p in range(QUARTERS):
            bias = lax.dynamic_index_in_dim(bias_up, quarter ^ p, 1, keepdims=False).reshape(1, shards * unit)
            act, slope, result = mlp_part(normed_two, w_up[p], bias, w_down[p], result)
            acts.append(act)
            slopes.append(slope)
            if layer == 0 and p == 0:
                far = after(late["one_far"], act)
                pieces = spread(proj_one, far)
                w_out_one = jnp.concatenate(in_order([piece[:, 3 * wide:] for piece in pieces], quarter), 1)
                heads_by_layer[1] = (pieces, w_out_one)
                pending_one["up"], pending_one["down"] = late["up"][1], late["down"][1]
                pending_one["up_far"] = across(after(pending_one["up"], far), 2)
        kept = (x_low, normed, own_qkv, other_kv, weights, inverses, attended, middle, normed_two, acts, slopes)
        return result.astype(BF16), kept

    pending_one = {}

    def scattered(block):
        bit = QUARTERS
        while bit < replicas:
            block = low_sum(block, across(block, bit))
            bit *= 2
        return lax.psum_scatter(block, "shard", scatter_dimension=0, tiled=True)

    def half_sum(block):
        cut = block.shape[1] // 2
        left, right = block[:, :cut], block[:, cut:]
        return low_sum(jnp.where(first, left, right), swap_sections(jnp.where(first, right, left)))

    def backward(cot, layer, kept, above):
        (proj, w_out), (w_up, w_down), vec = heads_by_layer[layer], hidden_by_layer[layer], vec_by_layer[layer]
        x_low, normed, own_qkv, other_kv, weights, inverses, attended, middle, normed_two, acts, slopes = kept
        order = (3, 1, 2, 0)
        g_down, g_up, up_sums, near_down, near_up = {}, {}, {}, {}, {}
        d_normed_two = jnp.zeros((frames, width), F32)
        for step, p in enumerate(order):
            g_down[p], g_up[p], up_sums[p], d_normed_two = mlp_back_part(
                cot, normed_two, acts[p], slopes[p], w_up[p], w_down[p], d_normed_two
            )
            if p & 1:
                near_down[p ^ 1] = across(g_down[p], 1)
                near_up[p ^ 1] = across(g_up[p], 1)
            if above is not None and step == 1:
                halves = [after(half, g_up[p]) for half in above["halves"]]
                above["mlp"] = scattered(jnp.concatenate(halves, 1))
        d_middle, mid_rows, d_heads, d_attn_parts = middle_back(quarter, d_normed_two, middle, cot, vec, w_out)
        if above is not None:
            far = after(above["far_proj"], mid_rows)
            above["half"] = half_sum(above["finish"](far))
        far_down = low_sum(g_down[2], after(near_down[2], mid_rows))
        results = {}
        for step, p in enumerate(order):
            head = d_heads[p]
            if step == 1:
                head = after(head, far_down)
                far_down = across(far_down, 2)
            elif step == 2:
                head = after(head, far_up)
                far_up = across(far_up, 2)
                if above is not None:
                    half = after(above["half"], results[order[1]][0])
                    above["proj"] = scattered(jnp.concatenate([half, above["vec"]], 1))
            elif step == 3 and above is not None:
                head = after(head, above["mlp"])
            results[p] = attend_back(own_qkv[p], other_kv[p], weights[p], inverses[p], head, heads, frames)
            if step == 0:
                far_up = low_sum(g_up[2], after(near_up[2], results[p][0]))
        last = results[order[3]][0]
        from_other = {p: across(results[p ^ 1][2], 1) for p in range(QUARTERS)}
        half_down = half_sum(low_sum(g_down[0], near_down[0], after(far_down, last)))
        g_proj, sums_in, near_proj = {}, {}, {}
        d_normed = jnp.zeros(normed.shape, F32)
        for p in order:
            g_proj[p], sums_in[p], d_normed = proj_back(
                normed, results[p][1], from_other[p], results[p][0], attended, d_attn_parts[p], proj[p], d_normed
            )
            if p & 1:
                near_proj[p ^ 1] = across(g_proj[p], 1)
        block = d_normed
        bit = shards // 2
        while bit >= 2:
            cut = block.shape[0] // 2
            block = block[:cut] + across(block[cut:].astype(BF16), bit).astype(F32)
            bit //= 2
        half_up = half_sum(low_sum(g_up[0], near_up[0], after(far_up, d_normed)))
        if layer == 1:
            far_proj = low_sum(g_proj[2], after(near_proj[2], block))
        else:
            far_proj = low_sum(g_proj[2], after(near_proj[2], d_normed))
        back, g_gain_one, g_shift_one = norm_back(x_low.astype(F32), vec[0], block)
        g_low = (d_middle + back).astype(BF16)
        g_low = after(g_low, far_proj)
        far_proj = across(far_proj, 2)
        vec_block = vector_block(
            quarter, [sums_in[p] for p in range(QUARTERS)], [up_sums[p] for p in range(QUARTERS)],
            g_gain_one, g_shift_one, mid_rows, shards,
        )
        if above is not None:
            g_low = after(g_low, above["proj"])

        def finish_proj(other):
            return low_sum(g_proj[0], near_proj[0], other)

        return g_low, {"halves": [half_down, half_up], "far_proj": far_proj, "finish": finish_proj, "vec": vec_block}

    x_one, kept_zero = forward(inputs, 0)
    y_one, kept_one = forward(x_one, 1)
    cot = [after(part, y_one) for part in pending_one["cot"]]
    g_one, one = backward(jnp.where(first, cot[0], cot[1]), 1, kept_one, None)
    g_zero, zero = backward(g_one, 0, kept_zero, one)
    y_one = after(y_one, g_one)
    out_slots = [transposed(y_one, 0, 1), transposed(y_one, 1, 1)]
    back_slots = [transposed(g_zero, 0, 0), transposed(g_zero, 1, 0)]
    edges_out = jnp.stack([jnp.where(first, b, o) for b, o in zip(back_slots, out_slots)])
    mlp_one, proj_one = one["mlp"], one["proj"]
    mlp_zero = scattered(jnp.concatenate([after(half, g_zero) for half in zero["halves"]], 1))
    far = after(zero["far_proj"], g_zero)
    proj_zero = scattered(jnp.concatenate([half_sum(zero["finish"](far)), zero["vec"]], 1))

    def exchanged(zero, one):
        return jnp.where(first, zero, one), swap_sections(jnp.where(first, one, zero))

    def joined(own, other):
        cut = width // 2
        parts = []
        for start in range(0, own.shape[1], cut):
            a, b = own[:, start:start + cut], other[:, start:start + cut]
            parts += [jnp.where(first, a, b), jnp.where(first, b, a)]
        return parts

    part = jnp.concatenate(joined(*exchanged(mlp_zero, mlp_one)), 1)
    f_down, f_up = placed_parts(
        functools.partial(place_mlp_kernel, shards=shards), quarter, spread(part, across(part, 2)),
        [mlp_down.shape[1:], mlp_up.shape[1:]],
    )
    own, other = exchanged(proj_zero, proj_one)
    cut = width // 2
    part = jnp.concatenate(
        joined(own[:, :cut], other[:, :cut]) + [low_sum(own[:, cut:], other[:, cut:])], 1
    )
    f_in, f_out, f_vec = placed_parts(
        place_proj_kernel, quarter, spread(part, across(part, 2)),
        [attn_in.shape[1:], attn_out.shape[1:], (128, rows)],
    )
    f_vec = f_vec[:vectors.shape[1]]
    return edges_out[None], f_in[None], f_out[None], f_up[None], f_down[None], f_vec[None]


def solution(mesh):
    placed = (
        P("section", "replica", "shard", None),
        P("section", "shard", None),
        P("section", "shard", None),
        P("section", "shard", None),
        P("section", "shard", None),
        P("section", None, None),
        P("replica", None),
    )
    return jax.shard_map(
        body,
        mesh=mesh,
        in_specs=placed,
        out_specs=(
            P("section", "replica", "shard", None),
            P("section", "shard", None),
            P("section", "shard", None),
            P("section", "shard", None),
            P("section", "shard", None),
            P("section", None, "shard"),
        ),
        check_vma=False,
    )
```

```python
import functools
import math

import jax
import jax.numpy as jnp
from jax import lax
from jax.experimental import pallas as pl
from jax.experimental.pallas import tpu as pltpu
from jax.sharding import PartitionSpec as P

H = 12
EPS = 1e-05
MASKED = -1e30
QUARTERS = 4
ATTEND_VMEM = 58 * 2**20
BF16 = jnp.bfloat16
F32 = jnp.float32
AXES = ("section", "shard", "replica")
NN = (((1,), (0,)), ((), ()))
NT = (((1,), (1,)), ((), ()))
TN = (((0,), (0,)), ((), ()))


def dot(a, b, dims=NN):
    return lax.dot_general(a, b, dims, preferred_element_type=F32)


def layer_norm(values, gain, shift):
    center = values - jnp.mean(values, -1, keepdims=True)
    spread = jnp.mean(center * center, -1, keepdims=True)
    return center * lax.rsqrt(spread + EPS) * gain + shift


def key_chunks(sources, size):
    chunks, base = [], 0
    for source in range(len(sources)):
        rows = sources[source].shape[0]
        for start in range(0, rows, size):
            chunks.append((source, start, base + start))
        base += rows
    return chunks


def attend_kernel(own_ref, other_ref, bias_ref, out_ref, exp_ref, inv_ref, score_ref, *, heads, frames, chunk):
    dim = own_ref.shape[1] // (3 * heads)
    wide = heads * dim
    sources = (own_ref, other_ref)
    chunks = key_chunks(sources, chunk)

    def one_head(head):
        at = head * dim
        query = own_ref[0:frames, 2 * wide + at:2 * wide + at + dim] * (dim ** -0.5)
        lane = lax.broadcasted_iota(jnp.int32, (frames, dim), 1)
        query = jnp.concatenate([query.astype(BF16), (lane == 0).astype(BF16)], 1)
        top = None
        for source, start, row in chunks:
            key = sources[source][start:start + chunk, at:at + dim]
            key = jnp.concatenate([key, bias_ref[row:row + chunk, :]], 1)
            score = dot(key, query, NT)
            score_ref[row:row + chunk, :] = score
            part = jnp.max(score, 0, keepdims=True)
            top = part if top is None else jnp.maximum(top, part)
        total = None
        for source, start, row in chunks:
            weight = jnp.exp(score_ref[row:row + chunk, :] - top).astype(BF16)
            exp_ref[0, row:row + chunk, :] = weight
            value = sources[source][start:start + chunk, wide + at:wide + at + dim]
            value = jnp.concatenate([value, jnp.ones_like(value)], 1)
            part = dot(value, weight, TN)
            total = part if total is None else total + part
        inverse = 1.0 / total[dim:dim + 1, :]
        inv_ref[head:head + 1, :] = inverse
        out_ref[:, at:at + dim] = (total[0:dim, :] * inverse).T.astype(BF16)

    for head in range(heads):
        pl.when(pl.program_id(0) == head)(functools.partial(one_head, head))


def whole_block(shape):
    return pl.BlockSpec(shape, lambda i: (0,) * len(shape))


def chunk_size(own, frames):
    chunk = min(256, frames)
    return frames if own.shape[0] % chunk else chunk


def attend(own, other, bias, heads, frames):
    keys = own.shape[0] + other.shape[0]
    wide = own.shape[1] // 3
    return pl.pallas_call(
        functools.partial(attend_kernel, heads=heads, frames=frames, chunk=chunk_size(own, frames)),
        grid=(heads,),
        in_specs=[whole_block(own.shape), whole_block(other.shape), whole_block(bias.shape)],
        out_specs=[
            whole_block((frames, wide)),
            pl.BlockSpec((1, keys, frames), lambda i: (i, 0, 0)),
            whole_block((heads, frames)),
        ],
        out_shape=(
            jax.ShapeDtypeStruct((frames, wide), BF16),
            jax.ShapeDtypeStruct((heads, keys, frames), BF16),
            jax.ShapeDtypeStruct((heads, frames), F32),
        ),
        scratch_shapes=[pltpu.VMEM((keys, frames), F32)],
        compiler_params=pltpu.CompilerParams(vmem_limit_bytes=ATTEND_VMEM),
        cost_estimate=pl.CostEstimate(
            flops=16 * keys * frames * wide, bytes_accessed=2 * heads * keys * frames, transcendentals=heads * keys * frames
        ),
        name="attend",
    )(own, other, bias)


def attend_back_kernel(own_ref, other_ref, exp_ref, inv_ref, dout_ref, dq_ref, down_ref, dother_ref, prod_ref, *, heads, frames, chunk):
    dim = own_ref.shape[1] // (3 * heads)
    wide = heads * dim
    scale = dim ** -0.5
    sources = (own_ref, other_ref)
    targets = (down_ref, dother_ref)
    chunks = key_chunks(sources, chunk)

    def one_head(head):
        at = head * dim
        query = (own_ref[0:frames, 2 * wide + at:2 * wide + at + dim] * scale).astype(BF16)
        inverse = inv_ref[head:head + 1, :]
        dout_t = dout_ref[:, at:at + dim].astype(F32).T * inverse
        dout = dout_t.T.astype(BF16)
        dout_t = dout_t.astype(BF16)
        delta = None
        for source, start, row in chunks:
            value = sources[source][start:start + chunk, wide + at:wide + at + dim]
            weight = exp_ref[0, row:row + chunk, :]
            prod = dot(value, dout_t) * weight.astype(F32)
            prod_ref[row:row + chunk, :] = prod
            part = jnp.sum(prod, 0, keepdims=True)
            delta = part if delta is None else delta + part
            targets[source][start:start + chunk, wide + at:wide + at + dim] = dot(weight, dout).astype(BF16)
        delta = delta * inverse
        dq_t = None
        for source, start, row in chunks:
            key = sources[source][start:start + chunk, at:at + dim]
            weight = exp_ref[0, row:row + chunk, :].astype(F32)
            ds = (prod_ref[row:row + chunk, :] - weight * delta).astype(BF16)
            targets[source][start:start + chunk, at:at + dim] = dot(ds, query).astype(BF16)
            part = dot(key, ds, TN)
            dq_t = part if dq_t is None else dq_t + part
        dq_ref[:, at:at + dim] = (dq_t.T * scale).astype(BF16)

    for head in range(heads):
        pl.when(pl.program_id(0) == head)(functools.partial(one_head, head))


def attend_back(own, other, weights, inverse, dout, heads, frames):
    keys = own.shape[0] + other.shape[0]
    wide = own.shape[1] // 3
    results = ((frames, wide), (own.shape[0], 2 * wide), (other.shape[0], 2 * wide))
    return pl.pallas_call(
        functools.partial(attend_back_kernel, heads=heads, frames=frames, chunk=chunk_size(own, frames)),
        grid=(heads,),
        in_specs=[
            whole_block(own.shape), whole_block(other.shape),
            pl.BlockSpec((1, keys, frames), lambda i: (i, 0, 0)),
            whole_block(inverse.shape), whole_block(dout.shape),
        ],
        out_specs=[whole_block(shape) for shape in results],
        out_shape=[jax.ShapeDtypeStruct(shape, BF16) for shape in results],
        scratch_shapes=[pltpu.VMEM((keys, frames), F32)],
        compiler_params=pltpu.CompilerParams(vmem_limit_bytes=ATTEND_VMEM),
        cost_estimate=pl.CostEstimate(
            flops=32 * keys * frames * wide, bytes_accessed=2 * heads * keys * frames, transcendentals=0
        ),
        name="attend_back",
    )(own, other, weights, inverse, dout)


def out_kernel(quarter_ref, a_ref, b_ref, c_ref, d_ref, weight_ref, x_ref, vec_ref, att_ref, mid_ref, norm_ref):
    parts = [ref[...] for ref in (a_ref, b_ref, c_ref, d_ref)]
    attended = jnp.concatenate(in_order(parts, quarter_ref[0]), 1)
    att_ref[...] = attended
    middle = x_ref[...].astype(F32) + dot(attended, weight_ref[...]) + vec_ref[4:5, :]
    mid_ref[...] = middle
    norm_ref[...] = layer_norm(middle, vec_ref[5:6, :], vec_ref[6:7, :]).astype(BF16)


def scalar_first(count):
    return [pl.BlockSpec(memory_space=pltpu.SMEM)] + [pl.BlockSpec(memory_space=pltpu.VMEM)] * count


def out_part(quarter, outs, weight, x_low, vec):
    shape = x_low.shape
    return pl.pallas_call(
        out_kernel,
        in_specs=scalar_first(7),
        out_shape=[jax.ShapeDtypeStruct(shape, kind) for kind in (BF16, F32, BF16)],
        compiler_params=pltpu.CompilerParams(vmem_limit_bytes=32 * 2**20),
        cost_estimate=pl.CostEstimate(
            flops=2 * math.prod(shape) * shape[1], bytes_accessed=14 * math.prod(shape), transcendentals=0
        ),
        name="out_part",
    )(quarter.reshape(1), *outs, weight, x_low, vec)


def norm_back(values, gain, grad):
    center = values - jnp.mean(values, -1, keepdims=True)
    inv = lax.rsqrt(jnp.mean(center * center, -1, keepdims=True) + EPS)
    unit_values = center * inv
    scaled = grad * gain
    back = inv * (
        scaled - jnp.mean(scaled, -1, keepdims=True)
        - unit_values * jnp.mean(scaled * unit_values, -1, keepdims=True)
    )
    return back, jnp.sum(grad * unit_values, 0, keepdims=True), jnp.sum(grad, 0, keepdims=True)


def middle_back_kernel(quarter_ref, grad_ref, mid_ref, cot_ref, vec_ref, weight_ref, dmid_ref, rows_ref, *part_refs):
    cot = cot_ref[...].astype(F32)
    back, gain, shift = norm_back(mid_ref[...], vec_ref[5:6, :], grad_ref[...])
    d_middle = cot + back
    dmid_ref[...] = d_middle
    d_attn = d_middle.astype(BF16)
    d_low = d_attn.astype(F32)
    rows_ref[...] = jnp.concatenate(
        [gain, shift, jnp.sum(d_low, 0, keepdims=True), jnp.sum(cot, 0, keepdims=True)], 0
    )
    d_attended = dot(d_attn, weight_ref[...], NT).astype(BF16)
    for refs, whole in ((part_refs[:QUARTERS], d_attended), (part_refs[QUARTERS:], d_attn)):
        wide = whole.shape[1] // QUARTERS
        parts = in_order([whole[:, p * wide:(p + 1) * wide] for p in range(QUARTERS)], quarter_ref[0])
        for ref, part in zip(refs, parts):
            ref[...] = part


def middle_back(quarter, grad, middle, cot, vec, weight):
    frames, width = middle.shape
    part = jax.ShapeDtypeStruct((frames, width // QUARTERS), BF16)
    results = pl.pallas_call(
        middle_back_kernel,
        in_specs=scalar_first(5),
        out_shape=[jax.ShapeDtypeStruct((frames, width), F32), jax.ShapeDtypeStruct((4, width), F32)]
        + [part] * (2 * QUARTERS),
        compiler_params=pltpu.CompilerParams(vmem_limit_bytes=32 * 2**20),
        cost_estimate=pl.CostEstimate(
            flops=2 * frames * width * width, bytes_accessed=18 * frames * width, transcendentals=0
        ),
        name="middle_back",
    )(quarter.reshape(1), grad, middle, cot, vec, weight)
    return results[0], results[1], results[2:2 + QUARTERS], results[2 + QUARTERS:]


def vector_kernel(quarter_ref, *refs, shards):
    ins, up_ins = refs[:QUARTERS], refs[QUARTERS:2 * QUARTERS]
    gain_ref, shift_ref, mid_ref, out_ref = refs[2 * QUARTERS:]
    width = out_ref.shape[0]
    wide, unit = width // QUARTERS, width // shards
    ins = in_order([ref[...] for ref in ins], quarter_ref[0])
    value_row, query_row = (
        jnp.concatenate([piece[:, i * wide:(i + 1) * wide] for piece in ins], 1) for i in range(1, 3)
    )
    ups = in_order([ref[...] for ref in up_ins], quarter_ref[0])
    up_row = jnp.concatenate(
        [piece[:, shard * unit:(shard + 1) * unit] for shard in range(shards) for piece in ups], 1
    )
    rows = [gain_ref[...], shift_ref[...], query_row, value_row, mid_ref[2:3, :], mid_ref[0:2, :], mid_ref[3:4, :]]
    rows += [up_row[:, start:start + width] for start in range(0, up_row.shape[1], width)]
    rows = jnp.concatenate(rows, 0)
    rows = jnp.concatenate([rows, jnp.zeros((128 - rows.shape[0], width), F32)], 0)
    out_ref[...] = rows.T.astype(BF16)


def vector_block(quarter, sums_in, up_sums, gain, shift, mid_rows, shards):
    width = gain.shape[1]
    return pl.pallas_call(
        functools.partial(vector_kernel, shards=shards),
        in_specs=scalar_first(2 * QUARTERS + 3),
        out_shape=jax.ShapeDtypeStruct((width, 128), BF16),
        compiler_params=pltpu.CompilerParams(vmem_limit_bytes=32 * 2**20),
        cost_estimate=pl.CostEstimate(flops=128 * width, bytes_accessed=512 * width, transcendentals=0),
        name="vector_block",
    )(quarter.reshape(1), *sums_in, *up_sums, gain, shift, mid_rows)


def column_tile(columns):
    return 256 if columns % 256 == 0 else columns


def mlp_kernel(in_ref, up_ref, bias_ref, down_ref, before_ref, act_ref, slope_ref, sum_ref):
    up = dot(in_ref[...], up_ref[...]) + bias_ref[...]
    cdf = 0.5 + 0.5 * lax.erf(up * (0.5 ** 0.5))
    pdf = jnp.exp(-0.5 * up * up) * 0.3989422804014327
    act = (up * cdf).astype(BF16)
    act_ref[...] = act
    slope_ref[...] = (cdf + up * pdf).astype(BF16)
    part = dot(act, down_ref[...])

    @pl.when(pl.program_id(0) == 0)
    def _():
        sum_ref[...] = before_ref[...] + part

    @pl.when(pl.program_id(0) > 0)
    def _():
        sum_ref[...] += part


def mlp_part(values, up, bias, down, before):
    rows, depth = values.shape
    columns = up.shape[1]
    tile = column_tile(columns)
    whole = pl.BlockSpec((rows, depth), lambda i: (0, 0))
    hidden = pl.BlockSpec((rows, tile), lambda i: (0, i))
    return pl.pallas_call(
        mlp_kernel,
        grid=(columns // tile,),
        in_specs=[
            whole,
            pl.BlockSpec((depth, tile), lambda i: (0, i)),
            pl.BlockSpec((1, tile), lambda i: (0, i)),
            pl.BlockSpec((tile, depth), lambda i: (i, 0)),
            whole,
        ],
        out_specs=[hidden, hidden, whole],
        out_shape=[
            jax.ShapeDtypeStruct((rows, columns), BF16),
            jax.ShapeDtypeStruct((rows, columns), BF16),
            jax.ShapeDtypeStruct((rows, depth), F32),
        ],
        compiler_params=pltpu.CompilerParams(vmem_limit_bytes=32 * 2**20),
        cost_estimate=pl.CostEstimate(
            flops=4 * rows * depth * columns, bytes_accessed=4 * (3 * rows * depth + depth * columns + rows * columns),
            transcendentals=2 * rows * columns,
        ),
        name="mlp_part",
    )(values, up, bias, down, before)


def mlp_back_kernel(grad_ref, in_ref, act_ref, slope_ref, up_ref, down_ref, before_ref, gd_ref, gu_ref, row_ref, sum_ref):
    grad = grad_ref[...]
    d_up = (dot(grad, down_ref[...], NT) * slope_ref[...].astype(F32)).astype(BF16)
    gd_ref[...] = dot(act_ref[...], grad, TN).astype(BF16)
    gu_ref[...] = dot(in_ref[...], d_up, TN).astype(BF16)
    row_ref[...] = jnp.sum(d_up.astype(F32), 0, keepdims=True)
    part = dot(d_up, up_ref[...], NT)

    @pl.when(pl.program_id(0) == 0)
    def _():
        sum_ref[...] = before_ref[...] + part

    @pl.when(pl.program_id(0) > 0)
    def _():
        sum_ref[...] += part


def mlp_back_part(grad, values, act, slope, up, down, before):
    rows, depth = values.shape
    columns = up.shape[1]
    tile = column_tile(columns)
    whole = pl.BlockSpec((rows, depth), lambda i: (0, 0))
    hidden = pl.BlockSpec((rows, tile), lambda i: (0, i))
    up_tile = pl.BlockSpec((depth, tile), lambda i: (0, i))
    down_tile = pl.BlockSpec((tile, depth), lambda i: (i, 0))
    return pl.pallas_call(
        mlp_back_kernel,
        grid=(columns // tile,),
        in_specs=[whole, whole, hidden, hidden, up_tile, down_tile, whole],
        out_specs=[down_tile, up_tile, pl.BlockSpec((1, tile), lambda i: (0, i)), whole],
        out_shape=[
            jax.ShapeDtypeStruct((columns, depth), BF16),
            jax.ShapeDtypeStruct((depth, columns), BF16),
            jax.ShapeDtypeStruct((1, columns), F32),
            jax.ShapeDtypeStruct((rows, depth), F32),
        ],
        compiler_params=pltpu.CompilerParams(vmem_limit_bytes=40 * 2**20),
        cost_estimate=pl.CostEstimate(
            flops=8 * rows * depth * columns, bytes_accessed=4 * (3 * rows * depth + 2 * depth * columns + rows * columns),
            transcendentals=0,
        ),
        name="mlp_back_part",
    )(grad, values, act, slope, up, down, before)


def proj_back_kernel(in_ref, own_ref, other_ref, query_ref, out_ref, grad_ref, weight_ref, before_ref, g_ref, row_ref, sum_ref):
    frames, wide = query_ref.shape
    both = (own_ref[...].astype(F32) + other_ref[...].astype(F32)).astype(BF16)
    query = query_ref[...]
    values = in_ref[...]
    g_ref[...] = jnp.concatenate(
        [dot(values, both, TN), dot(values[:frames], query, TN), dot(out_ref[...], grad_ref[...], TN)], 1
    ).astype(BF16)
    row_ref[...] = jnp.concatenate(
        [jnp.sum(both.astype(F32), 0, keepdims=True), jnp.sum(query.astype(F32), 0, keepdims=True)], 1
    )
    total = before_ref[...] + dot(both, weight_ref[:, :2 * wide], NT)
    own = total[:frames] + dot(query, weight_ref[:, 2 * wide:3 * wide], NT)
    sum_ref[0:frames, :] = own
    sum_ref[frames:, :] = total[frames:]


def proj_back(values, own, other, query, out, grad, weight, before):
    rows, depth = values.shape
    wide = query.shape[1]
    return pl.pallas_call(
        proj_back_kernel,
        out_shape=[
            jax.ShapeDtypeStruct(weight.shape, BF16),
            jax.ShapeDtypeStruct((1, 3 * wide), F32),
            jax.ShapeDtypeStruct((rows, depth), F32),
        ],
        compiler_params=pltpu.CompilerParams(vmem_limit_bytes=40 * 2**20),
        cost_estimate=pl.CostEstimate(
            flops=8 * rows * depth * 2 * wide, bytes_accessed=12 * rows * depth + 4 * depth * weight.shape[1],
            transcendentals=0,
        ),
        name="proj_back",
    )(values, own, other, query, out, grad, weight, before)


def place_proj_kernel(quarter_ref, a_ref, b_ref, c_ref, d_ref, qkv_ref, out_ref, vec_ref):
    pieces = [ref[...].astype(F32) for ref in (a_ref, b_ref, c_ref, d_ref)]
    width = out_ref.shape[1]
    wide = width // QUARTERS
    total = pieces[0][:, width:] + pieces[1][:, width:] + pieces[2][:, width:] + pieces[3][:, width:]
    vec_ref[...] = total.T
    pieces = in_order([piece[:, :width] for piece in pieces], quarter_ref[0])
    for column, part in ((0, 2), (1, 0), (2, 1)):
        qkv_ref[:, column * width:(column + 1) * width] = jnp.concatenate(
            [piece[:, part * wide:(part + 1) * wide] for piece in pieces], 1
        )
    out_ref[...] = jnp.concatenate([piece[:, 3 * wide:] for piece in pieces], 1)


def place_mlp_kernel(quarter_ref, a_ref, b_ref, c_ref, d_ref, down_ref, up_ref, *, shards):
    pieces = in_order([ref[...].astype(F32) for ref in (a_ref, b_ref, c_ref, d_ref)], quarter_ref[0])
    rows, width = pieces[0].shape[0], pieces[0].shape[1] // 2
    unit = width // shards
    for place in range(QUARTERS):
        down_ref[place * rows:(place + 1) * rows, :] = pieces[place][:, :width]
    for shard in range(shards):
        start = width + shard * unit
        up_ref[:, shard * QUARTERS * unit:(shard + 1) * QUARTERS * unit] = jnp.concatenate(
            [piece[:, start:start + unit] for piece in pieces], 1
        )


def placed_parts(kernel, quarter, pieces, shapes):
    size = sum(math.prod(shape) for shape in shapes)
    return pl.pallas_call(
        kernel,
        in_specs=scalar_first(QUARTERS),
        out_shape=[jax.ShapeDtypeStruct(shape, F32) for shape in shapes],
        compiler_params=pltpu.CompilerParams(vmem_limit_bytes=32 * 2**20),
        cost_estimate=pl.CostEstimate(flops=size, bytes_accessed=6 * size, transcendentals=0),
        name="placed_parts",
    )(quarter.reshape(1), *pieces)


def across(block, bit):
    count = lax.axis_size("replica")
    return lax.ppermute(block, "replica", [(i, i ^ bit) for i in range(count)])


def swap_sections(block):
    return lax.ppermute(block, "section", [(0, 1), (1, 0)])


def reversed_bits(index, count):
    result, bit = index * 0, 1
    while bit < count:
        result = result * 2 + index // bit % 2
        bit *= 2
    return result


def transposed(block, source, target):
    shards, replicas = lax.axis_size("shard"), lax.axis_size("replica")

    def flat(section, shard, replica):
        return (section * shards + shard) * replicas + replica

    route = []
    for shard in range(shards):
        for replica in range(replicas):
            group, place = divmod(replica, shards)
            here = (shard, replica)
            there = (reversed_bits(place, shards), group * shards + reversed_bits(shard, shards))
            if source is None:
                route += [(flat(s, *here), flat(s, *there)) for s in range(2)]
            else:
                route.append((flat(source, *here), flat(target, *there)))
    return lax.ppermute(block, AXES, route)


def in_order(pieces, quarter):
    odd, high = (quarter & 1) == 1, (quarter & 2) == 2
    a, b, c, d = pieces
    a, b, c, d = jnp.where(odd, b, a), jnp.where(odd, a, b), jnp.where(odd, d, c), jnp.where(odd, c, d)
    return jnp.where(high, c, a), jnp.where(high, d, b), jnp.where(high, a, c), jnp.where(high, b, d)


def after(value, *others):
    return lax.optimization_barrier((value, others))[0]


def spread(piece, far):
    return piece, across(piece, 1), far, across(far, 1)


def low_sum(*parts):
    total = parts[0].astype(F32)
    for part in parts[1:]:
        total = total + part.astype(F32)
    return total.astype(BF16)


def body(edges, attn_in, attn_out, mlp_up, mlp_down, vectors, key_mask):
    section = lax.axis_index("section")
    first = section == 0
    replica = lax.axis_index("replica")
    shards, replicas = lax.axis_size("shard"), lax.axis_size("replica")
    quarter = replica % QUARTERS
    edges_here = edges[0]
    clips, frames, width = edges_here.shape
    hidden = mlp_up.shape[2]
    dim = width // H
    heads = H // QUARTERS
    wide = heads * dim
    unit = hidden // (shards * QUARTERS)
    rows = attn_in.shape[1]
    assert clips == 2 and lax.axis_size("section") == 2 and replicas % shards == 0 and replicas % QUARTERS == 0

    def by_layer(own, other):
        return jnp.where(first, own, other), jnp.where(first, other, own)

    vec_by_layer = by_layer(vectors[0], swap_sections(vectors[0]))
    mask_row = transposed(
        lax.dynamic_index_in_dim(key_mask, section, 0, keepdims=False).astype(F32)[None], None, None
    )[0]
    inputs = jnp.where(first, transposed(edges_here[0], 0, 0), transposed(edges_here[1], 0, 1))

    def pick(block, axis):
        return lax.dynamic_index_in_dim(block, quarter, axis, keepdims=False)

    def gathered(block):
        return lax.all_gather(block, "shard", axis=0, tiled=True)

    query_in, key_in, value_in = (
        pick(attn_in[0][:, i * width:(i + 1) * width].reshape(rows, QUARTERS, wide), 1) for i in range(3)
    )
    own_proj = jnp.concatenate(
        [key_in, value_in, query_in, pick(attn_out[0].reshape(rows, QUARTERS, width // QUARTERS), 1)], 1
    )
    own_up = pick(mlp_up[0].reshape(rows, shards, QUARTERS, unit), 2).reshape(rows, shards * unit)
    own_down = pick(mlp_down[0].reshape(QUARTERS, unit, width), 0)
    proj_zero, proj_one = by_layer(own_proj, swap_sections(own_proj))
    proj_zero = gathered(proj_zero)
    own_up = after(own_up, inputs)
    own_down = after(own_down, own_up)
    proj_one = after(proj_one, own_down)
    own_up, own_down, proj_one = gathered(own_up), gathered(own_down), gathered(proj_one)

    def head_weights(block):
        pieces = spread(block, across(block, 2))
        return pieces, jnp.concatenate(in_order([piece[:, 3 * wide:] for piece in pieces], quarter), 1)

    def two_swapped(own, far):
        return own, far, [swap_sections(own), swap_sections(far)]

    def two_layers(own, far, others):
        near, away = by_layer(own, others[0]), by_layer(far, others[1])
        return (near[0], away[0]), (near[1], away[1])

    heads_by_layer = [head_weights(proj_zero), None]
    hidden_by_layer = [None, None]

    members = [0]
    bit = 2
    while bit < shards:
        members = members + [m ^ bit for m in members]
        bit *= 2
    members = members + [m ^ 1 for m in members]
    place = replica % shards
    bias_row = jnp.concatenate(
        [lax.dynamic_slice_in_dim(mask_row, reversed_bits(place ^ m, shards) * frames, frames, 0) for m in members]
    )
    bias_row = jnp.where(bias_row > 0, 0.0, MASKED).astype(BF16)
    lane = jnp.arange(dim)[None, :]
    key_bias = jnp.where(lane == 0, bias_row[:, None], jnp.zeros((), BF16))

    def chips_rows(block):
        bit = 2
        while bit < shards:
            block = jnp.concatenate([block, across(block, bit)], 0)
            bit *= 2
        return block

    def forward(x_low, layer):
        vec = vec_by_layer[layer]
        x_set = chips_rows(x_low)
        proj, w_out = heads_by_layer[layer]
        normed = layer_norm(x_set.astype(F32), vec[0], vec[1]).astype(BF16)
        zeros = jnp.zeros((QUARTERS, wide), F32)
        bias_in = jnp.stack([zeros, vec[3].reshape(QUARTERS, wide), vec[2].reshape(QUARTERS, wide)], 1)
        own_qkv, other_kv = {}, {}
        order = (0, 1, 2, 3)
        for p in order:
            bias = lax.dynamic_index_in_dim(bias_in, quarter ^ p, 0, keepdims=False).reshape(3 * wide)
            own_qkv[p] = (dot(normed, proj[p][:, :3 * wide]) + bias).astype(BF16)
            other_kv[p ^ 1] = across(own_qkv[p][:, :2 * wide], 1)
        outs, weights, inverses = {}, {}, {}
        late = {}
        if layer == 0:
            late["up_far"] = across(after(own_up, own_qkv[0]), 2)
        for step, p in enumerate(order):
            outs[p], weights[p], inverses[p] = attend(own_qkv[p], other_kv[p], key_bias, heads, frames)
            if layer == 0 and step == 0:
                late["up"] = two_swapped(after(own_up, outs[p]), after(late["up_far"], outs[p]))
                late["down_far"] = across(after(own_down, outs[p]), 2)
            elif layer == 0 and step == 2:
                late["down"] = two_swapped(own_down, after(late["down_far"], outs[p]))
            elif layer == 0 and step == 3:
                own, far, others = late["up"]
                late["up"] = two_layers(own, far, [after(other, outs[p]) for other in others])
                late["up_near"] = [across(piece, 1) for piece in late["up"][0]]
            elif layer == 1 and step == 1:
                cot = after(edges_here, outs[p])
                pending_one["cot"] = [transposed(cot[0], 1, 0), transposed(cot[1], 1, 1)]
        skip = after(x_low, proj_one) if layer == 0 else x_low
        attended, middle, normed_two = out_part(quarter, [outs[p] for p in range(QUARTERS)], w_out, skip, vec)
        if layer == 0:
            own, far, others = late["down"]
            late["down"] = two_layers(own, far, [after(other, middle) for other in others])
            late["down_near"] = [across(piece, 1) for piece in late["down"][0]]
            late["one_far"] = across(after(proj_one, middle), 2)
            hidden_by_layer[0] = [
                [pieces[0], near[0], pieces[1], near[1]]
                for pieces, near in ((late[name][0], late[name + "_near"]) for name in ("up", "down"))
            ]
        w_up, w_down = hidden_by_layer[layer]
        bias_up = vec[8:].reshape(shards, QUARTERS, unit)
        acts, slopes = {}, {}
        result = middle + vec[7]
        for step, p in enumerate((0, 2, 1, 3)):
            bias = lax.dynamic_index_in_dim(bias_up, quarter ^ p, 1, keepdims=False).reshape(1, shards * unit)
            acts[p], slopes[p], result = mlp_part(normed_two, w_up[p], bias, w_down[p], result)
            if layer == 0 and step == 1:
                pieces = spread(proj_one, after(late["one_far"], acts[p]))
                w_out_one = jnp.concatenate(in_order([piece[:, 3 * wide:] for piece in pieces], quarter), 1)
                heads_by_layer[1] = (pieces, w_out_one)
            elif layer == 0 and step == 2:
                ones = [[after(piece, acts[p]) for piece in late[name][1]] for name in ("up", "down")]
                hidden_by_layer[1] = [[a, across(a, 1), b, across(b, 1)] for a, b in ones]
        kept = (x_low, normed, own_qkv, other_kv, weights, inverses, attended, middle, normed_two, acts, slopes)
        return result.astype(BF16), kept

    pending_one = {}

    def scattered(block):
        bit = QUARTERS
        while bit < replicas:
            block = low_sum(block, across(block, bit))
            bit *= 2
        return lax.psum_scatter(block, "shard", scatter_dimension=0, tiled=True)

    def half_parts(block):
        cut = block.shape[1] // 2
        left, right = block[:, :cut], block[:, cut:]
        return jnp.where(first, left, right), jnp.where(first, right, left)

    def half_sum(block):
        kept_half, sent = half_parts(block)
        return low_sum(kept_half, swap_sections(sent))

    def backward(cot, layer, kept, above):
        (proj, w_out), (w_up, w_down), vec = heads_by_layer[layer], hidden_by_layer[layer], vec_by_layer[layer]
        x_low, normed, own_qkv, other_kv, weights, inverses, attended, middle, normed_two, acts, slopes = kept
        order = (3, 1, 2, 0)
        g_down, g_up, up_sums, near_down, near_up = {}, {}, {}, {}, {}
        d_normed_two = jnp.zeros((frames, width), F32)
        for step, p in enumerate(order):
            g_down[p], g_up[p], up_sums[p], d_normed_two = mlp_back_part(
                cot, normed_two, acts[p], slopes[p], w_up[p], w_down[p], d_normed_two
            )
            if p & 1:
                near_down[p ^ 1] = across(g_down[p], 1)
                near_up[p ^ 1] = across(g_up[p], 1)
            if above is not None and step == 1:
                halves = [after(half, g_up[p]) for half in above["halves"]]
                above["mlp"] = scattered(jnp.concatenate(halves, 1))
        d_middle, mid_rows, d_heads, d_attn_parts = middle_back(quarter, d_normed_two, middle, cot, vec, w_out)
        if above is not None:
            far = after(above["far_proj"], mid_rows)
            above["half"] = half_sum(above["finish"](far))

        def chip_halves(grads, near, token):
            return [half_parts(low_sum(grads[p], after(near[p], token))) for p in (0, 2)]

        down = chip_halves(g_down, near_down, mid_rows)
        up = None
        results = {}
        for step, p in enumerate(order):
            head = d_heads[p]
            if step == 1:
                head = after(head, *[sent for _, sent in down])
                down = [(kept_half, swap_sections(sent)) for kept_half, sent in down]
            elif step == 2:
                head = after(head, *[sent for _, sent in up])
                up = [(kept_half, swap_sections(sent)) for kept_half, sent in up]
                if above is not None:
                    half = after(above["half"], results[order[1]][0])
                    above["proj"] = scattered(jnp.concatenate([half, above["vec"]], 1))
            elif step == 3 and above is not None:
                head = after(head, above["mlp"])
            results[p] = attend_back(own_qkv[p], other_kv[p], weights[p], inverses[p], head, heads, frames)
            if step == 0:
                up = chip_halves(g_up, near_up, results[p][0])
            elif step == 2:
                down = [low_sum(a, after(b, results[p][0])) for a, b in down]
                down[1] = across(down[1], 2)
            elif step == 3:
                up = [low_sum(a, after(b, results[p][0])) for a, b in up]
                up[1] = across(up[1], 2)
        from_other = {p: across(results[p ^ 1][2], 1) for p in range(QUARTERS)}
        g_proj, sums_in, near_proj = {}, {}, {}
        d_normed = jnp.zeros(normed.shape, F32)
        for p in order:
            g_proj[p], sums_in[p], d_normed = proj_back(
                normed, results[p][1], from_other[p], results[p][0], attended, d_attn_parts[p], proj[p], d_normed
            )
            if p & 1:
                near_proj[p ^ 1] = across(g_proj[p], 1)
        block = d_normed
        bit = shards // 2
        while bit >= 2:
            cut = block.shape[0] // 2
            block = block[:cut] + across(block[cut:].astype(BF16), bit).astype(F32)
            bit //= 2
        half_down = low_sum(down[0], after(down[1], d_normed))
        half_up = low_sum(up[0], after(up[1], d_normed))
        if layer == 1:
            far_proj = low_sum(g_proj[2], after(near_proj[2], block))
        else:
            far_proj = low_sum(g_proj[2], after(near_proj[2], d_normed))
        back, g_gain_one, g_shift_one = norm_back(x_low.astype(F32), vec[0], block)
        g_low = (d_middle + back).astype(BF16)
        g_low = after(g_low, far_proj)
        far_proj = across(far_proj, 2)
        vec_block = vector_block(
            quarter, [sums_in[p] for p in range(QUARTERS)], [up_sums[p] for p in range(QUARTERS)],
            g_gain_one, g_shift_one, mid_rows, shards,
        )
        if above is not None:
            g_low = after(g_low, above["proj"])

        def finish_proj(other):
            return low_sum(g_proj[0], near_proj[0], other)

        return g_low, {"halves": [half_down, half_up], "far_proj": far_proj, "finish": finish_proj, "vec": vec_block}

    x_one, kept_zero = forward(inputs, 0)
    y_one, kept_one = forward(x_one, 1)
    cot = [after(part, y_one) for part in pending_one["cot"]]
    g_one, one = backward(jnp.where(first, cot[0], cot[1]), 1, kept_one, None)
    g_zero, zero = backward(g_one, 0, kept_zero, one)
    y_one = after(y_one, g_one)
    out_slots = [transposed(y_one, 0, 1), transposed(y_one, 1, 1)]
    back_slots = [transposed(g_zero, 0, 0), transposed(g_zero, 1, 0)]
    edges_out = jnp.stack([jnp.where(first, b, o) for b, o in zip(back_slots, out_slots)])
    mlp_one, proj_one = one["mlp"], one["proj"]
    mlp_zero = scattered(jnp.concatenate([after(half, g_zero) for half in zero["halves"]], 1))
    far = after(zero["far_proj"], g_zero)
    proj_zero = scattered(jnp.concatenate([half_sum(zero["finish"](far)), zero["vec"]], 1))

    def exchanged(zero, one):
        return jnp.where(first, zero, one), swap_sections(jnp.where(first, one, zero))

    def joined(own, other):
        cut = width // 2
        parts = []
        for start in range(0, own.shape[1], cut):
            a, b = own[:, start:start + cut], other[:, start:start + cut]
            parts += [jnp.where(first, a, b), jnp.where(first, b, a)]
        return parts

    part = jnp.concatenate(joined(*exchanged(mlp_zero, mlp_one)), 1)
    f_down, f_up = placed_parts(
        functools.partial(place_mlp_kernel, shards=shards), quarter, spread(part, across(part, 2)),
        [mlp_down.shape[1:], mlp_up.shape[1:]],
    )
    own, other = exchanged(proj_zero, proj_one)
    cut = width // 2
    part = jnp.concatenate(
        joined(own[:, :cut], other[:, :cut]) + [low_sum(own[:, cut:], other[:, cut:])], 1
    )
    f_in, f_out, f_vec = placed_parts(
        place_proj_kernel, quarter, spread(part, across(part, 2)),
        [attn_in.shape[1:], attn_out.shape[1:], (128, rows)],
    )
    f_vec = f_vec[:vectors.shape[1]]
    return edges_out[None], f_in[None], f_out[None], f_up[None], f_down[None], f_vec[None]


def solution(mesh):
    placed = (
        P("section", "replica", "shard", None),
        P("section", "shard", None),
        P("section", "shard", None),
        P("section", "shard", None),
        P("section", "shard", None),
        P("section", None, None),
        P("replica", None),
    )
    return jax.shard_map(
        body,
        mesh=mesh,
        in_specs=placed,
        out_specs=(
            P("section", "replica", "shard", None),
            P("section", "shard", None),
            P("section", "shard", None),
            P("section", "shard", None),
            P("section", "shard", None),
            P("section", None, "shard"),
        ),
        check_vma=False,
    )
```

```python
import functools
import math

import jax
import jax.numpy as jnp
from jax import lax
from jax.experimental import pallas as pl
from jax.experimental.pallas import tpu as pltpu
from jax.sharding import PartitionSpec as P

H = 12
EPS = 1e-05
MASKED = -1e30
QUARTERS = 4
ATTEND_VMEM = 58 * 2**20
BF16 = jnp.bfloat16
F32 = jnp.float32
AXES = ("section", "shard", "replica")
NN = (((1,), (0,)), ((), ()))
NT = (((1,), (1,)), ((), ()))
TN = (((0,), (0,)), ((), ()))


def dot(a, b, dims=NN):
    return lax.dot_general(a, b, dims, preferred_element_type=F32)


def layer_norm(values, gain, shift):
    center = values - jnp.mean(values, -1, keepdims=True)
    spread = jnp.mean(center * center, -1, keepdims=True)
    return center * lax.rsqrt(spread + EPS) * gain + shift


def key_chunks(sources, size):
    chunks, base = [], 0
    for source in range(len(sources)):
        rows = sources[source].shape[0]
        for start in range(0, rows, size):
            chunks.append((source, start, base + start))
        base += rows
    return chunks


def attend_kernel(own_ref, other_ref, bias_ref, out_ref, exp_ref, inv_ref, score_ref, *, heads, frames, chunk):
    dim = own_ref.shape[1] // (3 * heads)
    wide = heads * dim
    sources = (own_ref, other_ref)
    chunks = key_chunks(sources, chunk)

    def one_head(head):
        at = head * dim
        query = own_ref[0:frames, 2 * wide + at:2 * wide + at + dim] * (dim ** -0.5)
        lane = lax.broadcasted_iota(jnp.int32, (frames, dim), 1)
        query = jnp.concatenate([query.astype(BF16), (lane == 0).astype(BF16)], 1)
        top = None
        for source, start, row in chunks:
            key = sources[source][start:start + chunk, at:at + dim]
            key = jnp.concatenate([key, bias_ref[row:row + chunk, :]], 1)
            score = dot(key, query, NT)
            score_ref[row:row + chunk, :] = score
            part = jnp.max(score, 0, keepdims=True)
            top = part if top is None else jnp.maximum(top, part)
        total = None
        for source, start, row in chunks:
            weight = jnp.exp(score_ref[row:row + chunk, :] - top).astype(BF16)
            exp_ref[0, row:row + chunk, :] = weight
            value = sources[source][start:start + chunk, wide + at:wide + at + dim]
            value = jnp.concatenate([value, jnp.ones_like(value)], 1)
            part = dot(value, weight, TN)
            total = part if total is None else total + part
        inverse = 1.0 / total[dim:dim + 1, :]
        inv_ref[head:head + 1, :] = inverse
        out_ref[:, at:at + dim] = (total[0:dim, :] * inverse).T.astype(BF16)

    for head in range(heads):
        pl.when(pl.program_id(0) == head)(functools.partial(one_head, head))


def whole_block(shape):
    return pl.BlockSpec(shape, lambda i: (0,) * len(shape))


def chunk_size(own, frames):
    chunk = min(256, frames)
    return frames if own.shape[0] % chunk else chunk


def attend(own, other, bias, heads, frames):
    keys = own.shape[0] + other.shape[0]
    wide = own.shape[1] // 3
    return pl.pallas_call(
        functools.partial(attend_kernel, heads=heads, frames=frames, chunk=chunk_size(own, frames)),
        grid=(heads,),
        in_specs=[whole_block(own.shape), whole_block(other.shape), whole_block(bias.shape)],
        out_specs=[
            whole_block((frames, wide)),
            pl.BlockSpec((1, keys, frames), lambda i: (i, 0, 0)),
            whole_block((heads, frames)),
        ],
        out_shape=(
            jax.ShapeDtypeStruct((frames, wide), BF16),
            jax.ShapeDtypeStruct((heads, keys, frames), BF16),
            jax.ShapeDtypeStruct((heads, frames), F32),
        ),
        scratch_shapes=[pltpu.VMEM((keys, frames), F32)],
        compiler_params=pltpu.CompilerParams(vmem_limit_bytes=ATTEND_VMEM),
        cost_estimate=pl.CostEstimate(
            flops=16 * keys * frames * wide, bytes_accessed=2 * heads * keys * frames, transcendentals=heads * keys * frames
        ),
        name="attend",
    )(own, other, bias)


def attend_back_kernel(own_ref, other_ref, exp_ref, inv_ref, dout_ref, dq_ref, down_ref, dother_ref, prod_ref, *, heads, frames, chunk):
    dim = own_ref.shape[1] // (3 * heads)
    wide = heads * dim
    scale = dim ** -0.5
    sources = (own_ref, other_ref)
    targets = (down_ref, dother_ref)
    chunks = key_chunks(sources, chunk)

    def one_head(head):
        at = head * dim
        query = (own_ref[0:frames, 2 * wide + at:2 * wide + at + dim] * scale).astype(BF16)
        inverse = inv_ref[head:head + 1, :]
        dout_t = dout_ref[:, at:at + dim].astype(F32).T * inverse
        dout = dout_t.T.astype(BF16)
        dout_t = dout_t.astype(BF16)
        delta = None
        for source, start, row in chunks:
            value = sources[source][start:start + chunk, wide + at:wide + at + dim]
            weight = exp_ref[0, row:row + chunk, :]
            prod = dot(value, dout_t) * weight.astype(F32)
            prod_ref[row:row + chunk, :] = prod
            part = jnp.sum(prod, 0, keepdims=True)
            delta = part if delta is None else delta + part
            targets[source][start:start + chunk, wide + at:wide + at + dim] = dot(weight, dout).astype(BF16)
        delta = delta * inverse
        dq_t = None
        for source, start, row in chunks:
            key = sources[source][start:start + chunk, at:at + dim]
            weight = exp_ref[0, row:row + chunk, :].astype(F32)
            ds = (prod_ref[row:row + chunk, :] - weight * delta).astype(BF16)
            targets[source][start:start + chunk, at:at + dim] = dot(ds, query).astype(BF16)
            part = dot(key, ds, TN)
            dq_t = part if dq_t is None else dq_t + part
        dq_ref[:, at:at + dim] = (dq_t.T * scale).astype(BF16)

    for head in range(heads):
        pl.when(pl.program_id(0) == head)(functools.partial(one_head, head))


def attend_back(own, other, weights, inverse, dout, heads, frames):
    keys = own.shape[0] + other.shape[0]
    wide = own.shape[1] // 3
    results = ((frames, wide), (own.shape[0], 2 * wide), (other.shape[0], 2 * wide))
    return pl.pallas_call(
        functools.partial(attend_back_kernel, heads=heads, frames=frames, chunk=chunk_size(own, frames)),
        grid=(heads,),
        in_specs=[
            whole_block(own.shape), whole_block(other.shape),
            pl.BlockSpec((1, keys, frames), lambda i: (i, 0, 0)),
            whole_block(inverse.shape), whole_block(dout.shape),
        ],
        out_specs=[whole_block(shape) for shape in results],
        out_shape=[jax.ShapeDtypeStruct(shape, BF16) for shape in results],
        scratch_shapes=[pltpu.VMEM((keys, frames), F32)],
        compiler_params=pltpu.CompilerParams(vmem_limit_bytes=ATTEND_VMEM),
        cost_estimate=pl.CostEstimate(
            flops=32 * keys * frames * wide, bytes_accessed=2 * heads * keys * frames, transcendentals=0
        ),
        name="attend_back",
    )(own, other, weights, inverse, dout)


def out_kernel(quarter_ref, a_ref, b_ref, c_ref, d_ref, weight_ref, x_ref, vec_ref, att_ref, mid_ref, norm_ref):
    parts = [ref[...] for ref in (a_ref, b_ref, c_ref, d_ref)]
    attended = jnp.concatenate(in_order(parts, quarter_ref[0]), 1)
    att_ref[...] = attended
    middle = x_ref[...].astype(F32) + dot(attended, weight_ref[...]) + vec_ref[4:5, :]
    mid_ref[...] = middle
    norm_ref[...] = layer_norm(middle, vec_ref[5:6, :], vec_ref[6:7, :]).astype(BF16)


def scalar_first(count):
    return [pl.BlockSpec(memory_space=pltpu.SMEM)] + [pl.BlockSpec(memory_space=pltpu.VMEM)] * count


def out_part(quarter, outs, weight, x_low, vec):
    shape = x_low.shape
    return pl.pallas_call(
        out_kernel,
        in_specs=scalar_first(7),
        out_shape=[jax.ShapeDtypeStruct(shape, kind) for kind in (BF16, F32, BF16)],
        compiler_params=pltpu.CompilerParams(vmem_limit_bytes=32 * 2**20),
        cost_estimate=pl.CostEstimate(
            flops=2 * math.prod(shape) * shape[1], bytes_accessed=14 * math.prod(shape), transcendentals=0
        ),
        name="out_part",
    )(quarter.reshape(1), *outs, weight, x_low, vec)


def norm_back(values, gain, grad):
    center = values - jnp.mean(values, -1, keepdims=True)
    inv = lax.rsqrt(jnp.mean(center * center, -1, keepdims=True) + EPS)
    unit_values = center * inv
    scaled = grad * gain
    back = inv * (
        scaled - jnp.mean(scaled, -1, keepdims=True)
        - unit_values * jnp.mean(scaled * unit_values, -1, keepdims=True)
    )
    return back, jnp.sum(grad * unit_values, 0, keepdims=True), jnp.sum(grad, 0, keepdims=True)


def middle_back_kernel(quarter_ref, grad_ref, mid_ref, cot_ref, vec_ref, weight_ref, dmid_ref, rows_ref, *part_refs):
    cot = cot_ref[...].astype(F32)
    back, gain, shift = norm_back(mid_ref[...], vec_ref[5:6, :], grad_ref[...])
    d_middle = cot + back
    dmid_ref[...] = d_middle
    d_attn = d_middle.astype(BF16)
    d_low = d_attn.astype(F32)
    rows_ref[...] = jnp.concatenate(
        [gain, shift, jnp.sum(d_low, 0, keepdims=True), jnp.sum(cot, 0, keepdims=True)], 0
    )
    d_attended = dot(d_attn, weight_ref[...], NT).astype(BF16)
    for refs, whole in ((part_refs[:QUARTERS], d_attended), (part_refs[QUARTERS:], d_attn)):
        wide = whole.shape[1] // QUARTERS
        parts = in_order([whole[:, p * wide:(p + 1) * wide] for p in range(QUARTERS)], quarter_ref[0])
        for ref, part in zip(refs, parts):
            ref[...] = part


def middle_back(quarter, grad, middle, cot, vec, weight):
    frames, width = middle.shape
    part = jax.ShapeDtypeStruct((frames, width // QUARTERS), BF16)
    results = pl.pallas_call(
        middle_back_kernel,
        in_specs=scalar_first(5),
        out_shape=[jax.ShapeDtypeStruct((frames, width), F32), jax.ShapeDtypeStruct((4, width), F32)]
        + [part] * (2 * QUARTERS),
        compiler_params=pltpu.CompilerParams(vmem_limit_bytes=32 * 2**20),
        cost_estimate=pl.CostEstimate(
            flops=2 * frames * width * width, bytes_accessed=18 * frames * width, transcendentals=0
        ),
        name="middle_back",
    )(quarter.reshape(1), grad, middle, cot, vec, weight)
    return results[0], results[1], results[2:2 + QUARTERS], results[2 + QUARTERS:]


def vector_kernel(quarter_ref, *refs, shards):
    ins, up_ins = refs[:QUARTERS], refs[QUARTERS:2 * QUARTERS]
    gain_ref, shift_ref, mid_ref, out_ref = refs[2 * QUARTERS:]
    width = out_ref.shape[0]
    wide, unit = width // QUARTERS, width // shards
    ins = in_order([ref[...] for ref in ins], quarter_ref[0])
    value_row, query_row = (
        jnp.concatenate([piece[:, i * wide:(i + 1) * wide] for piece in ins], 1) for i in range(1, 3)
    )
    ups = in_order([ref[...] for ref in up_ins], quarter_ref[0])
    up_row = jnp.concatenate(
        [piece[:, shard * unit:(shard + 1) * unit] for shard in range(shards) for piece in ups], 1
    )
    rows = [gain_ref[...], shift_ref[...], query_row, value_row, mid_ref[2:3, :], mid_ref[0:2, :], mid_ref[3:4, :]]
    rows += [up_row[:, start:start + width] for start in range(0, up_row.shape[1], width)]
    rows = jnp.concatenate(rows, 0)
    rows = jnp.concatenate([rows, jnp.zeros((128 - rows.shape[0], width), F32)], 0)
    out_ref[...] = rows.T.astype(BF16)


def vector_block(quarter, sums_in, up_sums, gain, shift, mid_rows, shards):
    width = gain.shape[1]
    return pl.pallas_call(
        functools.partial(vector_kernel, shards=shards),
        in_specs=scalar_first(2 * QUARTERS + 3),
        out_shape=jax.ShapeDtypeStruct((width, 128), BF16),
        compiler_params=pltpu.CompilerParams(vmem_limit_bytes=32 * 2**20),
        cost_estimate=pl.CostEstimate(flops=128 * width, bytes_accessed=512 * width, transcendentals=0),
        name="vector_block",
    )(quarter.reshape(1), *sums_in, *up_sums, gain, shift, mid_rows)


def column_tile(columns):
    return 256 if columns % 256 == 0 else columns


def mlp_kernel(in_ref, up_ref, bias_ref, down_ref, before_ref, act_ref, slope_ref, sum_ref):
    up = dot(in_ref[...], up_ref[...]) + bias_ref[...]
    cdf = 0.5 + 0.5 * lax.erf(up * (0.5 ** 0.5))
    pdf = jnp.exp(-0.5 * up * up) * 0.3989422804014327
    act = (up * cdf).astype(BF16)
    act_ref[...] = act
    slope_ref[...] = (cdf + up * pdf).astype(BF16)
    part = dot(act, down_ref[...])

    @pl.when(pl.program_id(0) == 0)
    def _():
        sum_ref[...] = before_ref[...] + part

    @pl.when(pl.program_id(0) > 0)
    def _():
        sum_ref[...] += part


def mlp_part(values, up, bias, down, before):
    rows, depth = values.shape
    columns = up.shape[1]
    tile = column_tile(columns)
    whole = pl.BlockSpec((rows, depth), lambda i: (0, 0))
    hidden = pl.BlockSpec((rows, tile), lambda i: (0, i))
    return pl.pallas_call(
        mlp_kernel,
        grid=(columns // tile,),
        in_specs=[
            whole,
            pl.BlockSpec((depth, tile), lambda i: (0, i)),
            pl.BlockSpec((1, tile), lambda i: (0, i)),
            pl.BlockSpec((tile, depth), lambda i: (i, 0)),
            whole,
        ],
        out_specs=[hidden, hidden, whole],
        out_shape=[
            jax.ShapeDtypeStruct((rows, columns), BF16),
            jax.ShapeDtypeStruct((rows, columns), BF16),
            jax.ShapeDtypeStruct((rows, depth), F32),
        ],
        compiler_params=pltpu.CompilerParams(vmem_limit_bytes=32 * 2**20),
        cost_estimate=pl.CostEstimate(
            flops=4 * rows * depth * columns, bytes_accessed=4 * (3 * rows * depth + depth * columns + rows * columns),
            transcendentals=2 * rows * columns,
        ),
        name="mlp_part",
    )(values, up, bias, down, before)


def mlp_back_kernel(grad_ref, in_ref, act_ref, slope_ref, up_ref, down_ref, before_ref, gd_ref, gu_ref, row_ref, sum_ref):
    grad = grad_ref[...]
    d_up = (dot(grad, down_ref[...], NT) * slope_ref[...].astype(F32)).astype(BF16)
    gd_ref[...] = dot(act_ref[...], grad, TN).astype(BF16)
    gu_ref[...] = dot(in_ref[...], d_up, TN).astype(BF16)
    row_ref[...] = jnp.sum(d_up.astype(F32), 0, keepdims=True)
    part = dot(d_up, up_ref[...], NT)

    @pl.when(pl.program_id(0) == 0)
    def _():
        sum_ref[...] = before_ref[...] + part

    @pl.when(pl.program_id(0) > 0)
    def _():
        sum_ref[...] += part


def mlp_back_part(grad, values, act, slope, up, down, before):
    rows, depth = values.shape
    columns = up.shape[1]
    tile = column_tile(columns)
    whole = pl.BlockSpec((rows, depth), lambda i: (0, 0))
    hidden = pl.BlockSpec((rows, tile), lambda i: (0, i))
    up_tile = pl.BlockSpec((depth, tile), lambda i: (0, i))
    down_tile = pl.BlockSpec((tile, depth), lambda i: (i, 0))
    return pl.pallas_call(
        mlp_back_kernel,
        grid=(columns // tile,),
        in_specs=[whole, whole, hidden, hidden, up_tile, down_tile, whole],
        out_specs=[down_tile, up_tile, pl.BlockSpec((1, tile), lambda i: (0, i)), whole],
        out_shape=[
            jax.ShapeDtypeStruct((columns, depth), BF16),
            jax.ShapeDtypeStruct((depth, columns), BF16),
            jax.ShapeDtypeStruct((1, columns), F32),
            jax.ShapeDtypeStruct((rows, depth), F32),
        ],
        compiler_params=pltpu.CompilerParams(vmem_limit_bytes=40 * 2**20),
        cost_estimate=pl.CostEstimate(
            flops=8 * rows * depth * columns, bytes_accessed=4 * (3 * rows * depth + 2 * depth * columns + rows * columns),
            transcendentals=0,
        ),
        name="mlp_back_part",
    )(grad, values, act, slope, up, down, before)


def proj_back_kernel(in_ref, own_ref, other_ref, query_ref, out_ref, grad_ref, weight_ref, before_ref, g_ref, row_ref, sum_ref):
    frames, wide = query_ref.shape
    both = (own_ref[...].astype(F32) + other_ref[...].astype(F32)).astype(BF16)
    query = query_ref[...]
    values = in_ref[...]
    g_ref[...] = jnp.concatenate(
        [dot(values, both, TN), dot(values[:frames], query, TN), dot(out_ref[...], grad_ref[...], TN)], 1
    ).astype(BF16)
    row_ref[...] = jnp.concatenate(
        [jnp.sum(both.astype(F32), 0, keepdims=True), jnp.sum(query.astype(F32), 0, keepdims=True)], 1
    )
    total = before_ref[...] + dot(both, weight_ref[:, :2 * wide], NT)
    own = total[:frames] + dot(query, weight_ref[:, 2 * wide:3 * wide], NT)
    sum_ref[0:frames, :] = own
    sum_ref[frames:, :] = total[frames:]


def proj_back(values, own, other, query, out, grad, weight, before):
    rows, depth = values.shape
    wide = query.shape[1]
    return pl.pallas_call(
        proj_back_kernel,
        out_shape=[
            jax.ShapeDtypeStruct(weight.shape, BF16),
            jax.ShapeDtypeStruct((1, 3 * wide), F32),
            jax.ShapeDtypeStruct((rows, depth), F32),
        ],
        compiler_params=pltpu.CompilerParams(vmem_limit_bytes=40 * 2**20),
        cost_estimate=pl.CostEstimate(
            flops=8 * rows * depth * 2 * wide, bytes_accessed=12 * rows * depth + 4 * depth * weight.shape[1],
            transcendentals=0,
        ),
        name="proj_back",
    )(values, own, other, query, out, grad, weight, before)


def place_proj_kernel(quarter_ref, a_ref, b_ref, c_ref, d_ref, qkv_ref, out_ref, vec_ref):
    pieces = [ref[...].astype(F32) for ref in (a_ref, b_ref, c_ref, d_ref)]
    width = out_ref.shape[1]
    wide = width // QUARTERS
    total = pieces[0][:, width:] + pieces[1][:, width:] + pieces[2][:, width:] + pieces[3][:, width:]
    vec_ref[...] = total.T
    pieces = in_order([piece[:, :width] for piece in pieces], quarter_ref[0])
    for column, part in ((0, 2), (1, 0), (2, 1)):
        qkv_ref[:, column * width:(column + 1) * width] = jnp.concatenate(
            [piece[:, part * wide:(part + 1) * wide] for piece in pieces], 1
        )
    out_ref[...] = jnp.concatenate([piece[:, 3 * wide:] for piece in pieces], 1)


def place_mlp_kernel(quarter_ref, a_ref, b_ref, c_ref, d_ref, down_ref, up_ref, *, shards):
    pieces = in_order([ref[...].astype(F32) for ref in (a_ref, b_ref, c_ref, d_ref)], quarter_ref[0])
    rows, width = pieces[0].shape[0], pieces[0].shape[1] // 2
    unit = width // shards
    for place in range(QUARTERS):
        down_ref[place * rows:(place + 1) * rows, :] = pieces[place][:, :width]
    for shard in range(shards):
        start = width + shard * unit
        up_ref[:, shard * QUARTERS * unit:(shard + 1) * QUARTERS * unit] = jnp.concatenate(
            [piece[:, start:start + unit] for piece in pieces], 1
        )


def placed_parts(kernel, quarter, pieces, shapes):
    size = sum(math.prod(shape) for shape in shapes)
    return pl.pallas_call(
        kernel,
        in_specs=scalar_first(QUARTERS),
        out_shape=[jax.ShapeDtypeStruct(shape, F32) for shape in shapes],
        compiler_params=pltpu.CompilerParams(vmem_limit_bytes=32 * 2**20),
        cost_estimate=pl.CostEstimate(flops=size, bytes_accessed=6 * size, transcendentals=0),
        name="placed_parts",
    )(quarter.reshape(1), *pieces)


def across(block, bit):
    count = lax.axis_size("replica")
    return lax.ppermute(block, "replica", [(i, i ^ bit) for i in range(count)])


def swap_sections(block):
    return lax.ppermute(block, "section", [(0, 1), (1, 0)])


def reversed_bits(index, count):
    result, bit = index * 0, 1
    while bit < count:
        result = result * 2 + index // bit % 2
        bit *= 2
    return result


def transposed(block, source, target):
    shards, replicas = lax.axis_size("shard"), lax.axis_size("replica")

    def flat(section, shard, replica):
        return (section * shards + shard) * replicas + replica

    route = []
    for shard in range(shards):
        for replica in range(replicas):
            group, place = divmod(replica, shards)
            here = (shard, replica)
            there = (reversed_bits(place, shards), group * shards + reversed_bits(shard, shards))
            if source is None:
                route += [(flat(s, *here), flat(s, *there)) for s in range(2)]
            else:
                route.append((flat(source, *here), flat(target, *there)))
    return lax.ppermute(block, AXES, route)


def in_order(pieces, quarter):
    odd, high = (quarter & 1) == 1, (quarter & 2) == 2
    a, b, c, d = pieces
    a, b, c, d = jnp.where(odd, b, a), jnp.where(odd, a, b), jnp.where(odd, d, c), jnp.where(odd, c, d)
    return jnp.where(high, c, a), jnp.where(high, d, b), jnp.where(high, a, c), jnp.where(high, b, d)


def after(value, *others):
    return lax.optimization_barrier((value, others))[0]


def spread(piece, far):
    return piece, across(piece, 1), far, across(far, 1)


def low_sum(*parts):
    total = parts[0].astype(F32)
    for part in parts[1:]:
        total = total + part.astype(F32)
    return total.astype(BF16)


def body(edges, attn_in, attn_out, mlp_up, mlp_down, vectors, key_mask):
    section = lax.axis_index("section")
    first = section == 0
    replica = lax.axis_index("replica")
    shards, replicas = lax.axis_size("shard"), lax.axis_size("replica")
    quarter = replica % QUARTERS
    edges_here = edges[0]
    clips, frames, width = edges_here.shape
    hidden = mlp_up.shape[2]
    dim = width // H
    heads = H // QUARTERS
    wide = heads * dim
    unit = hidden // (shards * QUARTERS)
    rows = attn_in.shape[1]
    assert clips == 2 and lax.axis_size("section") == 2 and replicas % shards == 0 and replicas % QUARTERS == 0

    def by_layer(own, other):
        return jnp.where(first, own, other), jnp.where(first, other, own)

    vec_by_layer = by_layer(vectors[0], swap_sections(vectors[0]))
    mask_row = transposed(
        lax.dynamic_index_in_dim(key_mask, section, 0, keepdims=False).astype(F32)[None], None, None
    )[0]
    inputs = jnp.where(first, transposed(edges_here[0], 0, 0), transposed(edges_here[1], 0, 1))

    def pick(block, axis):
        return lax.dynamic_index_in_dim(block, quarter, axis, keepdims=False)

    def gathered(block):
        return lax.all_gather(block, "shard", axis=0, tiled=True)

    query_in, key_in, value_in = (
        pick(attn_in[0][:, i * width:(i + 1) * width].reshape(rows, QUARTERS, wide), 1) for i in range(3)
    )
    own_proj = jnp.concatenate(
        [key_in, value_in, query_in, pick(attn_out[0].reshape(rows, QUARTERS, width // QUARTERS), 1)], 1
    )
    own_up = pick(mlp_up[0].reshape(rows, shards, QUARTERS, unit), 2).reshape(rows, shards * unit)
    own_down = pick(mlp_down[0].reshape(QUARTERS, unit, width), 0)
    proj_zero, proj_one = by_layer(own_proj, swap_sections(own_proj))
    proj_zero = gathered(proj_zero)
    own_up = after(own_up, inputs)
    own_down = after(own_down, own_up)
    proj_one = after(proj_one, own_down)
    own_up, own_down, proj_one = gathered(own_up), gathered(own_down), gathered(proj_one)
    other_up = swap_sections(own_up)

    def head_weights(block):
        pieces = spread(block, across(block, 2))
        return pieces, jnp.concatenate(in_order([piece[:, 3 * wide:] for piece in pieces], quarter), 1)

    heads_by_layer = [head_weights(proj_zero), None]
    hidden_by_layer = [None, None]

    members = [0]
    bit = 2
    while bit < shards:
        members = members + [m ^ bit for m in members]
        bit *= 2
    members = members + [m ^ 1 for m in members]
    place = replica % shards
    bias_row = jnp.concatenate(
        [lax.dynamic_slice_in_dim(mask_row, reversed_bits(place ^ m, shards) * frames, frames, 0) for m in members]
    )
    bias_row = jnp.where(bias_row > 0, 0.0, MASKED).astype(BF16)
    lane = jnp.arange(dim)[None, :]
    key_bias = jnp.where(lane == 0, bias_row[:, None], jnp.zeros((), BF16))

    def chips_rows(block):
        bit = 2
        while bit < shards:
            block = jnp.concatenate([block, across(block, bit)], 0)
            bit *= 2
        return block

    def forward(x_low, layer):
        vec = vec_by_layer[layer]
        x_set = chips_rows(x_low)
        proj, w_out = heads_by_layer[layer]
        normed = layer_norm(x_set.astype(F32), vec[0], vec[1]).astype(BF16)
        zeros = jnp.zeros((QUARTERS, wide), F32)
        bias_in = jnp.stack([zeros, vec[3].reshape(QUARTERS, wide), vec[2].reshape(QUARTERS, wide)], 1)
        own_qkv, other_kv = {}, {}
        order = (0, 1, 2, 3)
        for p in order:
            bias = lax.dynamic_index_in_dim(bias_in, quarter ^ p, 0, keepdims=False).reshape(3 * wide)
            own_qkv[p] = (dot(normed, proj[p][:, :3 * wide]) + bias).astype(BF16)
            other_kv[p ^ 1] = across(own_qkv[p][:, :2 * wide], 1)
        outs, weights, inverses = {}, {}, {}
        late = {}
        for step, p in enumerate(order):
            own = own_qkv[p]
            if layer == 0 and step == 3:
                own = after(own, proj_one)
            outs[p], weights[p], inverses[p] = attend(own, other_kv[p], key_bias, heads, frames)
            if layer == 0 and step == 0:
                late["up"] = by_layer(own_up, after(other_up, outs[p]))
                late["up_far"] = across(late["up"][0], 2)
                other_down = swap_sections(after(own_down, outs[p]))
            elif layer == 0 and step == 2:
                late["down"] = by_layer(own_down, after(other_down, outs[p]))
                late["down_far"] = across(late["down"][0], 2)
                w_up = spread(late["up"][0], after(late["up_far"], outs[p]))
                late["one_far"] = across(after(proj_one, outs[p]), 2)
            elif layer == 0 and step == 3:
                w_down = spread(late["down"][0], after(late["down_far"], outs[p]))
                hidden_by_layer[0] = (w_up, w_down)
            elif layer == 1 and step == 0:
                late["down_far"] = across(after(pending_one["down"], outs[p]), 2)
            elif layer == 1 and step == 1:
                cot = after(edges_here, outs[p])
                pending_one["cot"] = [transposed(cot[0], 1, 0), transposed(cot[1], 1, 1)]
                w_up = spread(pending_one["up"], after(pending_one["up_far"], outs[p]))
            elif layer == 1 and step == 3:
                w_down = spread(pending_one["down"], after(late["down_far"], outs[p]))
                hidden_by_layer[1] = (w_up, w_down)
        attended, middle, normed_two = out_part(quarter, [outs[p] for p in range(QUARTERS)], w_out, x_low, vec)
        w_up, w_down = hidden_by_layer[layer]
        bias_up = vec[8:].reshape(shards, QUARTERS, unit)
        acts, slopes = [], []
        result = middle + vec[7]
        for p in range(QUARTERS):
            bias = lax.dynamic_index_in_dim(bias_up, quarter ^ p, 1, keepdims=False).reshape(1, shards * unit)
            if layer == 0 and p == QUARTERS - 1:
                result = after(result, late["one_far"])
            act, slope, result = mlp_part(normed_two, w_up[p], bias, w_down[p], result)
            acts.append(act)
            slopes.append(slope)
            if layer == 0 and p == 0:
                far = after(late["one_far"], act)
                pieces = spread(proj_one, far)
                w_out_one = jnp.concatenate(in_order([piece[:, 3 * wide:] for piece in pieces], quarter), 1)
                heads_by_layer[1] = (pieces, w_out_one)
                pending_one["up"], pending_one["down"] = late["up"][1], late["down"][1]
                pending_one["up_far"] = across(after(pending_one["up"], far), 2)
        kept = (x_low, normed, own_qkv, other_kv, weights, inverses, attended, middle, normed_two, acts, slopes)
        return result.astype(BF16), kept

    pending_one = {}

    def scattered(block):
        bit = QUARTERS
        while bit < replicas:
            block = low_sum(block, across(block, bit))
            bit *= 2
        return lax.psum_scatter(block, "shard", scatter_dimension=0, tiled=True)

    def half_sum(block):
        cut = block.shape[1] // 2
        left, right = block[:, :cut], block[:, cut:]
        return low_sum(jnp.where(first, left, right), swap_sections(jnp.where(first, right, left)))

    def backward(cot, layer, kept, above):
        (proj, w_out), (w_up, w_down), vec = heads_by_layer[layer], hidden_by_layer[layer], vec_by_layer[layer]
        x_low, normed, own_qkv, other_kv, weights, inverses, attended, middle, normed_two, acts, slopes = kept
        order = (3, 1, 2, 0)
        g_down, g_up, up_sums, near_down, near_up = {}, {}, {}, {}, {}
        d_normed_two = jnp.zeros((frames, width), F32)
        for step, p in enumerate(order):
            g_down[p], g_up[p], up_sums[p], d_normed_two = mlp_back_part(
                cot, normed_two, acts[p], slopes[p], w_up[p], w_down[p], d_normed_two
            )
            if p & 1:
                near_down[p ^ 1] = across(g_down[p], 1)
                near_up[p ^ 1] = across(g_up[p], 1)
            if above is not None and step == 1:
                halves = [after(half, g_up[p]) for half in above["halves"]]
                above["mlp"] = scattered(jnp.concatenate(halves, 1))
        d_middle, mid_rows, d_heads, d_attn_parts = middle_back(quarter, d_normed_two, middle, cot, vec, w_out)
        if above is not None:
            far = after(above["far_proj"], mid_rows)
            above["half"] = half_sum(above["finish"](far))
        far_down = low_sum(g_down[2], after(near_down[2], mid_rows))
        results = {}
        for step, p in enumerate(order):
            head = d_heads[p]
            if step == 1:
                head = after(head, far_down)
                far_down = across(far_down, 2)
            elif step == 2:
                head = after(head, far_up)
                if layer == 0:
                    far_up = across(far_up, 2)
                if above is not None:
                    half = after(above["half"], results[order[1]][0])
                    above["proj"] = scattered(jnp.concatenate([half, above["vec"]], 1))
            elif step == 3 and above is not None:
                head = after(head, above["mlp"])
            results[p] = attend_back(own_qkv[p], other_kv[p], weights[p], inverses[p], head, heads, frames)
            if step == 0:
                far_up = low_sum(g_up[2], after(near_up[2], results[p][0]))
        last = results[order[3]][0]
        from_other = {p: across(results[p ^ 1][2], 1) for p in range(QUARTERS)}
        half_down = half_sum(low_sum(g_down[0], near_down[0], after(far_down, last)))
        g_proj, sums_in, near_proj = {}, {}, {}
        d_normed = jnp.zeros(normed.shape, F32)
        for p in order:
            g_proj[p], sums_in[p], d_normed = proj_back(
                normed, results[p][1], from_other[p], results[p][0], attended, d_attn_parts[p], proj[p], d_normed
            )
            if p & 1:
                near_proj[p ^ 1] = across(g_proj[p], 1)
        block = d_normed
        bit = shards // 2
        while bit >= 2:
            cut = block.shape[0] // 2
            block = block[:cut] + across(block[cut:].astype(BF16), bit).astype(F32)
            bit //= 2
        if layer == 1:
            far_up = across(after(far_up, block), 2)
        half_up = half_sum(low_sum(g_up[0], near_up[0], after(far_up, d_normed)))
        if layer == 1:
            far_proj = low_sum(g_proj[2], after(near_proj[2], block))
        else:
            far_proj = low_sum(g_proj[2], after(near_proj[2], d_normed))
        back, g_gain_one, g_shift_one = norm_back(x_low.astype(F32), vec[0], block)
        g_low = (d_middle + back).astype(BF16)
        g_low = after(g_low, far_proj)
        far_proj = across(far_proj, 2)
        vec_block = vector_block(
            quarter, [sums_in[p] for p in range(QUARTERS)], [up_sums[p] for p in range(QUARTERS)],
            g_gain_one, g_shift_one, mid_rows, shards,
        )
        if above is not None:
            g_low = after(g_low, above["proj"])

        def finish_proj(other):
            return low_sum(g_proj[0], near_proj[0], other)

        return g_low, {"halves": [half_down, half_up], "far_proj": far_proj, "finish": finish_proj, "vec": vec_block}

    x_one, kept_zero = forward(inputs, 0)
    y_one, kept_one = forward(x_one, 1)
    cot = [after(part, y_one) for part in pending_one["cot"]]
    g_one, one = backward(jnp.where(first, cot[0], cot[1]), 1, kept_one, None)
    g_zero, zero = backward(g_one, 0, kept_zero, one)
    y_one = after(y_one, g_one)
    out_slots = [transposed(y_one, 0, 1), transposed(y_one, 1, 1)]
    g_zero = after(g_zero, *out_slots)
    back_slots = [transposed(g_zero, 0, 0), transposed(g_zero, 1, 0)]
    edges_out = jnp.stack([jnp.where(first, b, o) for b, o in zip(back_slots, out_slots)])
    mlp_one, proj_one = one["mlp"], one["proj"]
    mlp_zero = scattered(jnp.concatenate([after(half, g_zero) for half in zero["halves"]], 1))
    far = after(zero["far_proj"], g_zero)
    proj_zero = jnp.concatenate([half_sum(zero["finish"](far)), zero["vec"]], 1)
    proj_zero = scattered(after(proj_zero, *back_slots))

    def exchanged(zero, one):
        return jnp.where(first, zero, one), swap_sections(jnp.where(first, one, zero))

    def joined(own, other):
        cut = width // 2
        parts = []
        for start in range(0, own.shape[1], cut):
            a, b = own[:, start:start + cut], other[:, start:start + cut]
            parts += [jnp.where(first, a, b), jnp.where(first, b, a)]
        return parts

    part = jnp.concatenate(joined(*exchanged(mlp_zero, mlp_one)), 1)
    far = across(part, 2)
    f_down, f_up = placed_parts(
        functools.partial(place_mlp_kernel, shards=shards), quarter, spread(part, far),
        [mlp_down.shape[1:], mlp_up.shape[1:]],
    )
    proj_zero = after(proj_zero, far)
    own, other = exchanged(proj_zero, proj_one)
    cut = width // 2
    part = jnp.concatenate(
        joined(own[:, :cut], other[:, :cut]) + [low_sum(own[:, cut:], other[:, cut:])], 1
    )
    f_in, f_out, f_vec = placed_parts(
        place_proj_kernel, quarter, spread(part, across(part, 2)),
        [attn_in.shape[1:], attn_out.shape[1:], (128, rows)],
    )
    f_vec = f_vec[:vectors.shape[1]]
    return edges_out[None], f_in[None], f_out[None], f_up[None], f_down[None], f_vec[None]


def solution(mesh):
    placed = (
        P("section", "replica", "shard", None),
        P("section", "shard", None),
        P("section", "shard", None),
        P("section", "shard", None),
        P("section", "shard", None),
        P("section", None, None),
        P("replica", None),
    )
    return jax.shard_map(
        body,
        mesh=mesh,
        in_specs=placed,
        out_specs=(
            P("section", "replica", "shard", None),
            P("section", "shard", None),
            P("section", "shard", None),
            P("section", "shard", None),
            P("section", "shard", None),
            P("section", None, "shard"),
        ),
        check_vma=False,
    )
```

```python
import functools
import math

import jax
import jax.numpy as jnp
from jax import lax
from jax.experimental import pallas as pl
from jax.experimental.pallas import tpu as pltpu
from jax.sharding import PartitionSpec as P

H = 12
EPS = 1e-05
MASKED = -1e30
QUARTERS = 4
ATTEND_VMEM = 58 * 2**20
BF16 = jnp.bfloat16
F32 = jnp.float32
AXES = ("section", "shard", "replica")
NN = (((1,), (0,)), ((), ()))
NT = (((1,), (1,)), ((), ()))
TN = (((0,), (0,)), ((), ()))


def dot(a, b, dims=NN):
    return lax.dot_general(a, b, dims, preferred_element_type=F32)


def layer_norm(values, gain, shift):
    center = values - jnp.mean(values, -1, keepdims=True)
    spread = jnp.mean(center * center, -1, keepdims=True)
    return center * lax.rsqrt(spread + EPS) * gain + shift


def key_chunks(sources, size):
    chunks, base = [], 0
    for source in range(len(sources)):
        rows = sources[source].shape[0]
        for start in range(0, rows, size):
            chunks.append((source, start, base + start))
        base += rows
    return chunks


def attend_kernel(own_ref, other_ref, bias_ref, out_ref, exp_ref, inv_ref, score_ref, *, heads, frames, chunk):
    dim = own_ref.shape[1] // (3 * heads)
    wide = heads * dim
    sources = (own_ref, other_ref)
    chunks = key_chunks(sources, chunk)

    def one_head(head):
        at = head * dim
        query = own_ref[0:frames, 2 * wide + at:2 * wide + at + dim] * (dim ** -0.5)
        lane = lax.broadcasted_iota(jnp.int32, (frames, dim), 1)
        query = jnp.concatenate([query.astype(BF16), (lane == 0).astype(BF16)], 1)
        top = None
        for source, start, row in chunks:
            key = sources[source][start:start + chunk, at:at + dim]
            key = jnp.concatenate([key, bias_ref[row:row + chunk, :]], 1)
            score = dot(key, query, NT)
            score_ref[row:row + chunk, :] = score
            part = jnp.max(score, 0, keepdims=True)
            top = part if top is None else jnp.maximum(top, part)
        total = None
        for source, start, row in chunks:
            weight = jnp.exp(score_ref[row:row + chunk, :] - top).astype(BF16)
            exp_ref[0, row:row + chunk, :] = weight
            value = sources[source][start:start + chunk, wide + at:wide + at + dim]
            value = jnp.concatenate([value, jnp.ones_like(value)], 1)
            part = dot(value, weight, TN)
            total = part if total is None else total + part
        inverse = 1.0 / total[dim:dim + 1, :]
        inv_ref[head:head + 1, :] = inverse
        out_ref[:, at:at + dim] = (total[0:dim, :] * inverse).T.astype(BF16)

    for head in range(heads):
        pl.when(pl.program_id(0) == head)(functools.partial(one_head, head))


def whole_block(shape):
    return pl.BlockSpec(shape, lambda i: (0,) * len(shape))


def chunk_size(own, frames):
    chunk = min(256, frames)
    return frames if own.shape[0] % chunk else chunk


def attend(own, other, bias, heads, frames):
    keys = own.shape[0] + other.shape[0]
    wide = own.shape[1] // 3
    return pl.pallas_call(
        functools.partial(attend_kernel, heads=heads, frames=frames, chunk=chunk_size(own, frames)),
        grid=(heads,),
        in_specs=[whole_block(own.shape), whole_block(other.shape), whole_block(bias.shape)],
        out_specs=[
            whole_block((frames, wide)),
            pl.BlockSpec((1, keys, frames), lambda i: (i, 0, 0)),
            whole_block((heads, frames)),
        ],
        out_shape=(
            jax.ShapeDtypeStruct((frames, wide), BF16),
            jax.ShapeDtypeStruct((heads, keys, frames), BF16),
            jax.ShapeDtypeStruct((heads, frames), F32),
        ),
        scratch_shapes=[pltpu.VMEM((keys, frames), F32)],
        compiler_params=pltpu.CompilerParams(vmem_limit_bytes=ATTEND_VMEM),
        cost_estimate=pl.CostEstimate(
            flops=16 * keys * frames * wide, bytes_accessed=2 * heads * keys * frames, transcendentals=heads * keys * frames
        ),
        name="attend",
    )(own, other, bias)


def attend_back_kernel(own_ref, other_ref, exp_ref, inv_ref, dout_ref, dq_ref, down_ref, dother_ref, prod_ref, *, heads, frames, chunk):
    dim = own_ref.shape[1] // (3 * heads)
    wide = heads * dim
    scale = dim ** -0.5
    sources = (own_ref, other_ref)
    targets = (down_ref, dother_ref)
    chunks = key_chunks(sources, chunk)

    def one_head(head):
        at = head * dim
        query = (own_ref[0:frames, 2 * wide + at:2 * wide + at + dim] * scale).astype(BF16)
        inverse = inv_ref[head:head + 1, :]
        dout_t = dout_ref[:, at:at + dim].astype(F32).T * inverse
        dout = dout_t.T.astype(BF16)
        dout_t = dout_t.astype(BF16)
        delta = None
        for source, start, row in chunks:
            value = sources[source][start:start + chunk, wide + at:wide + at + dim]
            weight = exp_ref[0, row:row + chunk, :]
            prod = dot(value, dout_t) * weight.astype(F32)
            prod_ref[row:row + chunk, :] = prod
            part = jnp.sum(prod, 0, keepdims=True)
            delta = part if delta is None else delta + part
            targets[source][start:start + chunk, wide + at:wide + at + dim] = dot(weight, dout).astype(BF16)
        delta = delta * inverse
        dq_t = None
        for source, start, row in chunks:
            key = sources[source][start:start + chunk, at:at + dim]
            weight = exp_ref[0, row:row + chunk, :].astype(F32)
            ds = (prod_ref[row:row + chunk, :] - weight * delta).astype(BF16)
            targets[source][start:start + chunk, at:at + dim] = dot(ds, query).astype(BF16)
            part = dot(key, ds, TN)
            dq_t = part if dq_t is None else dq_t + part
        dq_ref[:, at:at + dim] = (dq_t.T * scale).astype(BF16)

    for head in range(heads):
        pl.when(pl.program_id(0) == head)(functools.partial(one_head, head))


def attend_back(own, other, weights, inverse, dout, heads, frames):
    keys = own.shape[0] + other.shape[0]
    wide = own.shape[1] // 3
    results = ((frames, wide), (own.shape[0], 2 * wide), (other.shape[0], 2 * wide))
    return pl.pallas_call(
        functools.partial(attend_back_kernel, heads=heads, frames=frames, chunk=chunk_size(own, frames)),
        grid=(heads,),
        in_specs=[
            whole_block(own.shape), whole_block(other.shape),
            pl.BlockSpec((1, keys, frames), lambda i: (i, 0, 0)),
            whole_block(inverse.shape), whole_block(dout.shape),
        ],
        out_specs=[whole_block(shape) for shape in results],
        out_shape=[jax.ShapeDtypeStruct(shape, BF16) for shape in results],
        scratch_shapes=[pltpu.VMEM((keys, frames), F32)],
        compiler_params=pltpu.CompilerParams(vmem_limit_bytes=ATTEND_VMEM),
        cost_estimate=pl.CostEstimate(
            flops=32 * keys * frames * wide, bytes_accessed=2 * heads * keys * frames, transcendentals=0
        ),
        name="attend_back",
    )(own, other, weights, inverse, dout)


def out_kernel(quarter_ref, a_ref, b_ref, c_ref, d_ref, weight_ref, x_ref, vec_ref, att_ref, mid_ref, norm_ref):
    parts = [ref[...] for ref in (a_ref, b_ref, c_ref, d_ref)]
    attended = jnp.concatenate(in_order(parts, quarter_ref[0]), 1)
    att_ref[...] = attended
    middle = x_ref[...].astype(F32) + dot(attended, weight_ref[...]) + vec_ref[4:5, :]
    mid_ref[...] = middle
    norm_ref[...] = layer_norm(middle, vec_ref[5:6, :], vec_ref[6:7, :]).astype(BF16)


def scalar_first(count):
    return [pl.BlockSpec(memory_space=pltpu.SMEM)] + [pl.BlockSpec(memory_space=pltpu.VMEM)] * count


def out_part(quarter, outs, weight, x_low, vec):
    shape = x_low.shape
    return pl.pallas_call(
        out_kernel,
        in_specs=scalar_first(7),
        out_shape=[jax.ShapeDtypeStruct(shape, kind) for kind in (BF16, F32, BF16)],
        compiler_params=pltpu.CompilerParams(vmem_limit_bytes=32 * 2**20),
        cost_estimate=pl.CostEstimate(
            flops=2 * math.prod(shape) * shape[1], bytes_accessed=14 * math.prod(shape), transcendentals=0
        ),
        name="out_part",
    )(quarter.reshape(1), *outs, weight, x_low, vec)


def norm_back(values, gain, grad):
    center = values - jnp.mean(values, -1, keepdims=True)
    inv = lax.rsqrt(jnp.mean(center * center, -1, keepdims=True) + EPS)
    unit_values = center * inv
    scaled = grad * gain
    back = inv * (
        scaled - jnp.mean(scaled, -1, keepdims=True)
        - unit_values * jnp.mean(scaled * unit_values, -1, keepdims=True)
    )
    return back, jnp.sum(grad * unit_values, 0, keepdims=True), jnp.sum(grad, 0, keepdims=True)


def middle_back_kernel(quarter_ref, grad_ref, mid_ref, cot_ref, vec_ref, weight_ref, dmid_ref, rows_ref, *part_refs):
    cot = cot_ref[...].astype(F32)
    back, gain, shift = norm_back(mid_ref[...], vec_ref[5:6, :], grad_ref[...])
    d_middle = cot + back
    dmid_ref[...] = d_middle
    d_attn = d_middle.astype(BF16)
    d_low = d_attn.astype(F32)
    rows_ref[...] = jnp.concatenate(
        [gain, shift, jnp.sum(d_low, 0, keepdims=True), jnp.sum(cot, 0, keepdims=True)], 0
    )
    d_attended = dot(d_attn, weight_ref[...], NT).astype(BF16)
    for refs, whole in ((part_refs[:QUARTERS], d_attended), (part_refs[QUARTERS:], d_attn)):
        wide = whole.shape[1] // QUARTERS
        parts = in_order([whole[:, p * wide:(p + 1) * wide] for p in range(QUARTERS)], quarter_ref[0])
        for ref, part in zip(refs, parts):
            ref[...] = part


def middle_back(quarter, grad, middle, cot, vec, weight):
    frames, width = middle.shape
    part = jax.ShapeDtypeStruct((frames, width // QUARTERS), BF16)
    results = pl.pallas_call(
        middle_back_kernel,
        in_specs=scalar_first(5),
        out_shape=[jax.ShapeDtypeStruct((frames, width), F32), jax.ShapeDtypeStruct((4, width), F32)]
        + [part] * (2 * QUARTERS),
        compiler_params=pltpu.CompilerParams(vmem_limit_bytes=32 * 2**20),
        cost_estimate=pl.CostEstimate(
            flops=2 * frames * width * width, bytes_accessed=18 * frames * width, transcendentals=0
        ),
        name="middle_back",
    )(quarter.reshape(1), grad, middle, cot, vec, weight)
    return results[0], results[1], results[2:2 + QUARTERS], results[2 + QUARTERS:]


def vector_kernel(quarter_ref, *refs, shards):
    ins, up_ins = refs[:QUARTERS], refs[QUARTERS:2 * QUARTERS]
    gain_ref, shift_ref, mid_ref, out_ref = refs[2 * QUARTERS:]
    width = out_ref.shape[0]
    wide, unit = width // QUARTERS, width // shards
    ins = in_order([ref[...] for ref in ins], quarter_ref[0])
    value_row, query_row = (
        jnp.concatenate([piece[:, i * wide:(i + 1) * wide] for piece in ins], 1) for i in range(1, 3)
    )
    ups = in_order([ref[...] for ref in up_ins], quarter_ref[0])
    up_row = jnp.concatenate(
        [piece[:, shard * unit:(shard + 1) * unit] for shard in range(shards) for piece in ups], 1
    )
    rows = [gain_ref[...], shift_ref[...], query_row, value_row, mid_ref[2:3, :], mid_ref[0:2, :], mid_ref[3:4, :]]
    rows += [up_row[:, start:start + width] for start in range(0, up_row.shape[1], width)]
    rows = jnp.concatenate(rows, 0)
    rows = jnp.concatenate([rows, jnp.zeros((128 - rows.shape[0], width), F32)], 0)
    out_ref[...] = rows.T.astype(BF16)


def vector_block(quarter, sums_in, up_sums, gain, shift, mid_rows, shards):
    width = gain.shape[1]
    return pl.pallas_call(
        functools.partial(vector_kernel, shards=shards),
        in_specs=scalar_first(2 * QUARTERS + 3),
        out_shape=jax.ShapeDtypeStruct((width, 128), BF16),
        compiler_params=pltpu.CompilerParams(vmem_limit_bytes=32 * 2**20),
        cost_estimate=pl.CostEstimate(flops=128 * width, bytes_accessed=512 * width, transcendentals=0),
        name="vector_block",
    )(quarter.reshape(1), *sums_in, *up_sums, gain, shift, mid_rows)


def column_tile(columns):
    return 256 if columns % 256 == 0 else columns


def mlp_kernel(in_ref, up_ref, bias_ref, down_ref, before_ref, act_ref, slope_ref, sum_ref):
    up = dot(in_ref[...], up_ref[...]) + bias_ref[...]
    cdf = 0.5 + 0.5 * lax.erf(up * (0.5 ** 0.5))
    pdf = jnp.exp(-0.5 * up * up) * 0.3989422804014327
    act = (up * cdf).astype(BF16)
    act_ref[...] = act
    slope_ref[...] = (cdf + up * pdf).astype(BF16)
    part = dot(act, down_ref[...])

    @pl.when(pl.program_id(0) == 0)
    def _():
        sum_ref[...] = before_ref[...] + part

    @pl.when(pl.program_id(0) > 0)
    def _():
        sum_ref[...] += part


def mlp_part(values, up, bias, down, before):
    rows, depth = values.shape
    columns = up.shape[1]
    tile = column_tile(columns)
    whole = pl.BlockSpec((rows, depth), lambda i: (0, 0))
    hidden = pl.BlockSpec((rows, tile), lambda i: (0, i))
    return pl.pallas_call(
        mlp_kernel,
        grid=(columns // tile,),
        in_specs=[
            whole,
            pl.BlockSpec((depth, tile), lambda i: (0, i)),
            pl.BlockSpec((1, tile), lambda i: (0, i)),
            pl.BlockSpec((tile, depth), lambda i: (i, 0)),
            whole,
        ],
        out_specs=[hidden, hidden, whole],
        out_shape=[
            jax.ShapeDtypeStruct((rows, columns), BF16),
            jax.ShapeDtypeStruct((rows, columns), BF16),
            jax.ShapeDtypeStruct((rows, depth), F32),
        ],
        compiler_params=pltpu.CompilerParams(vmem_limit_bytes=32 * 2**20),
        cost_estimate=pl.CostEstimate(
            flops=4 * rows * depth * columns, bytes_accessed=4 * (3 * rows * depth + depth * columns + rows * columns),
            transcendentals=2 * rows * columns,
        ),
        name="mlp_part",
    )(values, up, bias, down, before)


def mlp_back_kernel(grad_ref, in_ref, act_ref, slope_ref, up_ref, down_ref, before_ref, gd_ref, gu_ref, row_ref, sum_ref):
    grad = grad_ref[...]
    d_up = (dot(grad, down_ref[...], NT) * slope_ref[...].astype(F32)).astype(BF16)
    gd_ref[...] = dot(act_ref[...], grad, TN).astype(BF16)
    gu_ref[...] = dot(in_ref[...], d_up, TN).astype(BF16)
    row_ref[...] = jnp.sum(d_up.astype(F32), 0, keepdims=True)
    part = dot(d_up, up_ref[...], NT)

    @pl.when(pl.program_id(0) == 0)
    def _():
        sum_ref[...] = before_ref[...] + part

    @pl.when(pl.program_id(0) > 0)
    def _():
        sum_ref[...] += part


def mlp_back_part(grad, values, act, slope, up, down, before):
    rows, depth = values.shape
    columns = up.shape[1]
    tile = column_tile(columns)
    whole = pl.BlockSpec((rows, depth), lambda i: (0, 0))
    hidden = pl.BlockSpec((rows, tile), lambda i: (0, i))
    up_tile = pl.BlockSpec((depth, tile), lambda i: (0, i))
    down_tile = pl.BlockSpec((tile, depth), lambda i: (i, 0))
    return pl.pallas_call(
        mlp_back_kernel,
        grid=(columns // tile,),
        in_specs=[whole, whole, hidden, hidden, up_tile, down_tile, whole],
        out_specs=[down_tile, up_tile, pl.BlockSpec((1, tile), lambda i: (0, i)), whole],
        out_shape=[
            jax.ShapeDtypeStruct((columns, depth), BF16),
            jax.ShapeDtypeStruct((depth, columns), BF16),
            jax.ShapeDtypeStruct((1, columns), F32),
            jax.ShapeDtypeStruct((rows, depth), F32),
        ],
        compiler_params=pltpu.CompilerParams(vmem_limit_bytes=40 * 2**20),
        cost_estimate=pl.CostEstimate(
            flops=8 * rows * depth * columns, bytes_accessed=4 * (3 * rows * depth + 2 * depth * columns + rows * columns),
            transcendentals=0,
        ),
        name="mlp_back_part",
    )(grad, values, act, slope, up, down, before)


def proj_back_kernel(in_ref, own_ref, other_ref, query_ref, out_ref, grad_ref, weight_ref, before_ref, g_ref, row_ref, sum_ref):
    frames, wide = query_ref.shape
    both = (own_ref[...].astype(F32) + other_ref[...].astype(F32)).astype(BF16)
    query = query_ref[...]
    values = in_ref[...]
    g_ref[...] = jnp.concatenate(
        [dot(values, both, TN), dot(values[:frames], query, TN), dot(out_ref[...], grad_ref[...], TN)], 1
    ).astype(BF16)
    row_ref[...] = jnp.concatenate(
        [jnp.sum(both.astype(F32), 0, keepdims=True), jnp.sum(query.astype(F32), 0, keepdims=True)], 1
    )
    total = before_ref[...] + dot(both, weight_ref[:, :2 * wide], NT)
    own = total[:frames] + dot(query, weight_ref[:, 2 * wide:3 * wide], NT)
    sum_ref[0:frames, :] = own
    sum_ref[frames:, :] = total[frames:]


def proj_back(values, own, other, query, out, grad, weight, before):
    rows, depth = values.shape
    wide = query.shape[1]
    return pl.pallas_call(
        proj_back_kernel,
        out_shape=[
            jax.ShapeDtypeStruct(weight.shape, BF16),
            jax.ShapeDtypeStruct((1, 3 * wide), F32),
            jax.ShapeDtypeStruct((rows, depth), F32),
        ],
        compiler_params=pltpu.CompilerParams(vmem_limit_bytes=40 * 2**20),
        cost_estimate=pl.CostEstimate(
            flops=8 * rows * depth * 2 * wide, bytes_accessed=12 * rows * depth + 4 * depth * weight.shape[1],
            transcendentals=0,
        ),
        name="proj_back",
    )(values, own, other, query, out, grad, weight, before)


def place_proj_kernel(quarter_ref, a_ref, b_ref, c_ref, d_ref, qkv_ref, out_ref, vec_ref):
    pieces = [ref[...].astype(F32) for ref in (a_ref, b_ref, c_ref, d_ref)]
    width = out_ref.shape[1]
    wide = width // QUARTERS
    total = pieces[0][:, width:] + pieces[1][:, width:] + pieces[2][:, width:] + pieces[3][:, width:]
    vec_ref[...] = total.T
    pieces = in_order([piece[:, :width] for piece in pieces], quarter_ref[0])
    for column, part in ((0, 2), (1, 0), (2, 1)):
        qkv_ref[:, column * width:(column + 1) * width] = jnp.concatenate(
            [piece[:, part * wide:(part + 1) * wide] for piece in pieces], 1
        )
    out_ref[...] = jnp.concatenate([piece[:, 3 * wide:] for piece in pieces], 1)


def place_mlp_kernel(quarter_ref, a_ref, b_ref, c_ref, d_ref, down_ref, up_ref, *, shards):
    pieces = in_order([ref[...].astype(F32) for ref in (a_ref, b_ref, c_ref, d_ref)], quarter_ref[0])
    rows, width = pieces[0].shape[0], pieces[0].shape[1] // 2
    unit = width // shards
    for place in range(QUARTERS):
        down_ref[place * rows:(place + 1) * rows, :] = pieces[place][:, :width]
    for shard in range(shards):
        start = width + shard * unit
        up_ref[:, shard * QUARTERS * unit:(shard + 1) * QUARTERS * unit] = jnp.concatenate(
            [piece[:, start:start + unit] for piece in pieces], 1
        )


def placed_parts(kernel, quarter, pieces, shapes):
    size = sum(math.prod(shape) for shape in shapes)
    return pl.pallas_call(
        kernel,
        in_specs=scalar_first(QUARTERS),
        out_shape=[jax.ShapeDtypeStruct(shape, F32) for shape in shapes],
        compiler_params=pltpu.CompilerParams(vmem_limit_bytes=32 * 2**20),
        cost_estimate=pl.CostEstimate(flops=size, bytes_accessed=6 * size, transcendentals=0),
        name="placed_parts",
    )(quarter.reshape(1), *pieces)


def across(block, bit):
    count = lax.axis_size("replica")
    return lax.ppermute(block, "replica", [(i, i ^ bit) for i in range(count)])


def swap_sections(block):
    return lax.ppermute(block, "section", [(0, 1), (1, 0)])


def reversed_bits(index, count):
    result, bit = index * 0, 1
    while bit < count:
        result = result * 2 + index // bit % 2
        bit *= 2
    return result


def transposed(block, source, target):
    shards, replicas = lax.axis_size("shard"), lax.axis_size("replica")

    def flat(section, shard, replica):
        return (section * shards + shard) * replicas + replica

    route = []
    for shard in range(shards):
        for replica in range(replicas):
            group, place = divmod(replica, shards)
            here = (shard, replica)
            there = (reversed_bits(place, shards), group * shards + reversed_bits(shard, shards))
            if source is None:
                route += [(flat(s, *here), flat(s, *there)) for s in range(2)]
            else:
                route.append((flat(source, *here), flat(target, *there)))
    return lax.ppermute(block, AXES, route)


def in_order(pieces, quarter):
    odd, high = (quarter & 1) == 1, (quarter & 2) == 2
    a, b, c, d = pieces
    a, b, c, d = jnp.where(odd, b, a), jnp.where(odd, a, b), jnp.where(odd, d, c), jnp.where(odd, c, d)
    return jnp.where(high, c, a), jnp.where(high, d, b), jnp.where(high, a, c), jnp.where(high, b, d)


def after(value, *others):
    return lax.optimization_barrier((value, others))[0]


def spread(piece, far):
    return piece, across(piece, 1), far, across(far, 1)


def low_sum(*parts):
    total = parts[0].astype(F32)
    for part in parts[1:]:
        total = total + part.astype(F32)
    return total.astype(BF16)


def body(edges, attn_in, attn_out, mlp_up, mlp_down, vectors, key_mask):
    section = lax.axis_index("section")
    first = section == 0
    replica = lax.axis_index("replica")
    shards, replicas = lax.axis_size("shard"), lax.axis_size("replica")
    quarter = replica % QUARTERS
    edges_here = edges[0]
    clips, frames, width = edges_here.shape
    hidden = mlp_up.shape[2]
    dim = width // H
    heads = H // QUARTERS
    wide = heads * dim
    unit = hidden // (shards * QUARTERS)
    rows = attn_in.shape[1]
    assert clips == 2 and lax.axis_size("section") == 2 and replicas % shards == 0 and replicas % QUARTERS == 0

    def by_layer(own, other):
        return jnp.where(first, own, other), jnp.where(first, other, own)

    vec_by_layer = by_layer(vectors[0], swap_sections(vectors[0]))
    mask_row = transposed(
        lax.dynamic_index_in_dim(key_mask, section, 0, keepdims=False).astype(F32)[None], None, None
    )[0]
    inputs = jnp.where(first, transposed(edges_here[0], 0, 0), transposed(edges_here[1], 0, 1))

    def pick(block, axis):
        return lax.dynamic_index_in_dim(block, quarter, axis, keepdims=False)

    def gathered(block):
        return lax.all_gather(block, "shard", axis=0, tiled=True)

    query_in, key_in, value_in = (
        pick(attn_in[0][:, i * width:(i + 1) * width].reshape(rows, QUARTERS, wide), 1) for i in range(3)
    )
    own_proj = jnp.concatenate(
        [key_in, value_in, query_in, pick(attn_out[0].reshape(rows, QUARTERS, width // QUARTERS), 1)], 1
    )
    own_up = pick(mlp_up[0].reshape(rows, shards, QUARTERS, unit), 2).reshape(rows, shards * unit)
    own_down = pick(mlp_down[0].reshape(QUARTERS, unit, width), 0)
    proj_zero, proj_one = by_layer(own_proj, swap_sections(own_proj))
    proj_zero = gathered(proj_zero)
    own_up = after(own_up, inputs)
    own_down = after(own_down, own_up)
    proj_one = after(proj_one, own_down)
    own_up, own_down, proj_one = gathered(own_up), gathered(own_down), gathered(proj_one)
    other_up = swap_sections(own_up)

    def head_weights(block):
        pieces = spread(block, across(block, 2))
        return pieces, jnp.concatenate(in_order([piece[:, 3 * wide:] for piece in pieces], quarter), 1)

    heads_by_layer = [head_weights(proj_zero), None]
    hidden_by_layer = [None, None]

    members = [0]
    bit = 2
    while bit < shards:
        members = members + [m ^ bit for m in members]
        bit *= 2
    members = members + [m ^ 1 for m in members]
    place = replica % shards
    bias_row = jnp.concatenate(
        [lax.dynamic_slice_in_dim(mask_row, reversed_bits(place ^ m, shards) * frames, frames, 0) for m in members]
    )
    bias_row = jnp.where(bias_row > 0, 0.0, MASKED).astype(BF16)
    lane = jnp.arange(dim)[None, :]
    key_bias = jnp.where(lane == 0, bias_row[:, None], jnp.zeros((), BF16))

    def chips_rows(block):
        bit = 2
        while bit < shards:
            block = jnp.concatenate([block, across(block, bit)], 0)
            bit *= 2
        return block

    def forward(x_low, layer):
        vec = vec_by_layer[layer]
        x_set = chips_rows(x_low)
        proj, w_out = heads_by_layer[layer]
        normed = layer_norm(x_set.astype(F32), vec[0], vec[1]).astype(BF16)
        zeros = jnp.zeros((QUARTERS, wide), F32)
        bias_in = jnp.stack([zeros, vec[3].reshape(QUARTERS, wide), vec[2].reshape(QUARTERS, wide)], 1)
        own_qkv, other_kv = {}, {}
        order = (0, 1, 2, 3)
        for p in order:
            bias = lax.dynamic_index_in_dim(bias_in, quarter ^ p, 0, keepdims=False).reshape(3 * wide)
            own_qkv[p] = (dot(normed, proj[p][:, :3 * wide]) + bias).astype(BF16)
            other_kv[p ^ 1] = across(own_qkv[p][:, :2 * wide], 1)
        outs, weights, inverses = {}, {}, {}
        late = {}
        for step, p in enumerate(order):
            own = own_qkv[p]
            if layer == 0 and step == 3:
                own = after(own, proj_one)
            outs[p], weights[p], inverses[p] = attend(own, other_kv[p], key_bias, heads, frames)
            if layer == 0 and step == 0:
                late["up"] = by_layer(own_up, after(other_up, outs[p]))
                late["up_far"] = across(late["up"][0], 2)
                other_down = swap_sections(after(own_down, outs[p]))
            elif layer == 0 and step == 2:
                late["down"] = by_layer(own_down, after(other_down, outs[p]))
                late["down_far"] = across(late["down"][0], 2)
                w_up = spread(late["up"][0], after(late["up_far"], outs[p]))
                late["one_far"] = across(after(proj_one, outs[p]), 2)
            elif layer == 0 and step == 3:
                w_down = spread(late["down"][0], after(late["down_far"], outs[p]))
                hidden_by_layer[0] = (w_up, w_down)
            elif layer == 1 and step == 0:
                late["down_far"] = across(after(pending_one["down"], outs[p]), 2)
            elif layer == 1 and step == 1:
                cot = after(edges_here, outs[p])
                pending_one["cot"] = [transposed(cot[0], 1, 0), transposed(cot[1], 1, 1)]
                w_up = spread(pending_one["up"], after(pending_one["up_far"], outs[p]))
            elif layer == 1 and step == 3:
                w_down = spread(pending_one["down"], after(late["down_far"], outs[p]))
                hidden_by_layer[1] = (w_up, w_down)
        attended, middle, normed_two = out_part(quarter, [outs[p] for p in range(QUARTERS)], w_out, x_low, vec)
        w_up, w_down = hidden_by_layer[layer]
        bias_up = vec[8:].reshape(shards, QUARTERS, unit)
        acts, slopes = [], []
        result = middle + vec[7]
        for p in range(QUARTERS):
            bias = lax.dynamic_index_in_dim(bias_up, quarter ^ p, 1, keepdims=False).reshape(1, shards * unit)
            if layer == 0 and p == QUARTERS - 1:
                result = after(result, late["one_far"])
            act, slope, result = mlp_part(normed_two, w_up[p], bias, w_down[p], result)
            acts.append(act)
            slopes.append(slope)
            if layer == 0 and p == 0:
                far = after(late["one_far"], act)
                pieces = spread(proj_one, far)
                w_out_one = jnp.concatenate(in_order([piece[:, 3 * wide:] for piece in pieces], quarter), 1)
                heads_by_layer[1] = (pieces, w_out_one)
                pending_one["up"], pending_one["down"] = late["up"][1], late["down"][1]
                pending_one["up_far"] = across(after(pending_one["up"], far), 2)
        kept = (x_low, normed, own_qkv, other_kv, weights, inverses, attended, middle, normed_two, acts, slopes)
        return result.astype(BF16), kept

    pending_one = {}

    def scattered(block):
        bit = QUARTERS
        while bit < replicas:
            block = low_sum(block, across(block, bit))
            bit *= 2
        return lax.psum_scatter(block, "shard", scatter_dimension=0, tiled=True)

    def half_sum(block):
        cut = block.shape[1] // 2
        left, right = block[:, :cut], block[:, cut:]
        return low_sum(jnp.where(first, left, right), swap_sections(jnp.where(first, right, left)))

    def backward(cot, layer, kept, above):
        (proj, w_out), (w_up, w_down), vec = heads_by_layer[layer], hidden_by_layer[layer], vec_by_layer[layer]
        x_low, normed, own_qkv, other_kv, weights, inverses, attended, middle, normed_two, acts, slopes = kept
        order = (3, 1, 2, 0)
        g_down, g_up, up_sums, near_down, near_up = {}, {}, {}, {}, {}
        d_normed_two = jnp.zeros((frames, width), F32)
        for step, p in enumerate(order):
            g_down[p], g_up[p], up_sums[p], d_normed_two = mlp_back_part(
                cot, normed_two, acts[p], slopes[p], w_up[p], w_down[p], d_normed_two
            )
            if p & 1:
                near_down[p ^ 1] = across(g_down[p], 1)
                near_up[p ^ 1] = across(g_up[p], 1)
            if above is not None and step == 1:
                halves = [after(half, g_up[p]) for half in above["halves"]]
                above["mlp"] = scattered(jnp.concatenate(halves, 1))
        d_middle, mid_rows, d_heads, d_attn_parts = middle_back(quarter, d_normed_two, middle, cot, vec, w_out)
        if above is not None:
            far = after(above["far_proj"], mid_rows)
            above["half"] = half_sum(above["finish"](far))
        far_down = low_sum(g_down[2], after(near_down[2], mid_rows))
        results = {}
        for step, p in enumerate(order):
            head = d_heads[p]
            if step == 1:
                head = after(head, far_down)
                far_down = across(far_down, 2)
            elif step == 2:
                head = after(head, far_up)
                far_up = across(far_up, 2)
                if above is not None:
                    half = after(above["half"], results[order[1]][0])
                    above["proj"] = scattered(jnp.concatenate([half, above["vec"]], 1))
            elif step == 3 and above is not None:
                head = after(head, above["mlp"])
            results[p] = attend_back(own_qkv[p], other_kv[p], weights[p], inverses[p], head, heads, frames)
            if step == 0:
                far_up = low_sum(g_up[2], after(near_up[2], results[p][0]))
        last = results[order[3]][0]
        from_other = {p: across(results[p ^ 1][2], 1) for p in range(QUARTERS)}
        half_down = half_sum(low_sum(g_down[0], near_down[0], after(far_down, last)))
        g_proj, sums_in, near_proj = {}, {}, {}
        d_normed = jnp.zeros(normed.shape, F32)
        for p in order:
            g_proj[p], sums_in[p], d_normed = proj_back(
                normed, results[p][1], from_other[p], results[p][0], attended, d_attn_parts[p], proj[p], d_normed
            )
            if p & 1:
                near_proj[p ^ 1] = across(g_proj[p], 1)
        block = d_normed
        bit = shards // 2
        while bit >= 2:
            cut = block.shape[0] // 2
            block = block[:cut] + across(block[cut:].astype(BF16), bit).astype(F32)
            bit //= 2
        half_up = half_sum(low_sum(g_up[0], near_up[0], after(far_up, d_normed)))
        if layer == 1:
            far_proj = low_sum(g_proj[2], after(near_proj[2], block))
        else:
            far_proj = low_sum(g_proj[2], after(near_proj[2], d_normed))
        back, g_gain_one, g_shift_one = norm_back(x_low.astype(F32), vec[0], block)
        g_low = (d_middle + back).astype(BF16)
        g_low = after(g_low, far_proj)
        far_proj = across(far_proj, 2)
        vec_block = vector_block(
            quarter, [sums_in[p] for p in range(QUARTERS)], [up_sums[p] for p in range(QUARTERS)],
            g_gain_one, g_shift_one, mid_rows, shards,
        )
        if above is not None:
            g_low = after(g_low, above["proj"])

        def finish_proj(other):
            return low_sum(g_proj[0], near_proj[0], other)

        return g_low, {"halves": [half_down, half_up], "far_proj": far_proj, "finish": finish_proj, "vec": vec_block}

    x_one, kept_zero = forward(inputs, 0)
    y_one, kept_one = forward(x_one, 1)
    cot = [after(part, y_one) for part in pending_one["cot"]]
    g_one, one = backward(jnp.where(first, cot[0], cot[1]), 1, kept_one, None)
    g_zero, zero = backward(g_one, 0, kept_zero, one)
    y_one = after(y_one, g_one)
    out_slots = [transposed(y_one, 0, 1), transposed(y_one, 1, 1)]
    g_zero = after(g_zero, *out_slots)
    back_slots = [transposed(g_zero, 0, 0), transposed(g_zero, 1, 0)]
    edges_out = jnp.stack([jnp.where(first, b, o) for b, o in zip(back_slots, out_slots)])
    mlp_one, proj_one = one["mlp"], one["proj"]
    mlp_zero = scattered(jnp.concatenate([after(half, g_zero) for half in zero["halves"]], 1))
    far = after(zero["far_proj"], g_zero)
    proj_zero = jnp.concatenate([half_sum(zero["finish"](far)), zero["vec"]], 1)
    proj_zero = scattered(after(proj_zero, *back_slots))

    def exchanged(zero, one):
        return jnp.where(first, zero, one), swap_sections(jnp.where(first, one, zero))

    def joined(own, other):
        cut = width // 2
        parts = []
        for start in range(0, own.shape[1], cut):
            a, b = own[:, start:start + cut], other[:, start:start + cut]
            parts += [jnp.where(first, a, b), jnp.where(first, b, a)]
        return parts

    part = jnp.concatenate(joined(*exchanged(mlp_zero, mlp_one)), 1)
    far = across(part, 2)
    f_down, f_up = placed_parts(
        functools.partial(place_mlp_kernel, shards=shards), quarter, spread(part, far),
        [mlp_down.shape[1:], mlp_up.shape[1:]],
    )
    proj_zero = after(proj_zero, far)
    own, other = exchanged(proj_zero, proj_one)
    cut = width // 2
    part = jnp.concatenate(
        joined(own[:, :cut], other[:, :cut]) + [low_sum(own[:, cut:], other[:, cut:])], 1
    )
    f_in, f_out, f_vec = placed_parts(
        place_proj_kernel, quarter, spread(part, across(part, 2)),
        [attn_in.shape[1:], attn_out.shape[1:], (128, rows)],
    )
    f_vec = f_vec[:vectors.shape[1]]
    return edges_out[None], f_in[None], f_out[None], f_up[None], f_down[None], f_vec[None]


def solution(mesh):
    placed = (
        P("section", "replica", "shard", None),
        P("section", "shard", None),
        P("section", "shard", None),
        P("section", "shard", None),
        P("section", "shard", None),
        P("section", None, None),
        P("replica", None),
    )
    return jax.shard_map(
        body,
        mesh=mesh,
        in_specs=placed,
        out_specs=(
            P("section", "replica", "shard", None),
            P("section", "shard", None),
            P("section", "shard", None),
            P("section", "shard", None),
            P("section", "shard", None),
            P("section", None, "shard"),
        ),
        check_vma=False,
    )
```

```python
import functools
import math

import jax
import jax.numpy as jnp
from jax import lax
from jax.experimental import pallas as pl
from jax.experimental.pallas import tpu as pltpu
from jax.sharding import PartitionSpec as P

H = 12
EPS = 1e-05
MASKED = -1e30
QUARTERS = 4
ATTEND_VMEM = 58 * 2**20
BF16 = jnp.bfloat16
F32 = jnp.float32
AXES = ("section", "shard", "replica")
NN = (((1,), (0,)), ((), ()))
NT = (((1,), (1,)), ((), ()))
TN = (((0,), (0,)), ((), ()))


def dot(a, b, dims=NN):
    return lax.dot_general(a, b, dims, preferred_element_type=F32)


def layer_norm(values, gain, shift):
    center = values - jnp.mean(values, -1, keepdims=True)
    spread = jnp.mean(center * center, -1, keepdims=True)
    return center * lax.rsqrt(spread + EPS) * gain + shift


def key_chunks(sources, size):
    chunks, base = [], 0
    for source in range(len(sources)):
        rows = sources[source].shape[0]
        for start in range(0, rows, size):
            chunks.append((source, start, base + start))
        base += rows
    return chunks


def attend_kernel(own_ref, other_ref, bias_ref, out_ref, exp_ref, inv_ref, score_ref, *, heads, frames, chunk):
    dim = own_ref.shape[1] // (3 * heads)
    wide = heads * dim
    sources = (own_ref, other_ref)
    chunks = key_chunks(sources, chunk)

    def one_head(head):
        at = head * dim
        query = own_ref[0:frames, 2 * wide + at:2 * wide + at + dim] * (dim ** -0.5)
        lane = lax.broadcasted_iota(jnp.int32, (frames, dim), 1)
        query = jnp.concatenate([query.astype(BF16), (lane == 0).astype(BF16)], 1)
        top = None
        for source, start, row in chunks:
            key = sources[source][start:start + chunk, at:at + dim]
            key = jnp.concatenate([key, bias_ref[row:row + chunk, :]], 1)
            score = dot(key, query, NT)
            score_ref[row:row + chunk, :] = score
            part = jnp.max(score, 0, keepdims=True)
            top = part if top is None else jnp.maximum(top, part)
        total = None
        for source, start, row in chunks:
            weight = jnp.exp(score_ref[row:row + chunk, :] - top).astype(BF16)
            exp_ref[0, row:row + chunk, :] = weight
            value = sources[source][start:start + chunk, wide + at:wide + at + dim]
            value = jnp.concatenate([value, jnp.ones_like(value)], 1)
            part = dot(value, weight, TN)
            total = part if total is None else total + part
        inverse = 1.0 / total[dim:dim + 1, :]
        inv_ref[head:head + 1, :] = inverse
        out_ref[:, at:at + dim] = (total[0:dim, :] * inverse).T.astype(BF16)

    for head in range(heads):
        pl.when(pl.program_id(0) == head)(functools.partial(one_head, head))


def whole_block(shape):
    return pl.BlockSpec(shape, lambda i: (0,) * len(shape))


def chunk_size(own, frames):
    chunk = min(256, frames)
    return frames if own.shape[0] % chunk else chunk


def attend(own, other, bias, heads, frames):
    keys = own.shape[0] + other.shape[0]
    wide = own.shape[1] // 3
    return pl.pallas_call(
        functools.partial(attend_kernel, heads=heads, frames=frames, chunk=chunk_size(own, frames)),
        grid=(heads,),
        in_specs=[whole_block(own.shape), whole_block(other.shape), whole_block(bias.shape)],
        out_specs=[
            whole_block((frames, wide)),
            pl.BlockSpec((1, keys, frames), lambda i: (i, 0, 0)),
            whole_block((heads, frames)),
        ],
        out_shape=(
            jax.ShapeDtypeStruct((frames, wide), BF16),
            jax.ShapeDtypeStruct((heads, keys, frames), BF16),
            jax.ShapeDtypeStruct((heads, frames), F32),
        ),
        scratch_shapes=[pltpu.VMEM((keys, frames), F32)],
        compiler_params=pltpu.CompilerParams(vmem_limit_bytes=ATTEND_VMEM),
        cost_estimate=pl.CostEstimate(
            flops=16 * keys * frames * wide, bytes_accessed=2 * heads * keys * frames, transcendentals=heads * keys * frames
        ),
        name="attend",
    )(own, other, bias)


def attend_back_kernel(own_ref, other_ref, exp_ref, inv_ref, dout_ref, dq_ref, down_ref, dother_ref, prod_ref, *, heads, frames, chunk):
    dim = own_ref.shape[1] // (3 * heads)
    wide = heads * dim
    scale = dim ** -0.5
    sources = (own_ref, other_ref)
    targets = (down_ref, dother_ref)
    chunks = key_chunks(sources, chunk)

    def one_head(head):
        at = head * dim
        query = (own_ref[0:frames, 2 * wide + at:2 * wide + at + dim] * scale).astype(BF16)
        inverse = inv_ref[head:head + 1, :]
        dout_t = dout_ref[:, at:at + dim].astype(F32).T * inverse
        dout = dout_t.T.astype(BF16)
        dout_t = dout_t.astype(BF16)
        delta = None
        for source, start, row in chunks:
            value = sources[source][start:start + chunk, wide + at:wide + at + dim]
            weight = exp_ref[0, row:row + chunk, :]
            prod = dot(value, dout_t) * weight.astype(F32)
            prod_ref[row:row + chunk, :] = prod
            part = jnp.sum(prod, 0, keepdims=True)
            delta = part if delta is None else delta + part
            targets[source][start:start + chunk, wide + at:wide + at + dim] = dot(weight, dout).astype(BF16)
        delta = delta * inverse
        dq_t = None
        for source, start, row in chunks:
            key = sources[source][start:start + chunk, at:at + dim]
            weight = exp_ref[0, row:row + chunk, :].astype(F32)
            ds = (prod_ref[row:row + chunk, :] - weight * delta).astype(BF16)
            targets[source][start:start + chunk, at:at + dim] = dot(ds, query).astype(BF16)
            part = dot(key, ds, TN)
            dq_t = part if dq_t is None else dq_t + part
        dq_ref[:, at:at + dim] = (dq_t.T * scale).astype(BF16)

    for head in range(heads):
        pl.when(pl.program_id(0) == head)(functools.partial(one_head, head))


def attend_back(own, other, weights, inverse, dout, heads, frames):
    keys = own.shape[0] + other.shape[0]
    wide = own.shape[1] // 3
    results = ((frames, wide), (own.shape[0], 2 * wide), (other.shape[0], 2 * wide))
    return pl.pallas_call(
        functools.partial(attend_back_kernel, heads=heads, frames=frames, chunk=chunk_size(own, frames)),
        grid=(heads,),
        in_specs=[
            whole_block(own.shape), whole_block(other.shape),
            pl.BlockSpec((1, keys, frames), lambda i: (i, 0, 0)),
            whole_block(inverse.shape), whole_block(dout.shape),
        ],
        out_specs=[whole_block(shape) for shape in results],
        out_shape=[jax.ShapeDtypeStruct(shape, BF16) for shape in results],
        scratch_shapes=[pltpu.VMEM((keys, frames), F32)],
        compiler_params=pltpu.CompilerParams(vmem_limit_bytes=ATTEND_VMEM),
        cost_estimate=pl.CostEstimate(
            flops=32 * keys * frames * wide, bytes_accessed=2 * heads * keys * frames, transcendentals=0
        ),
        name="attend_back",
    )(own, other, weights, inverse, dout)


def out_kernel(quarter_ref, a_ref, b_ref, c_ref, d_ref, weight_ref, x_ref, vec_ref, att_ref, mid_ref, norm_ref):
    parts = [ref[...] for ref in (a_ref, b_ref, c_ref, d_ref)]
    attended = jnp.concatenate(in_order(parts, quarter_ref[0]), 1)
    att_ref[...] = attended
    middle = x_ref[...].astype(F32) + dot(attended, weight_ref[...]) + vec_ref[4:5, :]
    mid_ref[...] = middle
    norm_ref[...] = layer_norm(middle, vec_ref[5:6, :], vec_ref[6:7, :]).astype(BF16)


def scalar_first(count):
    return [pl.BlockSpec(memory_space=pltpu.SMEM)] + [pl.BlockSpec(memory_space=pltpu.VMEM)] * count


def out_part(quarter, outs, weight, x_low, vec):
    shape = x_low.shape
    return pl.pallas_call(
        out_kernel,
        in_specs=scalar_first(7),
        out_shape=[jax.ShapeDtypeStruct(shape, kind) for kind in (BF16, F32, BF16)],
        compiler_params=pltpu.CompilerParams(vmem_limit_bytes=32 * 2**20),
        cost_estimate=pl.CostEstimate(
            flops=2 * math.prod(shape) * shape[1], bytes_accessed=14 * math.prod(shape), transcendentals=0
        ),
        name="out_part",
    )(quarter.reshape(1), *outs, weight, x_low, vec)


def norm_back(values, gain, grad):
    center = values - jnp.mean(values, -1, keepdims=True)
    inv = lax.rsqrt(jnp.mean(center * center, -1, keepdims=True) + EPS)
    unit_values = center * inv
    scaled = grad * gain
    back = inv * (
        scaled - jnp.mean(scaled, -1, keepdims=True)
        - unit_values * jnp.mean(scaled * unit_values, -1, keepdims=True)
    )
    return back, jnp.sum(grad * unit_values, 0, keepdims=True), jnp.sum(grad, 0, keepdims=True)


def middle_back_kernel(quarter_ref, grad_ref, mid_ref, cot_ref, vec_ref, weight_ref, dmid_ref, rows_ref, *part_refs):
    cot = cot_ref[...].astype(F32)
    back, gain, shift = norm_back(mid_ref[...], vec_ref[5:6, :], grad_ref[...])
    d_middle = cot + back
    dmid_ref[...] = d_middle
    d_attn = d_middle.astype(BF16)
    d_low = d_attn.astype(F32)
    rows_ref[...] = jnp.concatenate(
        [gain, shift, jnp.sum(d_low, 0, keepdims=True), jnp.sum(cot, 0, keepdims=True)], 0
    )
    d_attended = dot(d_attn, weight_ref[...], NT).astype(BF16)
    for refs, whole in ((part_refs[:QUARTERS], d_attended), (part_refs[QUARTERS:], d_attn)):
        wide = whole.shape[1] // QUARTERS
        parts = in_order([whole[:, p * wide:(p + 1) * wide] for p in range(QUARTERS)], quarter_ref[0])
        for ref, part in zip(refs, parts):
            ref[...] = part


def middle_back(quarter, grad, middle, cot, vec, weight):
    frames, width = middle.shape
    part = jax.ShapeDtypeStruct((frames, width // QUARTERS), BF16)
    results = pl.pallas_call(
        middle_back_kernel,
        in_specs=scalar_first(5),
        out_shape=[jax.ShapeDtypeStruct((frames, width), F32), jax.ShapeDtypeStruct((4, width), F32)]
        + [part] * (2 * QUARTERS),
        compiler_params=pltpu.CompilerParams(vmem_limit_bytes=32 * 2**20),
        cost_estimate=pl.CostEstimate(
            flops=2 * frames * width * width, bytes_accessed=18 * frames * width, transcendentals=0
        ),
        name="middle_back",
    )(quarter.reshape(1), grad, middle, cot, vec, weight)
    return results[0], results[1], results[2:2 + QUARTERS], results[2 + QUARTERS:]


def vector_kernel(quarter_ref, *refs, shards):
    ins, up_ins = refs[:QUARTERS], refs[QUARTERS:2 * QUARTERS]
    gain_ref, shift_ref, mid_ref, out_ref = refs[2 * QUARTERS:]
    width = out_ref.shape[0]
    wide, unit = width // QUARTERS, width // shards
    ins = in_order([ref[...] for ref in ins], quarter_ref[0])
    value_row, query_row = (
        jnp.concatenate([piece[:, i * wide:(i + 1) * wide] for piece in ins], 1) for i in range(1, 3)
    )
    ups = in_order([ref[...] for ref in up_ins], quarter_ref[0])
    up_row = jnp.concatenate(
        [piece[:, shard * unit:(shard + 1) * unit] for shard in range(shards) for piece in ups], 1
    )
    rows = [gain_ref[...], shift_ref[...], query_row, value_row, mid_ref[2:3, :], mid_ref[0:2, :], mid_ref[3:4, :]]
    rows += [up_row[:, start:start + width] for start in range(0, up_row.shape[1], width)]
    rows = jnp.concatenate(rows, 0)
    rows = jnp.concatenate([rows, jnp.zeros((128 - rows.shape[0], width), F32)], 0)
    out_ref[...] = rows.T.astype(BF16)


def vector_block(quarter, sums_in, up_sums, gain, shift, mid_rows, shards):
    width = gain.shape[1]
    return pl.pallas_call(
        functools.partial(vector_kernel, shards=shards),
        in_specs=scalar_first(2 * QUARTERS + 3),
        out_shape=jax.ShapeDtypeStruct((width, 128), BF16),
        compiler_params=pltpu.CompilerParams(vmem_limit_bytes=32 * 2**20),
        cost_estimate=pl.CostEstimate(flops=128 * width, bytes_accessed=512 * width, transcendentals=0),
        name="vector_block",
    )(quarter.reshape(1), *sums_in, *up_sums, gain, shift, mid_rows)


def column_tile(columns):
    return 256 if columns % 256 == 0 else columns


def mlp_kernel(in_ref, up_ref, bias_ref, down_ref, before_ref, act_ref, slope_ref, sum_ref):
    up = dot(in_ref[...], up_ref[...]) + bias_ref[...]
    cdf = 0.5 + 0.5 * lax.erf(up * (0.5 ** 0.5))
    pdf = jnp.exp(-0.5 * up * up) * 0.3989422804014327
    act = (up * cdf).astype(BF16)
    act_ref[...] = act
    slope_ref[...] = (cdf + up * pdf).astype(BF16)
    part = dot(act, down_ref[...])

    @pl.when(pl.program_id(0) == 0)
    def _():
        sum_ref[...] = before_ref[...] + part

    @pl.when(pl.program_id(0) > 0)
    def _():
        sum_ref[...] += part


def mlp_part(values, up, bias, down, before):
    rows, depth = values.shape
    columns = up.shape[1]
    tile = column_tile(columns)
    whole = pl.BlockSpec((rows, depth), lambda i: (0, 0))
    hidden = pl.BlockSpec((rows, tile), lambda i: (0, i))
    return pl.pallas_call(
        mlp_kernel,
        grid=(columns // tile,),
        in_specs=[
            whole,
            pl.BlockSpec((depth, tile), lambda i: (0, i)),
            pl.BlockSpec((1, tile), lambda i: (0, i)),
            pl.BlockSpec((tile, depth), lambda i: (i, 0)),
            whole,
        ],
        out_specs=[hidden, hidden, whole],
        out_shape=[
            jax.ShapeDtypeStruct((rows, columns), BF16),
            jax.ShapeDtypeStruct((rows, columns), BF16),
            jax.ShapeDtypeStruct((rows, depth), F32),
        ],
        compiler_params=pltpu.CompilerParams(vmem_limit_bytes=32 * 2**20),
        cost_estimate=pl.CostEstimate(
            flops=4 * rows * depth * columns, bytes_accessed=4 * (3 * rows * depth + depth * columns + rows * columns),
            transcendentals=2 * rows * columns,
        ),
        name="mlp_part",
    )(values, up, bias, down, before)


def mlp_back_kernel(grad_ref, in_ref, act_ref, slope_ref, up_ref, down_ref, before_ref, gd_ref, gu_ref, row_ref, sum_ref):
    grad = grad_ref[...]
    d_up = (dot(grad, down_ref[...], NT) * slope_ref[...].astype(F32)).astype(BF16)
    gd_ref[...] = dot(act_ref[...], grad, TN).astype(BF16)
    gu_ref[...] = dot(in_ref[...], d_up, TN).astype(BF16)
    row_ref[...] = jnp.sum(d_up.astype(F32), 0, keepdims=True)
    part = dot(d_up, up_ref[...], NT)

    @pl.when(pl.program_id(0) == 0)
    def _():
        sum_ref[...] = before_ref[...] + part

    @pl.when(pl.program_id(0) > 0)
    def _():
        sum_ref[...] += part


def mlp_back_part(grad, values, act, slope, up, down, before):
    rows, depth = values.shape
    columns = up.shape[1]
    tile = column_tile(columns)
    whole = pl.BlockSpec((rows, depth), lambda i: (0, 0))
    hidden = pl.BlockSpec((rows, tile), lambda i: (0, i))
    up_tile = pl.BlockSpec((depth, tile), lambda i: (0, i))
    down_tile = pl.BlockSpec((tile, depth), lambda i: (i, 0))
    return pl.pallas_call(
        mlp_back_kernel,
        grid=(columns // tile,),
        in_specs=[whole, whole, hidden, hidden, up_tile, down_tile, whole],
        out_specs=[down_tile, up_tile, pl.BlockSpec((1, tile), lambda i: (0, i)), whole],
        out_shape=[
            jax.ShapeDtypeStruct((columns, depth), BF16),
            jax.ShapeDtypeStruct((depth, columns), BF16),
            jax.ShapeDtypeStruct((1, columns), F32),
            jax.ShapeDtypeStruct((rows, depth), F32),
        ],
        compiler_params=pltpu.CompilerParams(vmem_limit_bytes=40 * 2**20),
        cost_estimate=pl.CostEstimate(
            flops=8 * rows * depth * columns, bytes_accessed=4 * (3 * rows * depth + 2 * depth * columns + rows * columns),
            transcendentals=0,
        ),
        name="mlp_back_part",
    )(grad, values, act, slope, up, down, before)


def proj_back_kernel(in_ref, own_ref, other_ref, query_ref, out_ref, grad_ref, weight_ref, before_ref, g_ref, row_ref, sum_ref):
    frames, wide = query_ref.shape
    both = (own_ref[...].astype(F32) + other_ref[...].astype(F32)).astype(BF16)
    query = query_ref[...]
    values = in_ref[...]
    g_ref[...] = jnp.concatenate(
        [dot(values, both, TN), dot(values[:frames], query, TN), dot(out_ref[...], grad_ref[...], TN)], 1
    ).astype(BF16)
    row_ref[...] = jnp.concatenate(
        [jnp.sum(both.astype(F32), 0, keepdims=True), jnp.sum(query.astype(F32), 0, keepdims=True)], 1
    )
    total = before_ref[...] + dot(both, weight_ref[:, :2 * wide], NT)
    own = total[:frames] + dot(query, weight_ref[:, 2 * wide:3 * wide], NT)
    sum_ref[0:frames, :] = own
    sum_ref[frames:, :] = total[frames:]


def proj_back(values, own, other, query, out, grad, weight, before):
    rows, depth = values.shape
    wide = query.shape[1]
    return pl.pallas_call(
        proj_back_kernel,
        out_shape=[
            jax.ShapeDtypeStruct(weight.shape, BF16),
            jax.ShapeDtypeStruct((1, 3 * wide), F32),
            jax.ShapeDtypeStruct((rows, depth), F32),
        ],
        compiler_params=pltpu.CompilerParams(vmem_limit_bytes=40 * 2**20),
        cost_estimate=pl.CostEstimate(
            flops=8 * rows * depth * 2 * wide, bytes_accessed=12 * rows * depth + 4 * depth * weight.shape[1],
            transcendentals=0,
        ),
        name="proj_back",
    )(values, own, other, query, out, grad, weight, before)


def place_proj_kernel(quarter_ref, a_ref, b_ref, c_ref, d_ref, qkv_ref, out_ref, vec_ref):
    pieces = [ref[...].astype(F32) for ref in (a_ref, b_ref, c_ref, d_ref)]
    width = out_ref.shape[1]
    wide = width // QUARTERS
    total = pieces[0][:, width:] + pieces[1][:, width:] + pieces[2][:, width:] + pieces[3][:, width:]
    vec_ref[...] = total.T
    pieces = in_order([piece[:, :width] for piece in pieces], quarter_ref[0])
    for column, part in ((0, 2), (1, 0), (2, 1)):
        qkv_ref[:, column * width:(column + 1) * width] = jnp.concatenate(
            [piece[:, part * wide:(part + 1) * wide] for piece in pieces], 1
        )
    out_ref[...] = jnp.concatenate([piece[:, 3 * wide:] for piece in pieces], 1)


def place_mlp_kernel(quarter_ref, a_ref, b_ref, c_ref, d_ref, down_ref, up_ref, *, shards):
    pieces = in_order([ref[...].astype(F32) for ref in (a_ref, b_ref, c_ref, d_ref)], quarter_ref[0])
    rows, width = pieces[0].shape[0], pieces[0].shape[1] // 2
    unit = width // shards
    for place in range(QUARTERS):
        down_ref[place * rows:(place + 1) * rows, :] = pieces[place][:, :width]
    for shard in range(shards):
        start = width + shard * unit
        up_ref[:, shard * QUARTERS * unit:(shard + 1) * QUARTERS * unit] = jnp.concatenate(
            [piece[:, start:start + unit] for piece in pieces], 1
        )


def placed_parts(kernel, quarter, pieces, shapes):
    size = sum(math.prod(shape) for shape in shapes)
    return pl.pallas_call(
        kernel,
        in_specs=scalar_first(QUARTERS),
        out_shape=[jax.ShapeDtypeStruct(shape, F32) for shape in shapes],
        compiler_params=pltpu.CompilerParams(vmem_limit_bytes=32 * 2**20),
        cost_estimate=pl.CostEstimate(flops=size, bytes_accessed=6 * size, transcendentals=0),
        name="placed_parts",
    )(quarter.reshape(1), *pieces)


def across(block, bit):
    count = lax.axis_size("replica")
    return lax.ppermute(block, "replica", [(i, i ^ bit) for i in range(count)])


def swap_sections(block):
    return lax.ppermute(block, "section", [(0, 1), (1, 0)])


def reversed_bits(index, count):
    result, bit = index * 0, 1
    while bit < count:
        result = result * 2 + index // bit % 2
        bit *= 2
    return result


def transposed(block, source, target):
    shards, replicas = lax.axis_size("shard"), lax.axis_size("replica")

    def flat(section, shard, replica):
        return (section * shards + shard) * replicas + replica

    route = []
    for shard in range(shards):
        for replica in range(replicas):
            group, place = divmod(replica, shards)
            here = (shard, replica)
            there = (reversed_bits(place, shards), group * shards + reversed_bits(shard, shards))
            if source is None:
                route += [(flat(s, *here), flat(s, *there)) for s in range(2)]
            else:
                route.append((flat(source, *here), flat(target, *there)))
    return lax.ppermute(block, AXES, route)


def in_order(pieces, quarter):
    odd, high = (quarter & 1) == 1, (quarter & 2) == 2
    a, b, c, d = pieces
    a, b, c, d = jnp.where(odd, b, a), jnp.where(odd, a, b), jnp.where(odd, d, c), jnp.where(odd, c, d)
    return jnp.where(high, c, a), jnp.where(high, d, b), jnp.where(high, a, c), jnp.where(high, b, d)


def after(value, *others):
    return lax.optimization_barrier((value, others))[0]


def spread(piece, far):
    return piece, across(piece, 1), far, across(far, 1)


def low_sum(*parts):
    total = parts[0].astype(F32)
    for part in parts[1:]:
        total = total + part.astype(F32)
    return total.astype(BF16)


def body(edges, attn_in, attn_out, mlp_up, mlp_down, vectors, key_mask):
    section = lax.axis_index("section")
    first = section == 0
    replica = lax.axis_index("replica")
    shards, replicas = lax.axis_size("shard"), lax.axis_size("replica")
    quarter = replica % QUARTERS
    edges_here = edges[0]
    clips, frames, width = edges_here.shape
    hidden = mlp_up.shape[2]
    dim = width // H
    heads = H // QUARTERS
    wide = heads * dim
    unit = hidden // (shards * QUARTERS)
    rows = attn_in.shape[1]
    assert clips == 2 and lax.axis_size("section") == 2 and replicas % shards == 0 and replicas % QUARTERS == 0

    def by_layer(own, other):
        return jnp.where(first, own, other), jnp.where(first, other, own)

    vec_by_layer = by_layer(vectors[0], swap_sections(vectors[0]))
    mask_row = transposed(
        lax.dynamic_index_in_dim(key_mask, section, 0, keepdims=False).astype(F32)[None], None, None
    )[0]
    inputs = jnp.where(first, transposed(edges_here[0], 0, 0), transposed(edges_here[1], 0, 1))

    def pick(block, axis):
        return lax.dynamic_index_in_dim(block, quarter, axis, keepdims=False)

    def gathered(block):
        return lax.all_gather(block, "shard", axis=0, tiled=True)

    query_in, key_in, value_in = (
        pick(attn_in[0][:, i * width:(i + 1) * width].reshape(rows, QUARTERS, wide), 1) for i in range(3)
    )
    own_proj = jnp.concatenate(
        [key_in, value_in, query_in, pick(attn_out[0].reshape(rows, QUARTERS, width // QUARTERS), 1)], 1
    )
    own_up = pick(mlp_up[0].reshape(rows, shards, QUARTERS, unit), 2).reshape(rows, shards * unit)
    own_down = pick(mlp_down[0].reshape(QUARTERS, unit, width), 0)
    proj_zero, proj_one = by_layer(own_proj, swap_sections(own_proj))
    proj_zero = gathered(proj_zero)
    own_up = after(own_up, inputs)
    own_down = after(own_down, own_up)
    proj_one = after(proj_one, own_down)
    own_up, own_down, proj_one = gathered(own_up), gathered(own_down), gathered(proj_one)
    other_up = swap_sections(own_up)

    def head_weights(block):
        pieces = spread(block, across(block, 2))
        return pieces, jnp.concatenate(in_order([piece[:, 3 * wide:] for piece in pieces], quarter), 1)

    heads_by_layer = [head_weights(proj_zero), None]
    hidden_by_layer = [None, None]

    members = [0]
    bit = 2
    while bit < shards:
        members = members + [m ^ bit for m in members]
        bit *= 2
    members = members + [m ^ 1 for m in members]
    place = replica % shards
    bias_row = jnp.concatenate(
        [lax.dynamic_slice_in_dim(mask_row, reversed_bits(place ^ m, shards) * frames, frames, 0) for m in members]
    )
    bias_row = jnp.where(bias_row > 0, 0.0, MASKED).astype(BF16)
    lane = jnp.arange(dim)[None, :]
    key_bias = jnp.where(lane == 0, bias_row[:, None], jnp.zeros((), BF16))

    def chips_rows(block):
        bit = 2
        while bit < shards:
            block = jnp.concatenate([block, across(block, bit)], 0)
            bit *= 2
        return block

    def forward(x_low, layer):
        vec = vec_by_layer[layer]
        x_set = chips_rows(x_low)
        proj, w_out = heads_by_layer[layer]
        normed = layer_norm(x_set.astype(F32), vec[0], vec[1]).astype(BF16)
        zeros = jnp.zeros((QUARTERS, wide), F32)
        bias_in = jnp.stack([zeros, vec[3].reshape(QUARTERS, wide), vec[2].reshape(QUARTERS, wide)], 1)
        own_qkv, other_kv = {}, {}
        order = (0, 1, 2, 3)
        for p in order:
            bias = lax.dynamic_index_in_dim(bias_in, quarter ^ p, 0, keepdims=False).reshape(3 * wide)
            own_qkv[p] = (dot(normed, proj[p][:, :3 * wide]) + bias).astype(BF16)
            other_kv[p ^ 1] = across(own_qkv[p][:, :2 * wide], 1)
        outs, weights, inverses = {}, {}, {}
        late = {}
        for step, p in enumerate(order):
            own = own_qkv[p]
            if layer == 0 and step == 3:
                own = after(own, proj_one)
            outs[p], weights[p], inverses[p] = attend(own, other_kv[p], key_bias, heads, frames)
            if layer == 0 and step == 0:
                late["up"] = by_layer(own_up, after(other_up, outs[p]))
                late["up_far"] = across(late["up"][0], 2)
                other_down = swap_sections(after(own_down, outs[p]))
            elif layer == 0 and step == 2:
                late["down"] = by_layer(own_down, after(other_down, outs[p]))
                late["down_far"] = across(late["down"][0], 2)
                w_up = spread(late["up"][0], after(late["up_far"], outs[p]))
                late["one_far"] = across(after(proj_one, outs[p]), 2)
            elif layer == 0 and step == 3:
                w_down = spread(late["down"][0], after(late["down_far"], outs[p]))
                hidden_by_layer[0] = (w_up, w_down)
            elif layer == 1 and step == 0:
                late["down_far"] = across(after(pending_one["down"], outs[p]), 2)
            elif layer == 1 and step == 1:
                cot = after(edges_here, outs[p])
                pending_one["cot"] = [transposed(cot[0], 1, 0), transposed(cot[1], 1, 1)]
                w_up = spread(pending_one["up"], after(pending_one["up_far"], outs[p]))
            elif layer == 1 and step == 3:
                w_down = spread(pending_one["down"], after(late["down_far"], outs[p]))
                hidden_by_layer[1] = (w_up, w_down)
        attended, middle, normed_two = out_part(quarter, [outs[p] for p in range(QUARTERS)], w_out, x_low, vec)
        w_up, w_down = hidden_by_layer[layer]
        bias_up = vec[8:].reshape(shards, QUARTERS, unit)
        acts, slopes = [], []
        result = middle + vec[7]
        for p in range(QUARTERS):
            bias = lax.dynamic_index_in_dim(bias_up, quarter ^ p, 1, keepdims=False).reshape(1, shards * unit)
            if layer == 0 and p == QUARTERS - 1:
                result = after(result, late["one_far"])
            act, slope, result = mlp_part(normed_two, w_up[p], bias, w_down[p], result)
            acts.append(act)
            slopes.append(slope)
            if layer == 0 and p == 0:
                far = after(late["one_far"], act)
                pieces = spread(proj_one, far)
                w_out_one = jnp.concatenate(in_order([piece[:, 3 * wide:] for piece in pieces], quarter), 1)
                heads_by_layer[1] = (pieces, w_out_one)
                pending_one["up"], pending_one["down"] = late["up"][1], late["down"][1]
                pending_one["up_far"] = across(after(pending_one["up"], far), 2)
        kept = (x_low, normed, own_qkv, other_kv, weights, inverses, attended, middle, normed_two, acts, slopes)
        return result.astype(BF16), kept

    pending_one = {}

    def scattered(block):
        bit = QUARTERS
        while bit < replicas:
            block = low_sum(block, across(block, bit))
            bit *= 2
        return lax.psum_scatter(block, "shard", scatter_dimension=0, tiled=True)

    def half_sum(block):
        cut = block.shape[1] // 2
        left, right = block[:, :cut], block[:, cut:]
        return low_sum(jnp.where(first, left, right), swap_sections(jnp.where(first, right, left)))

    def backward(cot, layer, kept, above):
        (proj, w_out), (w_up, w_down), vec = heads_by_layer[layer], hidden_by_layer[layer], vec_by_layer[layer]
        x_low, normed, own_qkv, other_kv, weights, inverses, attended, middle, normed_two, acts, slopes = kept
        order = (3, 1, 2, 0)
        g_down, g_up, up_sums, near_down, near_up = {}, {}, {}, {}, {}
        d_normed_two = jnp.zeros((frames, width), F32)
        for step, p in enumerate(order):
            g_down[p], g_up[p], up_sums[p], d_normed_two = mlp_back_part(
                cot, normed_two, acts[p], slopes[p], w_up[p], w_down[p], d_normed_two
            )
            if p & 1:
                near_down[p ^ 1] = across(g_down[p], 1)
                near_up[p ^ 1] = across(g_up[p], 1)
            if above is not None and step == 1:
                halves = [after(half, g_up[p]) for half in above["halves"]]
                above["mlp"] = scattered(jnp.concatenate(halves, 1))
        d_middle, mid_rows, d_heads, d_attn_parts = middle_back(quarter, d_normed_two, middle, cot, vec, w_out)
        if above is not None:
            far = after(above["far_proj"], mid_rows)
            above["half"] = half_sum(above["finish"](far))
        far_down = low_sum(g_down[2], after(near_down[2], mid_rows))
        results = {}
        for step, p in enumerate(order):
            head = d_heads[p]
            if step == 1:
                head = after(head, far_down)
                far_down = across(far_down, 2)
            elif step == 2:
                head = after(head, far_up)
                far_up = across(far_up, 2)
                if above is not None:
                    half = after(above["half"], results[order[1]][0])
                    above["proj"] = scattered(jnp.concatenate([half, above["vec"]], 1))
            elif step == 3 and above is not None:
                head = after(head, above["mlp"], *above["slots"])
            results[p] = attend_back(own_qkv[p], other_kv[p], weights[p], inverses[p], head, heads, frames)
            if step == 0:
                far_up = low_sum(g_up[2], after(near_up[2], results[p][0]))
        last = results[order[3]][0]
        from_other = {p: across(results[p ^ 1][2], 1) for p in range(QUARTERS)}
        half_down = half_sum(low_sum(g_down[0], near_down[0], after(far_down, last)))
        g_proj, sums_in, near_proj = {}, {}, {}
        d_normed = jnp.zeros(normed.shape, F32)
        for p in order:
            g_proj[p], sums_in[p], d_normed = proj_back(
                normed, results[p][1], from_other[p], results[p][0], attended, d_attn_parts[p], proj[p], d_normed
            )
            if p & 1:
                near_proj[p ^ 1] = across(g_proj[p], 1)
        block = d_normed
        bit = shards // 2
        while bit >= 2:
            cut = block.shape[0] // 2
            block = block[:cut] + across(block[cut:].astype(BF16), bit).astype(F32)
            bit //= 2
        half_up = half_sum(low_sum(g_up[0], near_up[0], after(far_up, d_normed)))
        if layer == 1:
            far_proj = low_sum(g_proj[2], after(near_proj[2], block))
        else:
            far_proj = low_sum(g_proj[2], after(near_proj[2], d_normed))
        back, g_gain_one, g_shift_one = norm_back(x_low.astype(F32), vec[0], block)
        g_low = (d_middle + back).astype(BF16)
        g_low = after(g_low, far_proj)
        far_proj = across(far_proj, 2)
        vec_block = vector_block(
            quarter, [sums_in[p] for p in range(QUARTERS)], [up_sums[p] for p in range(QUARTERS)],
            g_gain_one, g_shift_one, mid_rows, shards,
        )
        if above is not None:
            g_low = after(g_low, above["proj"])

        def finish_proj(other):
            return low_sum(g_proj[0], near_proj[0], other)

        return g_low, {"halves": [half_down, half_up], "far_proj": far_proj, "finish": finish_proj, "vec": vec_block}

    x_one, kept_zero = forward(inputs, 0)
    y_one, kept_one = forward(x_one, 1)
    cot = [after(part, y_one) for part in pending_one["cot"]]
    g_one, one = backward(jnp.where(first, cot[0], cot[1]), 1, kept_one, None)
    y_one = after(y_one, g_one)
    out_slots = [transposed(y_one, 0, 1), transposed(y_one, 1, 1)]
    one["slots"] = out_slots
    g_zero, zero = backward(g_one, 0, kept_zero, one)
    back_slots = [transposed(g_zero, 0, 0), transposed(g_zero, 1, 0)]
    edges_out = jnp.stack([jnp.where(first, b, o) for b, o in zip(back_slots, out_slots)])
    mlp_one, proj_one = one["mlp"], one["proj"]
    mlp_zero = scattered(jnp.concatenate([after(half, g_zero) for half in zero["halves"]], 1))
    far = after(zero["far_proj"], g_zero)
    proj_zero = jnp.concatenate([half_sum(zero["finish"](far)), zero["vec"]], 1)
    proj_zero = scattered(after(proj_zero, *back_slots))

    def exchanged(zero, one):
        return jnp.where(first, zero, one), swap_sections(jnp.where(first, one, zero))

    def joined(own, other):
        cut = width // 2
        parts = []
        for start in range(0, own.shape[1], cut):
            a, b = own[:, start:start + cut], other[:, start:start + cut]
            parts += [jnp.where(first, a, b), jnp.where(first, b, a)]
        return parts

    part = jnp.concatenate(joined(*exchanged(mlp_zero, mlp_one)), 1)
    far = across(part, 2)
    f_down, f_up = placed_parts(
        functools.partial(place_mlp_kernel, shards=shards), quarter, spread(part, far),
        [mlp_down.shape[1:], mlp_up.shape[1:]],
    )
    proj_zero = after(proj_zero, far)
    own, other = exchanged(proj_zero, proj_one)
    cut = width // 2
    part = jnp.concatenate(
        joined(own[:, :cut], other[:, :cut]) + [low_sum(own[:, cut:], other[:, cut:])], 1
    )
    f_in, f_out, f_vec = placed_parts(
        place_proj_kernel, quarter, spread(part, across(part, 2)),
        [attn_in.shape[1:], attn_out.shape[1:], (128, rows)],
    )
    f_vec = f_vec[:vectors.shape[1]]
    return edges_out[None], f_in[None], f_out[None], f_up[None], f_down[None], f_vec[None]


def solution(mesh):
    placed = (
        P("section", "replica", "shard", None),
        P("section", "shard", None),
        P("section", "shard", None),
        P("section", "shard", None),
        P("section", "shard", None),
        P("section", None, None),
        P("replica", None),
    )
    return jax.shard_map(
        body,
        mesh=mesh,
        in_specs=placed,
        out_specs=(
            P("section", "replica", "shard", None),
            P("section", "shard", None),
            P("section", "shard", None),
            P("section", "shard", None),
            P("section", "shard", None),
            P("section", None, "shard"),
        ),
        check_vma=False,
    )
```
